32 devices in a mesh: rep: 8 (over z, y), grp: 4 (over x, core).
Axes of the slice: x: 2, y: 2, z: 4, core: 2. Of those that a mesh axis runs over, the one named last changes fastest.
Arguments:
- tokens: int32 [32, 1024], P(('rep', 'grp')), may hold values from 0 to 32
- mask: int32 [32, 1024], P(('rep', 'grp')), may hold values from 0 to 1, as said below
- targets: int32 [32, 1024], P(('rep', 'grp')), may hold values from 0 to 32
- mats_d: float32 [1, 480, 3840], P(None, 'grp')
- mats_down: float32 [1, 1920, 480], P(None, 'grp'), may hold values from -0.125 to 0.125
- mom_d: float32 [1, 480, 3840], P(None, 'grp'), may hold values from -4.5776367e-05 to 4.5776367e-05
- mom_down: float32 [1, 1920, 480], P(None, 'grp'), may hold values from -4.5776367e-05 to 4.5776367e-05
- err_d: float32 [8, 1, 480, 3840], P('rep', None, 'grp'), may hold values from -0.0009765625 to 0.0009765625
- err_down: float32 [8, 1, 1920, 480], P('rep', None, 'grp'), may hold values from -0.0009765625 to 0.0009765625
- q_d: float32 [1, 3840, 8], replicated, may hold values from -5 to 5
- q_down: float32 [1, 480, 8], replicated, may hold values from -5 to 5
- vectors: float32 [1, 6240], replicated
- vec_mom: float32 [1, 6240], replicated, may hold values from -0.00021362305 to 0.00021362305
- final_norm: float32 [2, 480], replicated
- final_mom: float32 [2, 480], replicated, may hold values from -0.00021362305 to 0.00021362305
- embed: float32 [33, 480], replicated, may hold values from -5 to 5
- embed_mom: float32 [33, 480], replicated, may hold values from -9.1552734e-05 to 9.1552734e-05
- head: float32 [481, 33], replicated, may hold values from -0.25 to 0.25
- head_mom: float32 [481, 33], replicated, may hold values from -9.1552734e-05 to 9.1552734e-05
Outputs:
- loss_sum: float32 [], replicated
- count: float32 [], replicated
- grad_norm: float32 [], replicated
- new_mats_d: float32 [1, 480, 3840], P(None, 'grp')
- new_mats_down: float32 [1, 1920, 480], P(None, 'grp')
- new_mom_d: float32 [1, 480, 3840], P(None, 'grp')
- new_mom_down: float32 [1, 1920, 480], P(None, 'grp')
- new_err_d: float32 [8, 1, 480, 3840], P('rep', None, 'grp')
- new_err_down: float32 [8, 1, 1920, 480], P('rep', None, 'grp')
- p_d: float32 [1, 480, 8], P(None, 'grp')
- p_down: float32 [1, 1920, 8], P(None, 'grp')
- new_q_d: float32 [1, 3840, 8], replicated
- new_q_down: float32 [1, 480, 8], replicated
- new_vectors: float32 [1, 6240], replicated
- new_vec_mom: float32 [1, 6240], replicated
- new_final_norm: float32 [2, 480], replicated
- new_final_mom: float32 [2, 480], replicated
- new_embed: float32 [33, 480], replicated
- new_embed_mom: float32 [33, 480], replicated
- new_head: float32 [481, 33], replicated
- new_head_mom: float32 [481, 33], replicated
The draws below stay inside these ranges and needn't reach their ends.
Inputs may be any that keep to these rules, and one draw needn't show every extreme that they name: `mask`: position 0 of every sequence counts.
All inputs are finite; a program needn't handle non-finite values.
Results may differ from the reference program's by a relative error of at most 0.015.
The reference program's roundings to bfloat16 on the way count: a program that leaves them out, or rounds other values in their place, can miss the bound.
Values may be sent and summed in bfloat16 or wider, within the bound.
No kernel may reach another device: no remote copies, remote signals or barrier semaphores. Data moves between devices by JAX's collectives and lax.ppermute only.
A program may use at most 320 MiB of HBM per device.

```python
import math
import jax
import jax.numpy as jnp
from jax import lax

D = 480
HEADS = 20
HDIM = 24
FF = 1920
V = 33
LAYERS = 1
SEQ = 1024
RANK = 8
NSEQ = 32
N_REP = 8
N_GRP = 4


def draw_mask(key, part):
    key = jax.random.fold_in(key, 4)
    seq_index = jnp.arange(N_REP * N_GRP, dtype=jnp.int32)[:, None]
    rep_pos = seq_index // N_GRP
    grp_pos = seq_index % N_GRP
    limit = 40 * (N_REP - 1 + 2 * rep_pos) * (N_GRP - 1 + 2 * grp_pos) // ((N_REP - 1) * (N_GRP - 1))
    roll = jax.random.randint(key, (N_REP * N_GRP, SEQ), 0, 1000)
    first = jnp.arange(SEQ, dtype=jnp.int32)[None, :] == 0
    return jnp.where((roll < limit) | first, 1, 0).astype(jnp.int32)


def draw_mats_d(key, part):
    key = jax.random.fold_in(key, 1)
    column = jnp.arange(4 * D + FF)
    scale = jnp.where((column >= 3 * D) & (column < 4 * D), 12.0, 1.0) / math.sqrt(D)
    return jax.random.normal(key, (LAYERS, D, 4 * D + FF), jnp.float32) * scale[None, None, :]


def draw_vectors(key, part):
    key = jax.random.fold_in(key, 2)
    first, second = jax.random.split(key)
    width = 9 * D + FF
    column = jnp.arange(width)
    inner = (column % D).astype(jnp.float32)
    is_gain = (column < D) | (column >= 6 * D) & (column < 7 * D)
    gains = (1.0 + 2.0 * inner / D) * jax.random.uniform(first, (LAYERS, width), jnp.float32, 0.7, 1.3)
    shifts = 0.2 * jax.random.normal(second, (LAYERS, width), jnp.float32)
    return jnp.where(is_gain[None, :], gains, shifts)


def draw_final_norm(key, part):
    key = jax.random.fold_in(key, 3)
    first, second = jax.random.split(key)
    inner = jnp.arange(D).astype(jnp.float32)
    gains = (1.0 + 2.0 * inner / D) * jax.random.uniform(first, (D,), jnp.float32, 0.7, 1.3)
    shifts = 0.2 * jax.random.normal(second, (D,), jnp.float32)
    return jnp.stack([gains, shifts])


def plant(entries, stream_key, least, largest):
    longest = entries.shape.index(max(entries.shape))
    spots = []
    for shift in (0, 1):
        where = [jax.random.randint(jax.random.fold_in(stream_key, axis), (), 0, length) for axis, length in enumerate(entries.shape)]
        where[longest] = (where[longest] + shift) % entries.shape[longest]
        spots.append(tuple(where))
    return entries.at[spots[0]].set(least).at[spots[1]].set(largest)


def level_of(key, extent, cuts, low, largest):
    level = 1.0
    for position, parts in cuts:
        heights = jax.random.uniform(jax.random.fold_in(jax.random.fold_in(key, 6), position), (parts,), jnp.float32, low / len(cuts), largest / len(cuts))
        level = level * jnp.repeat(jnp.exp(heights), extent[position] // parts).reshape((-1,) + (1,) * (len(extent) - 1 - position))
    return level


def gaussian(rng, shape, scale, reach, shards=(), kind=jnp.bfloat16):
    entries = scale * jax.random.normal(rng, shape, jnp.float32)
    if shards:
        entries = entries * level_of(rng, shape, shards, -0.22, 0.18)
    return jnp.clip(entries, -reach, reach).astype(kind)


def setup_inputs(seed: int = 0) -> dict:
    key_list = jax.random.split(jax.random.key(seed), 20)
    return {
        "tokens": plant(jax.random.randint(key_list[0], (NSEQ, SEQ), 0, V), jax.random.fold_in(key_list[0], 1), 0, V - 1).astype(jnp.int32),
        "mask": draw_mask(jax.random.fold_in(key_list[19], 71), 0),
        "targets": plant(jax.random.randint(key_list[2], (NSEQ, SEQ), 0, V), jax.random.fold_in(key_list[2], 1), 0, V - 1).astype(jnp.int32),
        "mats_d": draw_mats_d(jax.random.fold_in(key_list[19], 71), 0),
        "mats_down": gaussian(key_list[4], (LAYERS, FF, D), FF ** -0.5, 0.125, ((1, 4),), jnp.float32),
        "mom_d": gaussian(key_list[5], (LAYERS, D, 4 * D + FF), (0.005 * (12 * LAYERS * D * D) ** -0.5), 4.57763671875e-05, ((1, 4),), jnp.float32),
        "mom_down": gaussian(key_list[6], (LAYERS, FF, D), (0.005 * (12 * LAYERS * D * D) ** -0.5), 4.57763671875e-05, ((1, 4),), jnp.float32),
        "err_d": gaussian(key_list[7], (N_REP, LAYERS, D, 4 * D + FF), (0.3 * (12 * LAYERS * D * D * N_REP) ** -0.5), 0.0009765625, ((0, 8), (2, 4)), jnp.float32),
        "err_down": gaussian(key_list[8], (N_REP, LAYERS, FF, D), (0.3 * (12 * LAYERS * D * D * N_REP) ** -0.5), 0.0009765625, ((0, 8), (2, 4)), jnp.float32),
        "q_d": gaussian(key_list[9], (LAYERS, 4 * D + FF, RANK), 1.0, 5.0, (), jnp.float32),
        "q_down": gaussian(key_list[10], (LAYERS, D, RANK), 1.0, 5.0, (), jnp.float32),
        "vectors": draw_vectors(jax.random.fold_in(key_list[19], 71), 0),
        "vec_mom": gaussian(key_list[12], (LAYERS, 9 * D + FF), (0.025 * (12 * LAYERS * D * D) ** -0.5), 0.00021362305, (), jnp.float32),
        "final_norm": draw_final_norm(jax.random.fold_in(key_list[19], 71), 0),
        "final_mom": gaussian(key_list[14], (2, D), (0.025 * (12 * LAYERS * D * D) ** -0.5), 0.00021362305, (), jnp.float32),
        "embed": gaussian(key_list[15], (V, D), 1.0, 5.0, (), jnp.float32),
        "embed_mom": gaussian(key_list[16], (V, D), (0.01 * (12 * LAYERS * D * D) ** -0.5), 9.1552734375e-05, (), jnp.float32),
        "head": gaussian(key_list[17], (D + 1, V), D ** -0.5, 0.25, (), jnp.float32),
        "head_mom": gaussian(key_list[18], (D + 1, V), (0.01 * (12 * LAYERS * D * D) ** -0.5), 9.1552734375e-05, (), jnp.float32),
    }


@jax.custom_vjp
def low(v):
    return lax.optimization_barrier(v.astype(jnp.bfloat16)).astype(jnp.float32)

@jax.custom_vjp
def low_back(v):
    return v

def low_keep(v):
    return (low(v), None)

def low_pass(kept, grad):
    return (grad,)

def back_keep(v):
    return (v, None)

def back_low(kept, grad):
    return (low(grad),)
low.defvjp(low_keep, low_pass)
low_back.defvjp(back_keep, back_low)
EPS = 1e-05
BETA = 0.9
RATE_WIDE = 20000.0
RATE_LOWER = 3000.0
RATE_VECTOR = 20000.0
RATE_FINAL = 40000.0
RATE_EMBED = 60000.0
RATE_HEAD = 3000.0
CLIP = 0.005
HIGHEST = lax.Precision.HIGHEST

def product(left, right):
    return jnp.dot(left, right, precision=HIGHEST)

def layer_norm(value, gain, shift):
    center = value - lax.optimization_barrier(jnp.mean(value, -1, keepdims=True))
    spread = lax.optimization_barrier(jnp.mean(center * center, -1, keepdims=True))
    return center * lax.rsqrt(spread + EPS) * gain + shift

def tables(length, width):
    half = width // 2
    freq = 10000.0 ** (-jnp.arange(half, dtype=jnp.float32) * 2.0 / width)
    angle = jnp.arange(length, dtype=jnp.float32)[:, None] * freq[None, :]
    angle = jnp.concatenate([angle, angle], -1)
    return (jnp.cos(angle), jnp.sin(angle))

def rotary(value, cosine, sine):
    half = value.shape[-1] // 2
    turned = jnp.concatenate([-value[..., half:], value[..., :half]], -1)
    return value * cosine[:, None, :] + turned * sine[:, None, :]

def layer(resid, wide, down, vec, cosine, sine):
    length = resid.shape[0]
    normed = low(layer_norm(resid, vec[0:D], vec[D:2 * D]))
    act = low_back(product(normed, wide[:, :3 * D]) + vec[2 * D:5 * D])
    query = rotary(act[:, :D].reshape(length, HEADS, HDIM), cosine, sine) * HDIM ** (-0.5)
    keys = rotary(act[:, D:2 * D].reshape(length, HEADS, HDIM), cosine, sine)
    values = act[:, 2 * D:3 * D].reshape(length, HEADS, HDIM)
    query, keys, values = (low(query), low(keys), low(values))
    scores = low_back(jnp.einsum('qhe,khe->hqk', query, keys, precision=HIGHEST))
    expo = jnp.exp(scores - lax.optimization_barrier(jnp.max(scores, -1, keepdims=True)))
    probs = expo / lax.optimization_barrier(jnp.sum(expo, -1, keepdims=True))
    mixed = jnp.einsum('hqk,khe->qhe', low(probs), values, precision=HIGHEST).reshape(length, D)
    mixed = low(low_back(mixed))
    middle = resid + low_back(product(mixed, wide[:, 3 * D:4 * D]) + vec[5 * D:6 * D])
    normed2 = low(layer_norm(middle, vec[6 * D:7 * D], vec[7 * D:8 * D]))
    upper = low_back(product(normed2, wide[:, 4 * D:]) + vec[9 * D:])
    hidden = low(jax.nn.gelu(upper, approximate=False))
    return middle + low_back(product(hidden, down) + vec[8 * D:9 * D])

def masked_loss(picks, weight_mask, logits):
    shifted = logits - lax.optimization_barrier(jnp.max(logits, -1, keepdims=True))
    logp = shifted - jnp.log(lax.optimization_barrier(jnp.sum(jnp.exp(shifted), -1, keepdims=True)))
    return -jnp.sum(lax.optimization_barrier(jnp.sum(logp * picks, -1)) * weight_mask)

def seq_loss(weights, token_ids, row_mask, row_targets):
    wide, down, vectors, final_norm, embed, head = weights
    resid = embed[token_ids]
    cosine, sine = tables(SEQ, HDIM)
    for index in range(LAYERS):
        resid = layer(resid, wide[index], down[index], vectors[index], cosine, sine)
    final = low(layer_norm(resid, final_norm[0], final_norm[1]))
    logits = low_back(product(final, head[:D]) + head[D])
    picks = (row_targets[:, None] == jnp.arange(V, dtype=jnp.int32)[None, :]).astype(logits.dtype)
    return masked_loss(picks, row_mask.astype(logits.dtype), logits)

def group_loss(weights, toks, masks, targs):
    wide, down, vectors, final_norm, embed, head = weights
    rounded = (low(wide), low(down), vectors, final_norm, embed, jnp.concatenate([low(head[:D]), head[D:]], 0))

    def one_seq(item):
        return seq_loss(rounded, item[0], item[1], item[2])
    return jnp.sum(lax.map(jax.checkpoint(one_seq), (toks, masks, targs)))

def compress(grads, errors, start):
    merged = grads + errors
    sketch = jnp.einsum('glrc,lck->lrk', merged, start, precision=HIGHEST)
    gram = jnp.einsum('lrk,lrj->lkj', sketch, sketch, precision=HIGHEST)
    lower = jnp.linalg.cholesky(gram)
    basis = lax.linalg.triangular_solve(lower, sketch, left_side=False, lower=True, transpose_a=True)
    factor = jnp.einsum('glrc,lrk->lck', merged, basis, precision=HIGHEST)
    approx = jnp.einsum('lrk,lck->lrc', basis, factor, precision=HIGHEST)
    return (basis, factor, approx, merged - approx[None] / N_REP)

def renew(weight, moment, grad, scale, rate):
    new_moment = BETA * moment + scale * grad
    return (weight - rate * new_moment, new_moment)

def reference(tokens, mask, targets, mats_d, mats_down, mom_d, mom_down, err_d, err_down, q_d, q_down, vectors, vec_mom, final_norm, final_mom, embed, embed_mom, head, head_mom):
    weights = (mats_d, mats_down, vectors, final_norm, embed, head)
    count = jnp.sum(mask).astype(jnp.float32)
    toks = tokens.reshape(N_REP, N_GRP, SEQ)
    masks = mask.reshape(N_REP, N_GRP, SEQ)
    targs = targets.reshape(N_REP, N_GRP, SEQ)

    def one_group(item):

        def group_fn(params):
            return group_loss(params, item[0], item[1], item[2])
        loss, pull = jax.vjp(group_fn, weights)
        return (loss, pull(1.0 / count)[0])
    losses, grads = lax.map(one_group, (toks, masks, targs))
    g_wide, g_down, g_vec, g_fin, g_emb, g_head = grads
    p_wide, f_wide, a_wide, e_wide = compress(g_wide, err_d, q_d)
    p_down, f_down, a_down, e_down = compress(g_down, err_down, q_down)
    g_vec, g_fin = (lax.optimization_barrier(jnp.sum(g_vec, 0)), lax.optimization_barrier(jnp.sum(g_fin, 0)))
    g_emb, g_head = (lax.optimization_barrier(jnp.sum(g_emb, 0)), lax.optimization_barrier(jnp.sum(g_head, 0)))
    square = jnp.sum(a_wide * a_wide) + jnp.sum(a_down * a_down)
    square = square + jnp.sum(g_vec * g_vec) + jnp.sum(g_fin * g_fin) + jnp.sum(g_emb * g_emb) + jnp.sum(g_head * g_head)
    grad_norm = jnp.sqrt(square)
    scale = jnp.minimum(1.0, CLIP / grad_norm)
    new_wide, new_mom_wide = renew(mats_d, mom_d, a_wide, scale, RATE_WIDE)
    new_down, new_mom_dn = renew(mats_down, mom_down, a_down, scale, RATE_LOWER)
    new_vec, new_vmom = renew(vectors, vec_mom, g_vec, scale, RATE_VECTOR)
    new_fin, new_fmom = renew(final_norm, final_mom, g_fin, scale, RATE_FINAL)
    new_emb, new_emom = renew(embed, embed_mom, g_emb, scale, RATE_EMBED)
    new_head, new_hmom = renew(head, head_mom, g_head, scale, RATE_HEAD)
    return (jnp.sum(losses), count, grad_norm, new_wide, new_down, new_mom_wide, new_mom_dn, e_wide, e_down, p_wide, p_down, f_wide, f_down, new_vec, new_vmom, new_fin, new_fmom, new_emb, new_emom, new_head, new_hmom)
```

```python
from functools import partial

import jax
import jax.numpy as jnp
import numpy as np
from jax import lax
from jax.experimental import pallas as pl
from jax.experimental.pallas import tpu as pltpu
from jax.sharding import PartitionSpec as P

D = 480
HEADS = 20
HDIM = 24
V = 33
PAD = 32
TOK = 40
WIDE = 512
EPS = 1e-05
BETA = 0.9
RATE_WIDE = 20000.0
RATE_LOWER = 3000.0
RATE_VECTOR = 20000.0
RATE_FINAL = 40000.0
RATE_EMBED = 60000.0
RATE_HEAD = 3000.0
CLIP = 0.005
F32 = jnp.float32
B16 = jnp.bfloat16
MIB = 2**20


def params(limit=56):
    return pltpu.CompilerParams(vmem_limit_bytes=limit * MIB)


def nn(left, right):
    return jnp.dot(left, right, preferred_element_type=F32)


def nt(left, right):
    return lax.dot_general(left, right, (((1,), (1,)), ((), ())), preferred_element_type=F32)


def tn(left, right):
    return lax.dot_general(left, right, (((0,), (0,)), ((), ())), preferred_element_type=F32)


def thirds(value):
    top = value.astype(B16)
    rest = value - top.astype(F32)
    middle = rest.astype(B16)
    return top, middle, (rest - middle.astype(F32)).astype(B16)


def thirds_rows(value):
    return jnp.concatenate([part.astype(F32) for part in thirds(value)], 0).astype(B16)


def fold_rows(value):
    return value[0:8] + value[8:16] + value[16:24]


def exact_nt(left, right):
    return lax.dot_general(
        left, right, (((1,), (1,)), ((), ())),
        precision=lax.Precision.HIGHEST, preferred_element_type=F32,
    )


def exact_nn(left, right):
    return jnp.dot(left, right, precision=lax.Precision.HIGHEST, preferred_element_type=F32)


def norm_parts(value):
    center = value - jnp.mean(value, -1, keepdims=True)
    spread = jnp.mean(center * center, -1, keepdims=True)
    rstd = lax.rsqrt(spread + EPS)
    return center * rstd, rstd


def norm_back(grad, unit, rstd, gain):
    inner = grad * gain
    first = jnp.mean(inner, -1, keepdims=True)
    second = jnp.mean(inner * unit, -1, keepdims=True)
    return (
        rstd * (inner - first - unit * second),
        jnp.sum(grad * unit, 0, keepdims=True),
        jnp.sum(grad, 0, keepdims=True),
    )


def half_turn(value):
    return jnp.concatenate([value[HDIM // 2 :], value[: HDIM // 2]], 0)


def tail(rows, cols, ones):
    index = lax.broadcasted_iota(jnp.int32, (rows, cols), 0)
    return jnp.where(index < ones, 1.0, 0.0).astype(F32)


def lane_tail(rows, cols):
    index = lax.broadcasted_iota(jnp.int32, (rows, cols), 1)
    return jnp.where(index == 0, 1.0, 0.0).astype(F32)


def tables(length):
    half = HDIM // 2
    freq = np.float32(10000.0) ** (-np.arange(half, dtype=np.float32) * np.float32(2.0) / np.float32(HDIM))
    angle = np.arange(length, dtype=np.float32)[None, :] * freq.astype(np.float32)[:, None]
    cosine, sine = np.cos(angle), np.sin(angle)
    return (
        jnp.asarray(np.concatenate([cosine, cosine], 0), F32),
        jnp.asarray(np.concatenate([-sine, sine], 0), F32),
    )


def error_kernel(group, err_ref, errd_ref, q_ref, qd_ref, out_ref, row_ref):
    rows = err_ref.shape[0]
    out_ref[...] = jnp.zeros_like(out_ref)
    row_ref[...] = jnp.zeros_like(row_ref)
    row_ref[:, 0:rows] = exact_nt(q_ref[...], err_ref[...])
    out_ref[0:8, :] = pltpu.roll(row_ref[...], rows * group[0], 1)
    start = pl.multiple_of(8 + 8 * group[0], 8)
    out_ref[pl.ds(start, 8), 0:D] = exact_nt(qd_ref[...], errd_ref[...])


def embed_kernel(tok_ref, emb_ref, w_ref, vec_ref, bias_ref, cos_ref, sin_ref,
                 x_ref, h_ref, q_ref, k_ref, v_ref, emb_s):
    step = tok_ref.shape[1]

    @pl.when(pl.program_id(0) == 0)
    def _():
        emb_s[...] = jnp.zeros_like(emb_s)
        emb_s[0:V, :] = emb_ref[...]

    index = lax.broadcasted_iota(jnp.int32, (TOK, step), 0)
    hot = jnp.where(index == tok_ref[...], 1.0, 0.0).astype(F32)
    hot = jnp.concatenate([hot, hot, hot], 0).astype(B16)
    x = tn(hot, thirds_rows(emb_s[...]))
    x_ref[...] = x
    unit, _ = norm_parts(x)
    normed = unit * vec_ref[0:1, :] + vec_ref[1:2, :]
    act = nn(normed.astype(B16), w_ref[...]) + bias_ref[...]
    h_ref[...] = jnp.concatenate([normed.T, tail(16, step, 1)], 0).astype(B16)
    turned = act.T
    cosine, sine = cos_ref[...], sin_ref[...]
    zeros = tail(PAD - HDIM, step, 0)
    ones = tail(PAD - HDIM, step, 3)
    for head in range(HEADS):
        low = HDIM * head
        query = turned[low : low + HDIM]
        query = (query * cosine + half_turn(query) * sine) * HDIM ** (-0.5)
        q_ref[head] = jnp.concatenate([query, zeros], 0).astype(B16)
        keys = turned[D + low : D + low + HDIM]
        keys = keys * cosine + half_turn(keys) * sine
        k_ref[head] = jnp.concatenate([keys, zeros], 0).astype(B16)
        value = turned[2 * D + low : 2 * D + low + HDIM]
        v_ref[head] = jnp.concatenate([value, ones], 0).astype(B16)


def rows_of(value):
    return value.astype(F32).T.astype(B16)


def attend_kernel(q_ref, k_ref, v_ref, mix_ref, inv_ref, p_ref):
    scores = nn(rows_of(k_ref[0]), q_ref[0])
    top = jnp.max(scores, 0, keepdims=True)
    probs = jnp.exp(scores - top).astype(B16)
    p_ref[0] = probs
    out = nn(v_ref[0], probs)
    inverse = 1.0 / out[HDIM : HDIM + 1]
    mix_ref[...] = out[0:HDIM] * inverse
    inv_ref[0] = inverse


def gelu_parts(upper):
    size = jnp.abs(upper) * (0.5**0.5)
    bell = jnp.exp(-0.5 * upper * upper)
    t = 1.0 / (1.0 + 0.3275911 * size)
    poly = t * (0.254829592 + t * (-0.284496736 + t * (1.421413741 + t * (-1.453152027 + t * 1.061405429))))
    lower = 0.5 * poly * bell
    cdf = jnp.where(upper < 0, lower, 1.0 - lower)
    return upper * cdf, cdf + upper * (0.3989422804014327 * bell)


def middle_kernel(mix_ref, inv_ref, x_ref, mask_ref, tgt_ref, count_ref, vec_ref, bu_ref, fin_ref,
                  head_ref, wo_ref, wu_ref, wd_ref, q_ref, qd_ref,
                  dm_ref, dx_ref, go_ref, gu_ref, gd_ref, s_ref, e_ref,
                  acc_o, acc_u, acc_d, head_s, hid_s, slope_s):
    pid = pl.program_id(0)
    step = x_ref.shape[0]
    wide = wu_ref.shape[1]

    @pl.when(pid == 0)
    def _():
        acc_o[...] = jnp.zeros_like(acc_o)
        acc_u[...] = jnp.zeros_like(acc_u)
        acc_d[...] = jnp.zeros_like(acc_d)
        e_ref[...] = jnp.zeros_like(e_ref)
        s_ref[...] = jnp.zeros_like(s_ref)
        head_s[...] = jnp.zeros_like(head_s)
        head_s[0:V, 0 : D + 1] = head_ref[...]

    mix = mix_ref[...]
    mixed = jnp.concatenate([mix, tail(16, step, 1)], 0).astype(B16)
    middle = x_ref[...] + tn(mixed[0:D], wo_ref[...]) + vec_ref[5:6, :]
    unit2, rstd2 = norm_parts(middle)
    normed2 = unit2 * vec_ref[6:7, :] + vec_ref[7:8, :]
    normed2 = jnp.concatenate([normed2, lane_tail(step, WIDE - D)], 1).astype(B16)
    block = 384
    for low in range(0, wide, block):
        cut = slice(low, low + block)
        upper = nn(normed2[:, 0:D], wu_ref[:, cut]) + bu_ref[:, cut]
        hidden, slope = gelu_parts(upper)
        hid_s[:, cut] = hidden.astype(B16)
        slope_s[:, cut] = slope
    resid = middle + nn(hid_s[...], wd_ref[...]) + vec_ref[8:9, :]
    unit3, rstd3 = norm_parts(resid)
    final = unit3 * fin_ref[0:1, :] + fin_ref[1:2, :]
    final = jnp.concatenate([final, lane_tail(step, WIDE - D)], 1).astype(B16)

    lanes = lax.broadcasted_iota(jnp.int32, (TOK, WIDE), 1)
    bias = jnp.sum(jnp.where(lanes == D, head_s[...], 0.0), 1, keepdims=True)
    table = head_s[:, 0:D].astype(B16)
    rows = lax.broadcasted_iota(jnp.int32, (TOK, step), 0)
    logits = jnp.where(rows < V, nt(table, final[:, 0:D]) + bias, -1e30)
    shifted = logits - jnp.max(logits, 0, keepdims=True)
    expo = jnp.exp(shifted)
    total = jnp.sum(expo, 0, keepdims=True)
    picks = rows == tgt_ref[...]
    weight = mask_ref[...].astype(F32)
    picked = jnp.sum(jnp.where(picks, shifted, 0.0), 0, keepdims=True)
    loss = jnp.sum((jnp.log(total) - picked) * weight, 1, keepdims=True)
    grad_logits = (expo / total - jnp.where(picks, 1.0, 0.0)) * (weight * (1.0 / count_ref[...]))
    grad_logits = grad_logits.astype(B16)
    e_ref[16 : 16 + TOK, :] += nn(grad_logits, final)
    grad_resid, grad_fg, grad_fb = norm_back(tn(grad_logits, table), unit3, rstd3, fin_ref[0:1, :])

    grad_y = grad_resid.astype(B16)
    acc_d[...] += tn(hid_s[...], grad_y)
    for low in range(0, wide, block):
        cut = slice(low, low + block)
        grad_hidden = nt(grad_y, wd_ref[cut, :])
        hid_s[:, cut] = (grad_hidden * slope_s[:, cut]).astype(B16)
    acc_u[...] += tn(normed2, hid_s[...])
    grad_mid, grad_g2, grad_b2 = norm_back(nt(hid_s[...], wu_ref[...]), unit2, rstd2, vec_ref[6:7, :])
    grad_mid = grad_mid + grad_resid
    dx_ref[...] = grad_mid
    branch = grad_mid.astype(B16)
    acc_o[...] += nn(mixed, branch)
    grad_mixed = nt(wo_ref[...], branch).astype(B16).astype(F32)
    zeros = tail(PAD - HDIM - 3, step, 0)
    for head in range(HEADS):
        cut = slice(HDIM * head, HDIM * head + HDIM)
        scaled = (grad_mixed[cut] * inv_ref[head]).astype(B16).astype(F32)
        delta = -jnp.sum(scaled * mix[cut], 0, keepdims=True)
        top, mid, low = thirds(delta)
        dm_ref[head] = jnp.concatenate(
            [scaled, top.astype(F32), mid.astype(F32), low.astype(F32), zeros], 0
        ).astype(B16)
    e_ref[1:2, 0:D] += grad_g2
    e_ref[2:3, 0:D] += grad_b2
    e_ref[3:4, 0:D] += jnp.sum(grad_y.astype(F32), 0, keepdims=True)
    e_ref[8:9, 0:D] += grad_fg
    e_ref[9:10, 0:D] += grad_fb
    e_ref[10:11, :] += jnp.broadcast_to(loss, (1, WIDE))

    @pl.when(pid == pl.num_programs(0) - 1)
    def _():
        e_ref[0:1, 0:D] = acc_o[D : D + 1, :]
        for part in range(wide // D):
            e_ref[4 + part : 5 + part, 0:D] = acc_u[D : D + 1, D * part : D * part + D]
        go = acc_o[0:D, :].astype(B16)
        gu = acc_u[0:D, :].astype(B16)
        go_ref[...] = go
        gu_ref[...] = gu
        gd_ref[...] = acc_d[...].astype(B16)
        sketch = nt(thirds_rows(q_ref[:, 3 * D : 4 * D]), go) + nt(thirds_rows(q_ref[:, 4 * D :]), gu)
        s_ref[0:8, 0:D] = fold_rows(sketch)
        start = thirds_rows(qd_ref[...])
        for part in range(wide // D):
            piece = nt(start, gd_ref[D * part : D * part + D, :])
            s_ref[8 + 8 * part : 16 + 8 * part, 0:D] = fold_rows(piece)


def attend_back_kernel(p_ref, q_ref, k_ref, v_ref, dm_ref, cos_ref, sin_ref, da_ref):
    cosine, sine = cos_ref[...], sin_ref[...]
    parts = [[], [], []]
    for head in range(p_ref.shape[0]):
        probs = p_ref[head]
        grad = dm_ref[head]
        slope = nn(rows_of(v_ref[head]), grad)
        grad_scores = (probs.astype(F32) * slope).astype(B16)
        grad_value = nt(grad, probs)[0:HDIM]
        grad_keys = nt(q_ref[head], grad_scores)[0:HDIM]
        grad_query = nn(k_ref[head], grad_scores)[0:HDIM] * HDIM ** (-0.5)
        parts[0].append(grad_query * cosine + half_turn(grad_query * sine))
        parts[1].append(grad_keys * cosine + half_turn(grad_keys * sine))
        parts[2].append(grad_value)
    for index in range(3):
        da_ref[index] = jnp.concatenate(parts[index], 0).astype(B16)


def input_kernel(tok_ref, da_ref, h_ref, x_ref, dx_ref, w_ref, vec_ref, q_ref, s_ref, serr_ref, e_ref,
                 g_ref, out_ref, acc_w, acc_e):
    pid = pl.program_id(0)
    step = x_ref.shape[0]

    @pl.when(pid == 0)
    def _():
        acc_w[...] = jnp.zeros_like(acc_w)
        acc_e[...] = jnp.zeros_like(acc_e)
        out_ref[...] = jnp.zeros_like(out_ref)

    da = da_ref[...].reshape(3 * D, step)
    acc_w[...] += nt(h_ref[...], da)
    grad = nn(w_ref[...], da).T
    unit, rstd = norm_parts(x_ref[...])
    grad_x, grad_g, grad_b = norm_back(grad, unit, rstd, vec_ref[0:1, :])
    grad_x = grad_x + dx_ref[...]
    index = lax.broadcasted_iota(jnp.int32, (TOK, step), 0)
    hot = jnp.where(index == tok_ref[...], 1.0, 0.0).astype(B16)
    for part in thirds(grad_x):
        acc_e[...] += nn(hot, part)
    out_ref[40:41, 0:D] += grad_g
    out_ref[41:42, 0:D] += grad_b

    @pl.when(pid == pl.num_programs(0) - 1)
    def _():
        for part in range(3):
            out_ref[42 + part : 43 + part, 0:D] = acc_w[D : D + 1, D * part : D * part + D]
        g = acc_w[0:D, :].astype(B16)
        g_ref[...] = g
        out_ref[0:40, :] = s_ref[...] + serr_ref[...]
        out_ref[0:8, 0:D] += fold_rows(nt(thirds_rows(q_ref[:, 0 : 3 * D]), g))
        out_ref[48:104, :] = e_ref[...]
        out_ref[104 : 104 + TOK, 0:D] = acc_e[...]


def orthonormal(sketch, gram):
    basis = jnp.zeros_like(sketch[0])
    count = gram.shape[0]
    index = lax.broadcasted_iota(jnp.int32, (count, 1), 0)
    out = [jnp.zeros_like(part) for part in sketch]
    left = list(sketch)
    for step in range(count):
        pivot = gram[step : step + 1, step : step + 1]
        scale = 1.0 / jnp.sqrt(pivot)
        column = gram[:, step : step + 1] * scale
        row = gram[step : step + 1, :] * scale
        column = jnp.where(index > step, column, 0.0)
        gram = gram - column * row
        for place in range(len(left)):
            base = left[place][step : step + 1, :] * scale
            out[place] = jnp.where(index == step, base, out[place])
            left[place] = left[place] - column * base
    return out


def factor_kernel(group, a_ref, gi_ref, go_ref, gu_ref, gd_ref, err_ref, errd_ref,
                  p_ref, own_ref, f_ref, pad_s):
    rows = err_ref.shape[0]
    parts = gd_ref.shape[0] // D
    wide = a_ref[0:8, 0:D]
    down = [a_ref[8 + 8 * part : 16 + 8 * part, 0:D] for part in range(parts)]
    gram = exact_nt(wide, wide)
    (wide,) = orthonormal([wide], gram)
    gram = exact_nt(down[0], down[0])
    for part in range(1, parts):
        gram = gram + exact_nt(down[part], down[part])
    down = orthonormal(down, gram)
    p_ref[...] = jnp.zeros_like(p_ref)
    p_ref[0:8, 0:D] = wide
    for part in range(parts):
        p_ref[8 + 8 * part : 16 + 8 * part, 0:D] = down[part]
    own = pltpu.roll(p_ref[0:8, :], (WIDE - rows * group[0]) % WIDE, 1)
    start = pl.multiple_of(8 + 8 * group[0], 8)
    own_down = p_ref[pl.ds(start, 8), :]
    own_ref[0:8, :] = own
    own_ref[8:16, :] = own_down
    total = exact_nn(own[:, 0:rows], err_ref[...])
    three = thirds_rows(wide)
    f_ref[...] = jnp.zeros_like(f_ref)
    f_ref[0:8, :] = total
    f_ref[0:8, 0 : 3 * D] += fold_rows(nn(three, gi_ref[...]))
    f_ref[0:8, 3 * D : 4 * D] += fold_rows(nn(three, go_ref[...]))
    f_ref[0:8, 4 * D :] += fold_rows(nn(three, gu_ref[...]))
    total = exact_nn(own_down[:, 0:D], errd_ref[...])
    for part in range(parts):
        total = total + fold_rows(nn(thirds_rows(down[part]), gd_ref[D * part : D * part + D, :]))
    f_ref[8:16, 0:D] = total


def six(left, right):
    first, second = thirds(left), thirds(right)
    order = ((0, 0), (0, 1), (1, 0), (1, 1), (0, 2), (2, 0))
    left = jnp.concatenate([first[i].astype(F32) for i, _ in order], 0).astype(B16)
    right = jnp.concatenate([second[j].astype(F32) for _, j in order], 0).astype(B16)
    return tn(left, right)


def renew(weight, moment, grad, scale, rate):
    new_moment = BETA * moment + scale * grad
    return weight - rate * new_moment, new_moment


def finish_kernel(replicas, a_ref, p_ref, own_ref, f_ref, gi_ref, gr_ref, gd_ref,
                  w_ref, wd_ref, m_ref, md_ref, err_ref, errd_ref,
                  vec_ref, vmom_ref, fin_ref, fmom_ref, emb_ref, emom_ref, head_ref, hmom_ref,
                  norm_ref, nw_ref, nwd_ref, nm_ref, nmd_ref, ne_ref, ned_ref,
                  nvec_ref, nvmom_ref, nfin_ref, nfmom_ref, nemb_ref, nemom_ref, nhead_ref, nhmom_ref):
    rows = err_ref.shape[0]
    a = a_ref[...]
    square = jnp.sum(a[40:45, 0:D] * a[40:45, 0:D]) + jnp.sum(a[48:58, 0:D] * a[48:58, 0:D])
    square = square + jnp.sum(a[104 : 104 + V, 0:D] * a[104 : 104 + V, 0:D])
    lanes = lax.broadcasted_iota(jnp.int32, (V, WIDE), 1)
    square = square + jnp.sum(jnp.where(lanes <= D, a[64 : 64 + V] * a[64 : 64 + V], 0.0))
    basis = p_ref[...]
    factor = f_ref[...]
    gram = exact_nt(basis[0:8, 0:D], basis[0:8, 0:D])
    square = square + jnp.sum(gram * exact_nt(factor[0:8], factor[0:8]))
    gram = jnp.zeros((8, 8), F32)
    for part in range(1, basis.shape[0] // 8):
        piece = basis[8 * part : 8 * part + 8, 0:D]
        gram = gram + exact_nt(piece, piece)
    square = square + jnp.sum(gram * exact_nt(factor[8:16, 0:D], factor[8:16, 0:D]))
    norm = jnp.sqrt(square)
    norm_ref[...] = jnp.broadcast_to(norm, norm_ref.shape)
    scale = jnp.minimum(1.0, CLIP / norm)

    approx = six(own_ref[0:8, 0:rows], factor[0:8])
    nw_ref[...], nm_ref[...] = renew(w_ref[...], m_ref[...], approx, scale, RATE_WIDE)
    share = approx * (1.0 / replicas)
    ne_ref[:, 0 : 3 * D] = gi_ref[...].astype(F32) + err_ref[:, 0 : 3 * D] - share[:, 0 : 3 * D]
    ne_ref[:, 3 * D :] = gr_ref[...].astype(F32) + err_ref[:, 3 * D :] - share[:, 3 * D :]
    approx = six(own_ref[8:16, 0:D], factor[8:16, 0:D])
    nwd_ref[...], nmd_ref[...] = renew(wd_ref[...], md_ref[...], approx, scale, RATE_LOWER)
    ned_ref[...] = gd_ref[...].astype(F32) + errd_ref[...] - approx * (1.0 / replicas)

    places = (40, 41, 42, 43, 44, 48, 49, 50, 51, 52, 53, 54, 55)
    for row, place in enumerate(places):
        cut = slice(row, row + 1)
        nvec_ref[cut, :], nvmom_ref[cut, :] = renew(
            vec_ref[cut, :], vmom_ref[cut, :], a[place : place + 1, 0:D], scale, RATE_VECTOR
        )
    nfin_ref[...], nfmom_ref[...] = renew(fin_ref[...], fmom_ref[...], a[56:58, 0:D], scale, RATE_FINAL)
    nemb_ref[...], nemom_ref[...] = renew(
        emb_ref[...], emom_ref[...], a[104 : 104 + V, 0:D], scale, RATE_EMBED
    )
    nhead_ref[...], nhmom_ref[...] = renew(
        head_ref[...], hmom_ref[...], a[64 : 64 + V, 0 : D + 1], scale, RATE_HEAD
    )


def swap(value, axis, bit):
    size = lax.axis_size(axis)
    return lax.ppermute(value, axis, [(i, i ^ bit) for i in range(size)])


def bits_of(axis):
    size, bit, out = lax.axis_size(axis), 1, []
    while bit < size:
        out.append(bit)
        bit *= 2
    return out


def gather_rows(value, axis):
    place = lax.axis_index(axis)
    value = value[None]
    for bit in reversed(bits_of(axis)):
        other = swap(value, axis, bit)
        mine = (place & bit) == 0
        value = jnp.stack([jnp.where(mine, value, other), jnp.where(mine, other, value)], -3)
    return value.reshape(-1, value.shape[-1])


def add_all(value):
    for axis in ("grp", "rep"):
        for bit in bits_of(axis):
            value = value + swap(value, axis, bit)
    return value


def whole(shape):
    return pl.BlockSpec(shape, lambda *_: (0,) * len(shape))


def shards(tokens, mask, targets, mats_d, mats_down, mom_d, mom_down, err_d, err_down, q_d, q_down,
           vectors, vec_mom, final_norm, final_mom, embed, embed_mom, head, head_mom):
    length = tokens.shape[1]
    wide = mats_d.shape[2]
    hidden = wide - 4 * D
    rows = mats_d.shape[1]
    rows_down = mats_down.shape[1]
    step = 256
    steps = length // step
    group = lax.axis_index("grp").astype(jnp.int32).reshape(1)
    cosine, sine = tables(length)
    q_t, qd_t = q_d[0].T, q_down[0].T
    head_t = head.T
    vec = vectors.reshape(-1, D)
    err, errd = err_d[0, 0], err_down[0, 0]

    wide16 = mats_d[0].astype(B16)
    w_in = gather_rows(wide16[:, : 3 * D], "grp")
    w_rest = lax.all_gather(wide16[:, 3 * D :], "grp", axis=0, tiled=True)
    w_down = lax.all_gather(mats_down[0].astype(B16), "grp", axis=0, tiled=True)
    w_out, w_up = w_rest[:, :D], w_rest[:, D:]
    counted = jnp.broadcast_to(jnp.sum(mask.astype(F32)), (8, 128))
    counted = add_all(counted)[0:1, 0:1]

    prefetch = lambda grid, ins, outs, scratch: pltpu.PrefetchScalarGridSpec(
        num_scalar_prefetch=1, grid=grid, in_specs=ins, out_specs=outs, scratch_shapes=scratch
    )
    err_sketch = pl.pallas_call(
        error_kernel,
        grid_spec=prefetch(
            (1,),
            [whole((rows, wide)), whole((rows_down, D)), whole((8, wide)), whole((8, D))],
            whole((40, WIDE)),
            [pltpu.VMEM((8, WIDE), F32)],
        ),
        out_shape=jax.ShapeDtypeStruct((40, WIDE), F32),
        compiler_params=params(),
        name="error_sketch",
    )(group, err, errd, q_t, qd_t)

    cols = pl.BlockSpec((1, step), lambda i: (0, i))
    flat = pl.BlockSpec((step, D), lambda i: (i, 0))
    heads = pl.BlockSpec((HEADS, PAD, step), lambda i: (0, 0, i))
    wave = pl.BlockSpec((HDIM, step), lambda i: (0, i))
    x, h_t, query, keys, value = pl.pallas_call(
        embed_kernel,
        grid=(steps,),
        in_specs=[cols, whole((V, D)), whole((D, 3 * D)), whole(vec.shape), whole((1, 3 * D)), wave, wave],
        out_specs=[flat, pl.BlockSpec((D + 16, step), lambda i: (0, i)), heads, heads, heads],
        out_shape=[
            jax.ShapeDtypeStruct((length, D), F32),
            jax.ShapeDtypeStruct((D + 16, length), B16),
        ]
        + [jax.ShapeDtypeStruct((HEADS, PAD, length), B16)] * 3,
        scratch_shapes=[pltpu.VMEM((TOK, D), F32)],
        compiler_params=params(),
        name="embed_project",
    )(tokens, embed, w_in, vec, vectors[:, 2 * D : 5 * D], cosine, sine)

    one = pl.BlockSpec((1, PAD, length), lambda i: (i, 0, 0))
    mix, inverse, probs = pl.pallas_call(
        attend_kernel,
        grid=(HEADS,),
        in_specs=[one, one, one],
        out_specs=[
            pl.BlockSpec((HDIM, length), lambda i: (i, 0)),
            pl.BlockSpec((1, 1, length), lambda i: (i, 0, 0)),
            pl.BlockSpec((1, length, length), lambda i: (i, 0, 0)),
        ],
        out_shape=[
            jax.ShapeDtypeStruct((D, length), F32),
            jax.ShapeDtypeStruct((HEADS, 1, length), F32),
            jax.ShapeDtypeStruct((HEADS, length, length), B16),
        ],
        compiler_params=params(),
        name="attend",
    )(query, keys, value)

    grad_mix, grad_mid, g_out, g_up, g_down, sketch, early = pl.pallas_call(
        middle_kernel,
        grid=(steps,),
        in_specs=[
            pl.BlockSpec((D, step), lambda i: (0, i)),
            pl.BlockSpec((HEADS, 1, step), lambda i: (0, 0, i)),
            flat, cols, cols, whole((1, 1)), whole(vec.shape), whole((1, hidden)), whole((2, D)),
            whole((V, D + 1)), whole((D, D)), whole((D, hidden)), whole((hidden, D)),
            whole((8, wide)), whole((8, D)),
        ],
        out_specs=[
            heads, flat, whole((D, D)), whole((D, hidden)), whole((hidden, D)),
            whole((40, WIDE)), whole((56, WIDE)),
        ],
        out_shape=[
            jax.ShapeDtypeStruct((HEADS, PAD, length), B16),
            jax.ShapeDtypeStruct((length, D), F32),
            jax.ShapeDtypeStruct((D, D), B16),
            jax.ShapeDtypeStruct((D, hidden), B16),
            jax.ShapeDtypeStruct((hidden, D), B16),
            jax.ShapeDtypeStruct((40, WIDE), F32),
            jax.ShapeDtypeStruct((56, WIDE), F32),
        ],
        scratch_shapes=[
            pltpu.VMEM((D + 16, D), F32),
            pltpu.VMEM((WIDE, hidden), F32),
            pltpu.VMEM((hidden, D), F32),
            pltpu.VMEM((TOK, WIDE), F32),
            pltpu.VMEM((step, hidden), B16),
            pltpu.VMEM((step, hidden), F32),
        ],
        compiler_params=params(),
        name="feed_and_loss",
    )(mix, inverse, x, mask, targets, counted, vec, vectors[:, 9 * D :], final_norm, head_t,
      w_out, w_up, w_down, q_t, qd_t)

    own_rest = lax.psum_scatter(
        jnp.concatenate([g_out, g_up], 1), "grp", scatter_dimension=0, tiled=True
    )
    own_down = lax.psum_scatter(g_down, "grp", scatter_dimension=0, tiled=True)

    pair = 2
    two = pl.BlockSpec((pair, PAD, length), lambda i: (i, 0, 0))
    grad_act = pl.pallas_call(
        attend_back_kernel,
        grid=(HEADS // pair,),
        in_specs=[
            pl.BlockSpec((pair, length, length), lambda i: (i, 0, 0)),
            two, two, two, two, whole((HDIM, length)), whole((HDIM, length)),
        ],
        out_specs=pl.BlockSpec((3, pair * HDIM, length), lambda i: (0, i, 0)),
        out_shape=jax.ShapeDtypeStruct((3, D, length), B16),
        compiler_params=params(),
        name="attend_back",
    )(probs, query, keys, value, grad_mix, cosine, sine)

    g_in, shared = pl.pallas_call(
        input_kernel,
        grid=(steps,),
        in_specs=[
            cols, pl.BlockSpec((3, D, step), lambda i: (0, 0, i)),
            pl.BlockSpec((D + 16, step), lambda i: (0, i)), flat, flat, whole((D, 3 * D)),
            whole(vec.shape), whole((8, wide)), whole((40, WIDE)), whole((40, WIDE)), whole((56, WIDE)),
        ],
        out_specs=[whole((D, 3 * D)), whole((160, WIDE))],
        out_shape=[jax.ShapeDtypeStruct((D, 3 * D), B16), jax.ShapeDtypeStruct((160, WIDE), F32)],
        scratch_shapes=[pltpu.VMEM((D + 16, 3 * D), F32), pltpu.VMEM((TOK, D), F32)],
        compiler_params=params(),
        name="input_grads",
    )(tokens, grad_act, h_t, x, grad_mid, w_in, vec, q_t, sketch, err_sketch, early)

    own_in = lax.psum_scatter(g_in, "grp", scatter_dimension=0, tiled=True)
    shared = add_all(shared)

    basis, own, factor = pl.pallas_call(
        factor_kernel,
        grid_spec=prefetch(
            (1,),
            [
                whole((160, WIDE)), whole((D, 3 * D)), whole((D, D)), whole((D, hidden)), whole((hidden, D)),
                whole((rows, wide)), whole((rows_down, D)),
            ],
            [whole((40, WIDE)), whole((16, WIDE)), whole((16, wide))],
            [pltpu.VMEM((8, WIDE), F32)],
        ),
        out_shape=[
            jax.ShapeDtypeStruct((40, WIDE), F32),
            jax.ShapeDtypeStruct((16, WIDE), F32),
            jax.ShapeDtypeStruct((16, wide), F32),
        ],
        compiler_params=params(),
        name="left_factors",
    )(group, shared, g_in, g_out, g_up, g_down, err, errd)

    packed = add_all(jnp.concatenate([factor[0:8], factor[8:16, 0:D]], 1))
    factor_wide, factor_down = packed[:, :wide], packed[:, wide:]
    factor = jnp.concatenate([factor_wide, jnp.pad(factor_down, ((0, 0), (0, wide - D)))], 0)

    same = lambda value: jax.ShapeDtypeStruct(value.shape, F32)
    replicas = lax.axis_size("rep")
    small = (vec, vec_mom.reshape(-1, D), final_norm, final_mom, embed, embed_mom, head_t, head_mom.T)
    outs = pl.pallas_call(
        partial(finish_kernel, replicas),
        out_shape=[
            jax.ShapeDtypeStruct((8, 128), F32),
            same(mats_d[0]), same(mats_down[0]), same(mats_d[0]), same(mats_down[0]),
            same(err), same(errd),
        ]
        + [same(item) for item in small],
        compiler_params=params(),
        name="finish",
    )(shared, basis, own, factor, own_in, own_rest, own_down,
      mats_d[0], mats_down[0], mom_d[0], mom_down[0], err, errd, *small)
    (norm, new_wide, new_down, new_mom_wide, new_mom_dn, new_err, new_errd,
     new_vec, new_vmom, new_fin, new_fmom, new_emb, new_emom, new_head, new_hmom) = outs
    return (
        shared[58, 0],
        counted[0, 0],
        norm[0, 0],
        new_wide[None],
        new_down[None],
        new_mom_wide[None],
        new_mom_dn[None],
        new_err[None, None],
        new_errd[None, None],
        own[0:8, :rows].T[None],
        own[8:16, :rows_down].T[None],
        factor_wide.T[None],
        factor_down.T[None],
        new_vec.reshape(1, -1),
        new_vmom.reshape(1, -1),
        new_fin,
        new_fmom,
        new_emb,
        new_emom,
        new_head.T,
        new_hmom.T,
    )


def solution(mesh):
    whole_seq = P(("rep", "grp"), None)
    by_rows = P(None, "grp", None)
    by_replica = P("rep", None, "grp", None)
    placed = (
        (whole_seq,) * 3 + (by_rows,) * 4 + (by_replica,) * 2 + (P(),) * 10
    )
    given = (P(),) * 3 + (by_rows,) * 4 + (by_replica,) * 2 + (by_rows,) * 2 + (P(),) * 10
    return jax.shard_map(shards, mesh=mesh, in_specs=placed, out_specs=given, check_vma=False)
```

```python
from functools import partial

import jax
import jax.numpy as jnp
import numpy as np
from jax import lax
from jax.experimental import pallas as pl
from jax.experimental.pallas import tpu as pltpu
from jax.sharding import PartitionSpec as P

D = 480
HEADS = 20
HDIM = 24
V = 33
PAD = 32
TOK = 40
WIDE = 512
EPS = 1e-05
BETA = 0.9
RATE_WIDE = 20000.0
RATE_LOWER = 3000.0
RATE_VECTOR = 20000.0
RATE_FINAL = 40000.0
RATE_EMBED = 60000.0
RATE_HEAD = 3000.0
CLIP = 0.005
F32 = jnp.float32
B16 = jnp.bfloat16
MIB = 2**20


def params(limit=56):
    return pltpu.CompilerParams(vmem_limit_bytes=limit * MIB)


def nn(left, right):
    return jnp.dot(left, right, preferred_element_type=F32)


def nt(left, right):
    return lax.dot_general(left, right, (((1,), (1,)), ((), ())), preferred_element_type=F32)


def tn(left, right):
    return lax.dot_general(left, right, (((0,), (0,)), ((), ())), preferred_element_type=F32)


def thirds(value):
    top = value.astype(B16)
    rest = value - top.astype(F32)
    middle = rest.astype(B16)
    return top, middle, (rest - middle.astype(F32)).astype(B16)


def thirds_rows(value):
    return jnp.concatenate([part.astype(F32) for part in thirds(value)], 0).astype(B16)


def fold_rows(value):
    return value[0:8] + value[8:16] + value[16:24]


def exact_nt(left, right):
    return lax.dot_general(
        left, right, (((1,), (1,)), ((), ())),
        precision=lax.Precision.HIGHEST, preferred_element_type=F32,
    )


def exact_nn(left, right):
    return jnp.dot(left, right, precision=lax.Precision.HIGHEST, preferred_element_type=F32)


def norm_parts(value):
    center = value - jnp.mean(value, -1, keepdims=True)
    spread = jnp.mean(center * center, -1, keepdims=True)
    rstd = lax.rsqrt(spread + EPS)
    return center * rstd, rstd


def norm_back(grad, unit, rstd, gain):
    inner = grad * gain
    first = jnp.mean(inner, -1, keepdims=True)
    second = jnp.mean(inner * unit, -1, keepdims=True)
    return (
        rstd * (inner - first - unit * second),
        jnp.sum(grad * unit, 0, keepdims=True),
        jnp.sum(grad, 0, keepdims=True),
    )


def half_turn(value):
    return jnp.concatenate([value[HDIM // 2 :], value[: HDIM // 2]], 0)


def tail(rows, cols, ones):
    index = lax.broadcasted_iota(jnp.int32, (rows, cols), 0)
    return jnp.where(index < ones, 1.0, 0.0).astype(F32)


def lane_tail(rows, cols):
    index = lax.broadcasted_iota(jnp.int32, (rows, cols), 1)
    return jnp.where(index == 0, 1.0, 0.0).astype(F32)


def tables(length):
    half = HDIM // 2
    freq = np.float32(10000.0) ** (-np.arange(half, dtype=np.float32) * np.float32(2.0) / np.float32(HDIM))
    angle = np.arange(length, dtype=np.float32)[None, :] * freq.astype(np.float32)[:, None]
    cosine, sine = np.cos(angle), np.sin(angle)
    return (
        jnp.asarray(np.concatenate([cosine, cosine], 0), F32),
        jnp.asarray(np.concatenate([-sine, sine], 0), F32),
    )


def error_kernel(group, err_ref, errd_ref, q_ref, qd_ref, out_ref, row_ref):
    rows = err_ref.shape[0]
    out_ref[...] = jnp.zeros_like(out_ref)
    row_ref[...] = jnp.zeros_like(row_ref)
    row_ref[:, 0:rows] = exact_nt(q_ref[...], err_ref[...])
    out_ref[0:8, :] = pltpu.roll(row_ref[...], rows * group[0], 1)
    start = pl.multiple_of(8 + 8 * group[0], 8)
    out_ref[pl.ds(start, 8), 0:D] = exact_nt(qd_ref[...], errd_ref[...])


def embed_kernel(tok_ref, emb_ref, w_ref, vec_ref, cos_ref, sin_ref,
                 x_ref, h_ref, q_ref, k_ref, v_ref, emb_s):
    step = tok_ref.shape[1]

    @pl.when(pl.program_id(0) == 0)
    def _():
        emb_s[...] = jnp.zeros_like(emb_s)
        emb_s[0:V, :] = emb_ref[...]

    index = lax.broadcasted_iota(jnp.int32, (TOK, step), 0)
    hot = jnp.where(index == tok_ref[...], 1.0, 0.0).astype(F32)
    hot = jnp.concatenate([hot, hot, hot], 0).astype(B16)
    x = tn(hot, thirds_rows(emb_s[...]))
    x_ref[...] = x
    unit, _ = norm_parts(x)
    normed = unit * vec_ref[:, 0:D] + vec_ref[:, D : 2 * D]
    act = nn(normed.astype(B16), w_ref[...]) + vec_ref[:, 2 * D : 5 * D]
    h_ref[...] = jnp.concatenate([normed.T, tail(16, step, 1)], 0).astype(B16)
    turned = act.T
    cosine, sine = cos_ref[...], sin_ref[...]
    zeros = tail(PAD - HDIM, step, 0)
    ones = tail(PAD - HDIM, step, 3)
    for head in range(HEADS):
        low = HDIM * head
        query = turned[low : low + HDIM]
        query = (query * cosine + half_turn(query) * sine) * HDIM ** (-0.5)
        q_ref[head] = jnp.concatenate([query, zeros], 0).astype(B16)
        keys = turned[D + low : D + low + HDIM]
        keys = keys * cosine + half_turn(keys) * sine
        k_ref[head] = jnp.concatenate([keys, zeros], 0).astype(B16)
        value = turned[2 * D + low : 2 * D + low + HDIM]
        v_ref[head] = jnp.concatenate([value, ones], 0).astype(B16)


def rows_of(value):
    return value.astype(F32).T.astype(B16)


def attend_kernel(q_ref, k_ref, v_ref, mix_ref, inv_ref, p_ref):
    scores = nn(rows_of(k_ref[0]), q_ref[0])
    top = jnp.max(scores, 0, keepdims=True)
    probs = jnp.exp(scores - top).astype(B16)
    p_ref[0] = probs
    out = nn(v_ref[0], probs)
    inverse = 1.0 / out[HDIM : HDIM + 1]
    mix_ref[...] = out[0:HDIM] * inverse
    inv_ref[0] = inverse


def gelu_parts(upper):
    size = jnp.abs(upper) * (0.5**0.5)
    bell = jnp.exp(-0.5 * upper * upper)
    t = 1.0 / (1.0 + 0.3275911 * size)
    poly = t * (0.254829592 + t * (-0.284496736 + t * (1.421413741 + t * (-1.453152027 + t * 1.061405429))))
    lower = 0.5 * poly * bell
    cdf = jnp.where(upper < 0, lower, 1.0 - lower)
    return upper * cdf, cdf + upper * (0.3989422804014327 * bell)


def middle_kernel(mixa_ref, mixb_ref, inva_ref, invb_ref, x_ref, mask_ref, tgt_ref, count_ref, vec_ref, fin_ref,
                  head_ref, wr_ref, wd_ref, q_ref, qd_ref,
                  dm_ref, dx_ref, gr_ref, gd_ref, s_ref, e_ref,
                  acc_o, acc_u, acc_d, head_s, hid_s, slope_s):
    pid = pl.program_id(0)
    step = x_ref.shape[0]
    wide = wd_ref.shape[0]
    wo = slice(wide, wide + D)

    @pl.when(pid == 0)
    def _():
        acc_o[...] = jnp.zeros_like(acc_o)
        acc_u[...] = jnp.zeros_like(acc_u)
        acc_d[...] = jnp.zeros_like(acc_d)
        e_ref[...] = jnp.zeros_like(e_ref)
        s_ref[...] = jnp.zeros_like(s_ref)
        head_s[...] = jnp.zeros_like(head_s)
        head_s[0:V, 0 : D + 1] = head_ref[...]

    mix = jnp.concatenate([mixa_ref[...], mixb_ref[...]], 0)
    half = inva_ref.shape[0]
    mixed = jnp.concatenate([mix, tail(16, step, 1)], 0).astype(B16)
    middle = x_ref[...] + tn(mixed[0:D], wr_ref[:, wo]) + vec_ref[:, 5 * D : 6 * D]
    unit2, rstd2 = norm_parts(middle)
    gain2 = vec_ref[:, 6 * D : 7 * D]
    normed2 = unit2 * gain2 + vec_ref[:, 7 * D : 8 * D]
    normed2 = jnp.concatenate([normed2, lane_tail(step, WIDE - D)], 1).astype(B16)
    bias_up = vec_ref[:, 9 * D :]
    block = 384
    for low in range(0, wide, block):
        cut = slice(low, low + block)
        upper = nn(normed2[:, 0:D], wr_ref[:, cut]) + bias_up[:, cut]
        hidden, slope = gelu_parts(upper)
        hid_s[:, cut] = hidden.astype(B16)
        slope_s[:, cut] = slope
    resid = middle + nn(hid_s[...], wd_ref[...]) + vec_ref[:, 8 * D : 9 * D]
    unit3, rstd3 = norm_parts(resid)
    final = unit3 * fin_ref[0:1, :] + fin_ref[1:2, :]
    final = jnp.concatenate([final, lane_tail(step, WIDE - D)], 1).astype(B16)

    lanes = lax.broadcasted_iota(jnp.int32, (TOK, WIDE), 1)
    bias = jnp.sum(jnp.where(lanes == D, head_s[...], 0.0), 1, keepdims=True)
    table = head_s[:, 0:D].astype(B16)
    rows = lax.broadcasted_iota(jnp.int32, (TOK, step), 0)
    logits = jnp.where(rows < V, nt(table, final[:, 0:D]) + bias, -1e30)
    shifted = logits - jnp.max(logits, 0, keepdims=True)
    expo = jnp.exp(shifted)
    total = jnp.sum(expo, 0, keepdims=True)
    picks = rows == tgt_ref[...]
    weight = mask_ref[...].astype(F32)
    picked = jnp.sum(jnp.where(picks, shifted, 0.0), 0, keepdims=True)
    loss = jnp.sum((jnp.log(total) - picked) * weight, 1, keepdims=True)
    grad_logits = (expo / total - jnp.where(picks, 1.0, 0.0)) * (weight * (1.0 / count_ref[...]))
    grad_logits = grad_logits.astype(B16)
    e_ref[16 : 16 + TOK, :] += nn(grad_logits, final)
    grad_resid, grad_fg, grad_fb = norm_back(tn(grad_logits, table), unit3, rstd3, fin_ref[0:1, :])

    grad_y = grad_resid.astype(B16)
    acc_d[...] += tn(hid_s[...], grad_y)
    for low in range(0, wide, block):
        cut = slice(low, low + block)
        grad_hidden = nt(grad_y, wd_ref[cut, :])
        hid_s[:, cut] = (grad_hidden * slope_s[:, cut]).astype(B16)
    acc_u[...] += tn(normed2, hid_s[...])
    grad_mid, grad_g2, grad_b2 = norm_back(nt(hid_s[...], wr_ref[:, 0:wide]), unit2, rstd2, gain2)
    grad_mid = grad_mid + grad_resid
    dx_ref[...] = grad_mid
    branch = grad_mid.astype(B16)
    acc_o[...] += nn(mixed, branch)
    grad_mixed = nt(wr_ref[:, wo], branch).astype(B16).astype(F32)
    zeros = tail(PAD - HDIM - 3, step, 0)
    for head in range(HEADS):
        cut = slice(HDIM * head, HDIM * head + HDIM)
        inverse = inva_ref[head] if head < half else invb_ref[head - half]
        scaled = (grad_mixed[cut] * inverse).astype(B16).astype(F32)
        delta = -jnp.sum(scaled * mix[cut], 0, keepdims=True)
        top, mid, low = thirds(delta)
        dm_ref[head] = jnp.concatenate(
            [scaled, top.astype(F32), mid.astype(F32), low.astype(F32), zeros], 0
        ).astype(B16)
    e_ref[1:2, 0:D] += grad_g2
    e_ref[2:3, 0:D] += grad_b2
    e_ref[3:4, 0:D] += jnp.sum(grad_y.astype(F32), 0, keepdims=True)
    e_ref[8:9, 0:D] += grad_fg
    e_ref[9:10, 0:D] += grad_fb
    e_ref[10:11, :] += jnp.broadcast_to(loss, (1, WIDE))

    @pl.when(pid == pl.num_programs(0) - 1)
    def _():
        e_ref[0:1, 0:D] = acc_o[D : D + 1, :]
        for part in range(wide // D):
            e_ref[4 + part : 5 + part, 0:D] = acc_u[D : D + 1, D * part : D * part + D]
        go = acc_o[0:D, :].astype(B16)
        gu = acc_u[0:D, :].astype(B16)
        gr_ref[:, 0:wide] = gu
        gr_ref[:, wo] = go
        gd_ref[...] = acc_d[...].astype(B16)
        sketch = nt(thirds_rows(q_ref[:, 3 * D : 4 * D]), go) + nt(thirds_rows(q_ref[:, 4 * D :]), gu)
        s_ref[0:8, 0:D] = fold_rows(sketch)
        start = thirds_rows(qd_ref[...])
        for part in range(wide // D):
            piece = nt(start, gd_ref[D * part : D * part + D, :])
            s_ref[8 + 8 * part : 16 + 8 * part, 0:D] = fold_rows(piece)


def attend_back_kernel(p_ref, q_ref, k_ref, v_ref, dm_ref, cos_ref, sin_ref, da_ref):
    cosine, sine = cos_ref[...], sin_ref[...]
    parts = [[], [], []]
    for head in range(p_ref.shape[0]):
        probs = p_ref[head]
        grad = dm_ref[head]
        slope = nn(rows_of(v_ref[head]), grad)
        grad_scores = (probs.astype(F32) * slope).astype(B16)
        grad_value = nt(grad, probs)[0:HDIM]
        grad_keys = nt(q_ref[head], grad_scores)[0:HDIM]
        grad_query = nn(k_ref[head], grad_scores)[0:HDIM] * HDIM ** (-0.5)
        parts[0].append(grad_query * cosine + half_turn(grad_query * sine))
        parts[1].append(grad_keys * cosine + half_turn(grad_keys * sine))
        parts[2].append(grad_value)
    for index in range(3):
        da_ref[index] = jnp.concatenate(parts[index], 0).astype(B16)


def input_kernel(group, tok_ref, daa_ref, dab_ref, h_ref, x_ref, dx_ref, w_ref, vec_ref, q_ref, s_ref, serr_ref, e_ref,
                 g_ref, *rest):
    *out_refs, out_ref, acc_w, acc_e = rest
    pid = pl.program_id(0)
    step = x_ref.shape[0]

    @pl.when(pid == 0)
    def _():
        acc_w[...] = jnp.zeros_like(acc_w)
        acc_e[...] = jnp.zeros_like(acc_e)
        out_ref[...] = jnp.zeros_like(out_ref)

    da = jnp.concatenate([ref[part] for part in range(3) for ref in (daa_ref, dab_ref)], 0)
    acc_w[...] += nt(h_ref[...], da)
    grad = nn(w_ref[...], da).T
    unit, rstd = norm_parts(x_ref[...])
    grad_x, grad_g, grad_b = norm_back(grad, unit, rstd, vec_ref[:, 0:D])
    grad_x = grad_x + dx_ref[...]
    index = lax.broadcasted_iota(jnp.int32, (TOK, step), 0)
    hot = jnp.where(index == tok_ref[...], 1.0, 0.0).astype(B16)
    for part in thirds(grad_x):
        acc_e[...] += nn(hot, part)
    out_ref[40:41, 0:D] += grad_g
    out_ref[41:42, 0:D] += grad_b

    @pl.when(pid == pl.num_programs(0) - 1)
    def _():
        for part in range(3):
            out_ref[42 + part : 43 + part, 0:D] = acc_w[D : D + 1, D * part : D * part + D]
        g = acc_w[0:D, :].astype(B16)
        g_ref[...] = g
        out_ref[0:40, :] = s_ref[...] + serr_ref[...]
        out_ref[0:8, 0:D] += fold_rows(nt(thirds_rows(q_ref[:, 0 : 3 * D]), g))
        out_ref[45:48, :] = e_ref[8:11, :]
        out_ref[48:56, :] = e_ref[0:8, :]
        out_ref[56 : 56 + V, 0:D] = acc_e[0:V, :]
        out_ref[56 + V : 56 + 2 * V, :] = e_ref[16 : 16 + V, :]
        size = out_refs[0].shape[0]
        for place, ref in enumerate(out_refs):
            ref[...] = out_ref[pl.ds(pl.multiple_of((group[0] ^ place) * size, 8), size), :]


def orthonormal(sketch, gram):
    basis = jnp.zeros_like(sketch[0])
    count = gram.shape[0]
    index = lax.broadcasted_iota(jnp.int32, (count, 1), 0)
    out = [jnp.zeros_like(part) for part in sketch]
    left = list(sketch)
    for step in range(count):
        pivot = gram[step : step + 1, step : step + 1]
        scale = 1.0 / jnp.sqrt(pivot)
        column = gram[:, step : step + 1] * scale
        row = gram[step : step + 1, :] * scale
        column = jnp.where(index > step, column, 0.0)
        gram = gram - column * row
        for place in range(len(left)):
            base = left[place][step : step + 1, :] * scale
            out[place] = jnp.where(index == step, base, out[place])
            left[place] = left[place] - column * base
    return out


def factor_kernel(group, *refs):
    count = (len(refs) - 10) // 2
    chunks, rest = refs[:count], refs[count:]
    gi_ref, gr_ref, gd_ref, err_ref, errd_ref, a_ref, p_ref, own_ref, ownd_ref = rest[:9]
    out_refs, f_s = rest[9:-1], rest[-1]
    rows, wide_cols = err_ref.shape
    parts = gd_ref.shape[0] // D
    hidden = gd_ref.shape[0]
    size = chunks[0].shape[0]
    for place, ref in enumerate(chunks):
        a_ref[pl.ds(pl.multiple_of((group[0] ^ place) * size, 8), size), :] = ref[...]
    wide = a_ref[0:8, 0:D]
    down = [a_ref[8 + 8 * part : 16 + 8 * part, 0:D] for part in range(parts)]
    gram = exact_nt(wide, wide)
    (wide,) = orthonormal([wide], gram)
    gram = exact_nt(down[0], down[0])
    for part in range(1, parts):
        gram = gram + exact_nt(down[part], down[part])
    down = orthonormal(down, gram)
    p_ref[...] = jnp.zeros_like(p_ref)
    p_ref[0:8, 0:D] = wide
    for part in range(parts):
        p_ref[8 + 8 * part : 16 + 8 * part, 0:D] = down[part]
    own = pltpu.roll(p_ref[0:8, :], (WIDE - rows * group[0]) % WIDE, 1)[:, 0:rows]
    own_down = p_ref[pl.ds(pl.multiple_of(8 + 8 * group[0], 8), 8), :][:, 0:D]
    own_ref[...] = own
    ownd_ref[...] = own_down
    three = thirds_rows(wide)
    f_s[...] = jnp.zeros_like(f_s)
    f_s[:, 0:wide_cols] = exact_nn(own, err_ref[...])
    f_s[:, 0 : 3 * D] += fold_rows(nn(three, gi_ref[...]))
    f_s[:, 4 * D : 4 * D + hidden] += fold_rows(nn(three, gr_ref[:, 0:hidden]))
    f_s[:, 3 * D : 4 * D] += fold_rows(nn(three, gr_ref[:, hidden:]))
    total = exact_nn(own_down, errd_ref[...])
    for part in range(parts):
        total = total + fold_rows(nn(thirds_rows(down[part]), gd_ref[D * part : D * part + D, :]))
    f_s[:, wide_cols : wide_cols + D] = total
    size = out_refs[0].shape[1]
    for place, ref in enumerate(out_refs):
        ref[...] = f_s[:, pl.ds(pl.multiple_of((group[0] ^ place) * size, 128), size)]


def six(left, right):
    first, second = thirds(left), thirds(right)
    order = ((0, 0), (0, 1), (1, 0), (1, 1), (0, 2), (2, 0))
    left = jnp.concatenate([first[i].astype(F32) for i, _ in order], 0).astype(B16)
    right = jnp.concatenate([second[j].astype(F32) for _, j in order], 0).astype(B16)
    return tn(left, right)


def renew(weight, moment, grad, scale, rate):
    new_moment = BETA * moment + scale * grad
    return weight - rate * new_moment, new_moment


def finish_kernel(replicas, group, *refs):
    count = len(refs) - 39
    chunks, rest = refs[:count], refs[count:]
    (a_ref, p_ref, own_ref, ownd_ref, gi_ref, gr_ref, gd_ref,
     w_ref, wd_ref, m_ref, md_ref, err_ref, errd_ref,
     vec_ref, vmom_ref, fin_ref, fmom_ref, emb_ref, emom_ref, head_ref, hmom_ref,
     norm_ref, nq_ref, nqd_ref, nw_ref, nwd_ref, nm_ref, nmd_ref, ne_ref, ned_ref,
     nvec_ref, nvmom_ref, nfin_ref, nfmom_ref, nemb_ref, nemom_ref, nhead_ref, nhmom_ref, f_s) = rest
    wide_cols = err_ref.shape[1]
    hidden = wide_cols - 4 * D
    size = chunks[0].shape[1]
    for place, ref in enumerate(chunks):
        f_s[:, pl.ds(pl.multiple_of((group[0] ^ place) * size, 128), size)] = ref[...]
    factor, factor_down = f_s[:, 0:wide_cols], f_s[:, wide_cols : wide_cols + D]
    nq_ref[...] = factor
    nqd_ref[...] = factor_down
    a = a_ref[...]
    square = jnp.sum(a[40:47, 0:D] * a[40:47, 0:D]) + jnp.sum(a[48:56, 0:D] * a[48:56, 0:D])
    emb, top = a[56 : 56 + V, 0:D], a[56 + V : 56 + 2 * V, 0 : D + 1]
    square = square + jnp.sum(emb * emb) + jnp.sum(top * top)
    basis = p_ref[...]
    gram = exact_nt(basis[0:8, 0:D], basis[0:8, 0:D])
    square = square + jnp.sum(gram * exact_nt(factor, factor))
    gram = jnp.zeros((8, 8), F32)
    for part in range(1, basis.shape[0] // 8):
        piece = basis[8 * part : 8 * part + 8, 0:D]
        gram = gram + exact_nt(piece, piece)
    square = square + jnp.sum(gram * exact_nt(factor_down, factor_down))
    norm = jnp.sqrt(square)
    norm_ref[...] = jnp.broadcast_to(norm, norm_ref.shape)
    scale = jnp.minimum(1.0, CLIP / norm)

    approx = six(own_ref[...], factor)
    nw_ref[...], nm_ref[...] = renew(w_ref[...], m_ref[...], approx, scale, RATE_WIDE)
    share = approx * (1.0 / replicas)
    for cut, ref, start in (
        (slice(0, 3 * D), gi_ref, 0), (slice(3 * D, 4 * D), gr_ref, hidden), (slice(4 * D, wide_cols), gr_ref, 0),
    ):
        size = cut.stop - cut.start
        ne_ref[:, cut] = ref[:, start : start + size].astype(F32) + err_ref[:, cut] - share[:, cut]
    approx = six(ownd_ref[...], factor_down)
    nwd_ref[...], nmd_ref[...] = renew(wd_ref[...], md_ref[...], approx, scale, RATE_LOWER)
    ned_ref[...] = gd_ref[...].astype(F32) + errd_ref[...] - approx * (1.0 / replicas)

    places = (40, 41, 42, 43, 44, 48, 49, 50, 51, 52, 53, 54, 55)
    for row, place in enumerate(places):
        cut = slice(D * row, D * row + D)
        nvec_ref[:, cut], nvmom_ref[:, cut] = renew(
            vec_ref[:, cut], vmom_ref[:, cut], a[place : place + 1, 0:D], scale, RATE_VECTOR
        )
    nfin_ref[...], nfmom_ref[...] = renew(fin_ref[...], fmom_ref[...], a[45:47, 0:D], scale, RATE_FINAL)
    nemb_ref[...], nemom_ref[...] = renew(emb_ref[...], emom_ref[...], emb, scale, RATE_EMBED)
    nhead_ref[...], nhmom_ref[...] = renew(head_ref[...], hmom_ref[...], top, scale, RATE_HEAD)


def swap(value, axis, bit):
    size = lax.axis_size(axis)
    return lax.ppermute(value, axis, [(i, i ^ bit) for i in range(size)])


def bits_of(axis):
    size, bit, out = lax.axis_size(axis), 1, []
    while bit < size:
        out.append(bit)
        bit *= 2
    return out


def tie(*values):
    return lax.optimization_barrier(values)


def add_chunks(pieces):
    got = [swap(piece, "grp", place) for place, piece in enumerate(pieces) if place]
    total = pieces[0]
    for piece in got:
        total = total + piece
    for bit in bits_of("rep"):
        total = total + swap(total, "rep", bit)
    return [total] + [swap(total, "grp", place) for place in range(1, len(pieces))]


def whole(shape):
    return pl.BlockSpec(shape, lambda *_: (0,) * len(shape))


def shards(tokens, mask, targets, mats_d, mats_down, mom_d, mom_down, err_d, err_down, q_d, q_down,
           vectors, vec_mom, final_norm, final_mom, embed, embed_mom, head, head_mom):
    length = tokens.shape[1]
    wide = mats_d.shape[2]
    hidden = wide - 4 * D
    rows = mats_d.shape[1]
    rows_down = mats_down.shape[1]
    step = 256
    steps = length // step
    index = lax.axis_index("grp").astype(jnp.int32)
    group = index.reshape(1)
    members = lax.axis_size("grp")
    cosine, sine = tables(length)
    q_t, qd_t = q_d[0].T, q_down[0].T
    head_t = head.T
    err, errd = err_d[0, 0], err_down[0, 0]

    def call(kernel, name, grid, ins, outs, shapes, scratch=()):
        return pl.pallas_call(
            kernel,
            grid_spec=pltpu.PrefetchScalarGridSpec(
                num_scalar_prefetch=1, grid=grid, in_specs=ins, out_specs=outs, scratch_shapes=scratch
            ),
            out_shape=shapes,
            compiler_params=params(),
            name=name,
        )

    shape = jax.ShapeDtypeStruct
    rounds = [("grp", bit) for bit in bits_of("grp")] + [("rep", bit) for bit in bits_of("rep")]

    def advance(value, times=1):
        for _ in range(min(times, len(rounds))):
            value = value + swap(value, *rounds.pop(0))
        return value

    wide16 = mats_d[0].astype(B16)
    w_in = wide16[None, :, : 3 * D]
    counted = jnp.broadcast_to(jnp.sum(mask.astype(F32)), (8, 128))
    for turn, bit in enumerate(reversed(bits_of("grp"))):
        other = swap(w_in, "grp", bit)
        more = advance(counted)
        if turn == 0:
            err_sketch = call(
                error_kernel, "error_sketch", (1,),
                [whole((rows, wide)), whole((rows_down, D)), whole((8, wide)), whole((8, D))],
                whole((40, WIDE)), shape((40, WIDE), F32), [pltpu.VMEM((8, WIDE), F32)],
            )(group, err, errd, q_t, qd_t)
            other, more, err_sketch = tie(other, more, err_sketch)
        else:
            other, more = tie(other, more)
        counted = more
        mine = (index & bit) == 0
        w_in = jnp.stack([jnp.where(mine, w_in, other), jnp.where(mine, other, w_in)], -3)
    w_in = w_in.reshape(-1, 3 * D)
    w_rest = lax.all_gather(
        jnp.concatenate([wide16[:, 4 * D :], wide16[:, 3 * D : 4 * D]], 1), "grp", axis=0, tiled=True
    )
    w_down = lax.all_gather(mats_down[0].astype(B16), "grp", axis=0, tiled=True)

    cols = pl.BlockSpec((1, step), lambda i, *_: (0, i))
    flat = pl.BlockSpec((step, D), lambda i, *_: (i, 0))
    heads = pl.BlockSpec((HEADS, PAD, step), lambda i, *_: (0, 0, i))
    wave = pl.BlockSpec((HDIM, step), lambda i, *_: (0, i))
    ext = pl.BlockSpec((D + 16, step), lambda i, *_: (0, i))
    more = advance(counted)
    x, h_t, query, keys, value = pl.pallas_call(
        embed_kernel,
        grid=(steps,),
        in_specs=[cols, whole((V, D)), whole((D, 3 * D)), whole(vectors.shape), wave, wave],
        out_specs=[flat, ext, heads, heads, heads],
        out_shape=[shape((length, D), F32), shape((D + 16, length), B16)]
        + [shape((HEADS, PAD, length), B16)] * 3,
        scratch_shapes=[pltpu.VMEM((TOK, D), F32)],
        compiler_params=params(),
        name="embed_project",
    )(tokens, embed, w_in, vectors, cosine, sine)
    query, counted = tie(query, more)

    half = HEADS // 2
    mixes, inverses, probs = [], [], []
    for part in range(2):
        one = pl.BlockSpec((1, PAD, length), lambda i, part=part: (i + half * part, 0, 0))
        more = advance(counted, 1 + part * len(rounds))
        mix, inverse, prob = pl.pallas_call(
            attend_kernel,
            grid=(half,),
            in_specs=[one, one, one],
            out_specs=[
                pl.BlockSpec((HDIM, length), lambda i: (i, 0)),
                pl.BlockSpec((1, 1, length), lambda i: (i, 0, 0)),
                pl.BlockSpec((1, length, length), lambda i: (i, 0, 0)),
            ],
            out_shape=[
                shape((half * HDIM, length), F32),
                shape((half, 1, length), F32),
                shape((half, length, length), B16),
            ],
            compiler_params=params(),
            name="attend",
        )(query, keys, value)
        mix, query, counted = tie(mix, query, more)
        mixes.append(mix)
        inverses.append(inverse)
        probs.append(prob)
    counted = counted[0:1, 0:1]

    grad_mix, grad_mid, g_rest, g_down, sketch, early = pl.pallas_call(
        middle_kernel,
        grid=(steps,),
        in_specs=[pl.BlockSpec((half * HDIM, step), lambda i: (0, i))] * 2
        + [pl.BlockSpec((half, 1, step), lambda i: (0, 0, i))] * 2
        + [
            flat, cols, cols, whole((1, 1)), whole(vectors.shape), whole((2, D)),
            whole((V, D + 1)), whole((D, D + hidden)), whole((hidden, D)),
            whole((8, wide)), whole((8, D)),
        ],
        out_specs=[
            heads, flat, whole((D, D + hidden)), whole((hidden, D)), whole((40, WIDE)), whole((56, WIDE)),
        ],
        out_shape=[
            shape((HEADS, PAD, length), B16),
            shape((length, D), F32),
            shape((D, D + hidden), B16),
            shape((hidden, D), B16),
            shape((40, WIDE), F32),
            shape((56, WIDE), F32),
        ],
        scratch_shapes=[
            pltpu.VMEM((D + 16, D), F32),
            pltpu.VMEM((WIDE, hidden), F32),
            pltpu.VMEM((hidden, D), F32),
            pltpu.VMEM((TOK, WIDE), F32),
            pltpu.VMEM((step, hidden), B16),
            pltpu.VMEM((step, hidden), F32),
        ],
        compiler_params=params(),
        name="feed_and_loss",
    )(*mixes, *inverses, x, mask, targets, counted, vectors, final_norm, head_t,
      w_rest, w_down, q_t, qd_t)

    scatter = partial(lax.psum_scatter, axis_name="grp", scatter_dimension=0, tiled=True)
    own_down = scatter(g_down)
    own_rest = scatter(g_rest)
    pair = 2
    turned = half // pair
    grad_acts = []
    for part in range(2):
        two = pl.BlockSpec((pair, PAD, length), lambda i, part=part: (i + turned * part, 0, 0))
        grad_act = pl.pallas_call(
            attend_back_kernel,
            grid=(turned,),
            in_specs=[
                pl.BlockSpec((pair, length, length), lambda i: (i, 0, 0)),
                two, two, two, two, whole((HDIM, length)), whole((HDIM, length)),
            ],
            out_specs=pl.BlockSpec((3, pair * HDIM, length), lambda i: (0, i, 0)),
            out_shape=shape((3, half * HDIM, length), B16),
            compiler_params=params(),
            name="attend_back",
        )(probs[part], query, keys, value, grad_mix, cosine, sine)
        if part == 0:
            own_down, grad_act, grad_mix = tie(own_down, grad_act, grad_mix)
        grad_acts.append(grad_act)

    act = pl.BlockSpec((3, half * HDIM, step), lambda i, *_: (0, 0, i))
    size = 128 // members
    g_in, *pieces = call(
        input_kernel, "input_grads", (steps,),
        [
            cols, act, act, ext, flat, flat, whole((D, 3 * D)),
            whole(vectors.shape), whole((8, wide)), whole((40, WIDE)), whole((40, WIDE)), whole((56, WIDE)),
        ],
        [whole((D, 3 * D))] + [whole((size, WIDE))] * members,
        [shape((D, 3 * D), B16)] + [shape((size, WIDE), F32)] * members,
        [pltpu.VMEM((128, WIDE), F32), pltpu.VMEM((D + 16, 3 * D), F32), pltpu.VMEM((TOK, D), F32)],
    )(group, tokens, *grad_acts, h_t, x, grad_mid, w_in, vectors, q_t, sketch, err_sketch, early)
    own_rest, *pieces = tie(own_rest, *pieces)
    own_in = scatter(g_in)

    chunks = add_chunks(pieces)
    span = -(-(wide + WIDE) // (128 * members)) * 128
    shared, basis, own, ownd, *pieces = call(
        factor_kernel, "left_factors", (1,),
        [whole((size, WIDE))] * members
        + [
            whole((D, 3 * D)), whole((D, D + hidden)), whole((hidden, D)),
            whole((rows, wide)), whole((rows_down, D)),
        ],
        [whole((128, WIDE)), whole((40, WIDE)), whole((8, rows)), whole((8, rows_down))]
        + [whole((8, span))] * members,
        [
            shape((128, WIDE), F32), shape((40, WIDE), F32), shape((8, rows), F32), shape((8, rows_down), F32),
        ]
        + [shape((8, span), F32)] * members,
        [pltpu.VMEM((8, span * members), F32)],
    )(group, *chunks, g_in, g_rest, g_down, err, errd)
    chunks = add_chunks(pieces)

    same = lambda value: shape(value.shape, F32)
    replicas = lax.axis_size("rep")
    small = (vectors, vec_mom, final_norm, final_mom, embed, embed_mom, head_t, head_mom.T)
    given = (
        *chunks, shared, basis, own, ownd, own_in, own_rest, own_down,
        mats_d[0], mats_down[0], mom_d[0], mom_down[0], err, errd, *small,
    )
    shapes = [
        shape((8, 128), F32), shape((8, wide), F32), shape((8, D), F32),
        same(mats_d[0]), same(mats_down[0]), same(mats_d[0]), same(mats_down[0]), same(err), same(errd),
    ] + [same(item) for item in small]
    outs = call(
        partial(finish_kernel, replicas), "finish", (1,),
        [whole(item.shape) for item in given], [whole(item.shape) for item in shapes], shapes,
        [pltpu.VMEM((8, span * members), F32)],
    )(group, *given)
    (norm, new_q, new_qd, new_wide, new_down, new_mom_wide, new_mom_dn, new_err, new_errd,
     new_vec, new_vmom, new_fin, new_fmom, new_emb, new_emom, new_head, new_hmom) = outs
    return (
        shared[47, 0],
        counted[0, 0],
        norm[0, 0],
        new_wide[None],
        new_down[None],
        new_mom_wide[None],
        new_mom_dn[None],
        new_err[None, None],
        new_errd[None, None],
        own.T[None],
        ownd.T[None],
        new_q.T[None],
        new_qd.T[None],
        new_vec,
        new_vmom,
        new_fin,
        new_fmom,
        new_emb,
        new_emom,
        new_head.T,
        new_hmom.T,
    )


def solution(mesh):
    whole_seq = P(("rep", "grp"), None)
    by_rows = P(None, "grp", None)
    by_replica = P("rep", None, "grp", None)
    placed = (
        (whole_seq,) * 3 + (by_rows,) * 4 + (by_replica,) * 2 + (P(),) * 10
    )
    given = (P(),) * 3 + (by_rows,) * 4 + (by_replica,) * 2 + (by_rows,) * 2 + (P(),) * 10
    return jax.shard_map(shards, mesh=mesh, in_specs=placed, out_specs=given, check_vma=False)
```

```python
from functools import partial

import jax
import jax.numpy as jnp
import numpy as np
from jax import lax
from jax.experimental import pallas as pl
from jax.experimental.pallas import tpu as pltpu
from jax.sharding import PartitionSpec as P

D = 480
HEADS = 20
HDIM = 24
V = 33
PAD = 32
TOK = 40
WIDE = 512
EPS = 1e-05
BETA = 0.9
RATE_WIDE = 20000.0
RATE_LOWER = 3000.0
RATE_VECTOR = 20000.0
RATE_FINAL = 40000.0
RATE_EMBED = 60000.0
RATE_HEAD = 3000.0
CLIP = 0.005
F32 = jnp.float32
B16 = jnp.bfloat16
MIB = 2**20


def params(limit=56):
    return pltpu.CompilerParams(vmem_limit_bytes=limit * MIB)


def nn(left, right):
    return jnp.dot(left, right, preferred_element_type=F32)


def nt(left, right):
    return lax.dot_general(left, right, (((1,), (1,)), ((), ())), preferred_element_type=F32)


def tn(left, right):
    return lax.dot_general(left, right, (((0,), (0,)), ((), ())), preferred_element_type=F32)


def thirds(value):
    top = value.astype(B16)
    rest = value - top.astype(F32)
    middle = rest.astype(B16)
    return top, middle, (rest - middle.astype(F32)).astype(B16)


def thirds_rows(value):
    return jnp.concatenate([part.astype(F32) for part in thirds(value)], 0).astype(B16)


def fold_rows(value):
    return value[0:8] + value[8:16] + value[16:24]


def exact_nt(left, right):
    return lax.dot_general(
        left, right, (((1,), (1,)), ((), ())),
        precision=lax.Precision.HIGHEST, preferred_element_type=F32,
    )


def exact_nn(left, right):
    return jnp.dot(left, right, precision=lax.Precision.HIGHEST, preferred_element_type=F32)


def norm_parts(value):
    center = value - jnp.mean(value, -1, keepdims=True)
    spread = jnp.mean(center * center, -1, keepdims=True)
    rstd = lax.rsqrt(spread + EPS)
    return center * rstd, rstd


def norm_back(grad, unit, rstd, gain):
    inner = grad * gain
    first = jnp.mean(inner, -1, keepdims=True)
    second = jnp.mean(inner * unit, -1, keepdims=True)
    return (
        rstd * (inner - first - unit * second),
        jnp.sum(grad * unit, 0, keepdims=True),
        jnp.sum(grad, 0, keepdims=True),
    )


def half_turn(value):
    return jnp.concatenate([value[HDIM // 2 :], value[: HDIM // 2]], 0)


def tail(rows, cols, ones):
    index = lax.broadcasted_iota(jnp.int32, (rows, cols), 0)
    return jnp.where(index < ones, 1.0, 0.0).astype(F32)


def lane_tail(rows, cols):
    index = lax.broadcasted_iota(jnp.int32, (rows, cols), 1)
    return jnp.where(index == 0, 1.0, 0.0).astype(F32)


def tables(length):
    half = HDIM // 2
    freq = np.float32(10000.0) ** (-np.arange(half, dtype=np.float32) * np.float32(2.0) / np.float32(HDIM))
    angle = np.arange(length, dtype=np.float32)[None, :] * freq.astype(np.float32)[:, None]
    cosine, sine = np.cos(angle), np.sin(angle)
    return (
        jnp.asarray(np.concatenate([cosine, cosine], 0), F32),
        jnp.asarray(np.concatenate([-sine, sine], 0), F32),
    )


def error_kernel(group, err_ref, errd_ref, q_ref, qd_ref, out_ref, row_ref):
    rows = err_ref.shape[0]
    out_ref[...] = jnp.zeros_like(out_ref)
    row_ref[...] = jnp.zeros_like(row_ref)
    row_ref[:, 0:rows] = exact_nt(q_ref[...], err_ref[...])
    out_ref[0:8, :] = pltpu.roll(row_ref[...], rows * group[0], 1)
    start = pl.multiple_of(8 + 8 * group[0], 8)
    out_ref[pl.ds(start, 8), 0:D] = exact_nt(qd_ref[...], errd_ref[...])


def embed_kernel(tok_ref, emb_ref, vec_ref, x_ref, h_ref, ht_ref, emb_s):
    step = tok_ref.shape[1]

    @pl.when(pl.program_id(0) == 0)
    def _():
        emb_s[...] = jnp.zeros_like(emb_s)
        emb_s[0:V, :] = emb_ref[...]

    index = lax.broadcasted_iota(jnp.int32, (TOK, step), 0)
    hot = jnp.where(index == tok_ref[...], 1.0, 0.0).astype(F32)
    hot = jnp.concatenate([hot, hot, hot], 0).astype(B16)
    x = tn(hot, thirds_rows(emb_s[...]))
    x_ref[...] = x
    unit, _ = norm_parts(x)
    normed = unit * vec_ref[:, 0:D] + vec_ref[:, D : 2 * D]
    h_ref[...] = normed.astype(B16)
    ht_ref[...] = jnp.concatenate([normed.T, tail(16, step, 1)], 0).astype(B16)


def spot(group, place, size, unit):
    return pl.ds(pl.multiple_of((group[0] ^ place) * size, unit), size)


def assemble(group, chunks, wide_s, out_s):
    for place, ref in enumerate(chunks):
        wide_s[spot(group, place, ref.shape[0], 8), :] = ref[...].astype(F32)
    out_s[...] = wide_s[...].astype(B16)


def project_kernel(members, group, h_ref, *refs):
    chunks = refs[:members]
    vec_ref, cos_ref, sin_ref, q_ref, k_ref, v_ref, wide_s, w_s = refs[members:]
    step = h_ref.shape[0]

    @pl.when(pl.program_id(0) == 0)
    def _():
        assemble(group, chunks, wide_s, w_s)

    act = nn(h_ref[...], w_s[...]) + vec_ref[:, 2 * D : 5 * D]
    turned = act.T
    cosine, sine = cos_ref[...], sin_ref[...]
    zeros = tail(PAD - HDIM, step, 0)
    ones = tail(PAD - HDIM, step, 3)
    for head in range(HEADS):
        low = HDIM * head
        query = turned[low : low + HDIM]
        query = (query * cosine + half_turn(query) * sine) * HDIM ** (-0.5)
        q_ref[head] = jnp.concatenate([query, zeros], 0).astype(B16)
        keys = turned[D + low : D + low + HDIM]
        keys = keys * cosine + half_turn(keys) * sine
        k_ref[head] = jnp.concatenate([keys, zeros], 0).astype(B16)
        value = turned[2 * D + low : 2 * D + low + HDIM]
        v_ref[head] = jnp.concatenate([value, ones], 0).astype(B16)


def rows_of(value):
    return value.astype(F32).T.astype(B16)


def attend_kernel(q_ref, k_ref, v_ref, mix_ref, inv_ref, p_ref):
    scores = nn(rows_of(k_ref[0]), q_ref[0])
    top = jnp.max(scores, 0, keepdims=True)
    probs = jnp.exp(scores - top).astype(B16)
    p_ref[0] = probs
    out = nn(v_ref[0], probs)
    inverse = 1.0 / out[HDIM : HDIM + 1]
    mix_ref[...] = out[0:HDIM] * inverse
    inv_ref[0] = inverse


def gelu_parts(upper):
    size = jnp.abs(upper) * (0.5**0.5)
    bell = jnp.exp(-0.5 * upper * upper)
    t = 1.0 / (1.0 + 0.3275911 * size)
    poly = t * (0.254829592 + t * (-0.284496736 + t * (1.421413741 + t * (-1.453152027 + t * 1.061405429))))
    lower = 0.5 * poly * bell
    cdf = jnp.where(upper < 0, lower, 1.0 - lower)
    return upper * cdf, cdf + upper * (0.3989422804014327 * bell)


def middle_kernel(members, group, mixa_ref, mixb_ref, inva_ref, invb_ref, x_ref, mask_ref, tgt_ref,
                  count_ref, vec_ref, fin_ref, head_ref, q_ref, qd_ref, *refs):
    chunks, chunks_down, refs = refs[:members], refs[members : 2 * members], refs[2 * members :]
    dm_ref, dx_ref, s_ref, e_ref, *refs = refs
    outs, outs_down, refs = refs[:members], refs[members : 2 * members], refs[2 * members :]
    acc_o, acc_u, acc_d, head_s, hid_s, slope_s, wide_s, wr_ref, wd_ref = refs
    pid = pl.program_id(0)
    step = x_ref.shape[0]
    wide = wd_ref.shape[0]
    wo = slice(wide, wide + D)

    @pl.when(pid == 0)
    def _():
        acc_o[...] = jnp.zeros_like(acc_o)
        acc_u[...] = jnp.zeros_like(acc_u)
        acc_d[...] = jnp.zeros_like(acc_d)
        e_ref[...] = jnp.zeros_like(e_ref)
        s_ref[...] = jnp.zeros_like(s_ref)
        head_s[...] = jnp.zeros_like(head_s)
        head_s[0:V, 0 : D + 1] = head_ref[...]
        assemble(group, chunks, wide_s, wr_ref)
        for place, ref in enumerate(chunks_down):
            wd_ref[spot(group, place, ref.shape[0], 16), :] = ref[...]

    mix = jnp.concatenate([mixa_ref[...], mixb_ref[...]], 0)
    half = inva_ref.shape[0]
    mixed = jnp.concatenate([mix, tail(16, step, 1)], 0).astype(B16)
    middle = x_ref[...] + tn(mixed[0:D], wr_ref[:, wo]) + vec_ref[:, 5 * D : 6 * D]
    unit2, rstd2 = norm_parts(middle)
    gain2 = vec_ref[:, 6 * D : 7 * D]
    normed2 = unit2 * gain2 + vec_ref[:, 7 * D : 8 * D]
    normed2 = jnp.concatenate([normed2, lane_tail(step, WIDE - D)], 1).astype(B16)
    bias_up = vec_ref[:, 9 * D :]
    block = 384
    for low in range(0, wide, block):
        cut = slice(low, low + block)
        upper = nn(normed2[:, 0:D], wr_ref[:, cut]) + bias_up[:, cut]
        hidden, slope = gelu_parts(upper)
        hid_s[:, cut] = hidden.astype(B16)
        slope_s[:, cut] = slope
    resid = middle + nn(hid_s[...], wd_ref[...]) + vec_ref[:, 8 * D : 9 * D]
    unit3, rstd3 = norm_parts(resid)
    final = unit3 * fin_ref[0:1, :] + fin_ref[1:2, :]
    final = jnp.concatenate([final, lane_tail(step, WIDE - D)], 1).astype(B16)

    lanes = lax.broadcasted_iota(jnp.int32, (TOK, WIDE), 1)
    bias = jnp.sum(jnp.where(lanes == D, head_s[...], 0.0), 1, keepdims=True)
    table = head_s[:, 0:D].astype(B16)
    rows = lax.broadcasted_iota(jnp.int32, (TOK, step), 0)
    logits = jnp.where(rows < V, nt(table, final[:, 0:D]) + bias, -1e30)
    shifted = logits - jnp.max(logits, 0, keepdims=True)
    expo = jnp.exp(shifted)
    total = jnp.sum(expo, 0, keepdims=True)
    picks = rows == tgt_ref[...]
    weight = mask_ref[...].astype(F32)
    picked = jnp.sum(jnp.where(picks, shifted, 0.0), 0, keepdims=True)
    loss = jnp.sum((jnp.log(total) - picked) * weight, 1, keepdims=True)
    grad_logits = (expo / total - jnp.where(picks, 1.0, 0.0)) * (weight * (1.0 / count_ref[0:1, 0:1]))
    grad_logits = grad_logits.astype(B16)
    e_ref[16 : 16 + TOK, :] += nn(grad_logits, final)
    grad_resid, grad_fg, grad_fb = norm_back(tn(grad_logits, table), unit3, rstd3, fin_ref[0:1, :])

    grad_y = grad_resid.astype(B16)
    acc_d[...] += tn(hid_s[...], grad_y)
    for low in range(0, wide, block):
        cut = slice(low, low + block)
        grad_hidden = nt(grad_y, wd_ref[cut, :])
        hid_s[:, cut] = (grad_hidden * slope_s[:, cut]).astype(B16)
    acc_u[...] += tn(normed2, hid_s[...])
    grad_mid, grad_g2, grad_b2 = norm_back(nt(hid_s[...], wr_ref[:, 0:wide]), unit2, rstd2, gain2)
    grad_mid = grad_mid + grad_resid
    dx_ref[...] = grad_mid
    branch = grad_mid.astype(B16)
    acc_o[...] += nn(mixed, branch)
    grad_mixed = nt(wr_ref[:, wo], branch).astype(B16).astype(F32)
    zeros = tail(PAD - HDIM - 3, step, 0)
    for head in range(HEADS):
        cut = slice(HDIM * head, HDIM * head + HDIM)
        inverse = inva_ref[head] if head < half else invb_ref[head - half]
        scaled = (grad_mixed[cut] * inverse).astype(B16).astype(F32)
        delta = -jnp.sum(scaled * mix[cut], 0, keepdims=True)
        top, mid, low = thirds(delta)
        dm_ref[head] = jnp.concatenate(
            [scaled, top.astype(F32), mid.astype(F32), low.astype(F32), zeros], 0
        ).astype(B16)
    e_ref[1:2, 0:D] += grad_g2
    e_ref[2:3, 0:D] += grad_b2
    e_ref[3:4, 0:D] += jnp.sum(grad_y.astype(F32), 0, keepdims=True)
    e_ref[8:9, 0:D] += grad_fg
    e_ref[9:10, 0:D] += grad_fb
    e_ref[10:11, :] += jnp.broadcast_to(loss, (1, WIDE))

    @pl.when(pid == pl.num_programs(0) - 1)
    def _():
        e_ref[0:1, 0:D] = acc_o[D : D + 1, :]
        for part in range(wide // D):
            e_ref[4 + part : 5 + part, 0:D] = acc_u[D : D + 1, D * part : D * part + D]
        go = acc_o[0:D, :].astype(B16)
        gu = acc_u[0:D, :].astype(B16)
        sketch = nt(thirds_rows(q_ref[:, 3 * D : 4 * D]), go) + nt(thirds_rows(q_ref[:, 4 * D :]), gu)
        s_ref[0:8, 0:D] = fold_rows(sketch)
        start = thirds_rows(qd_ref[...])
        for part in range(wide // D):
            piece = nt(start, acc_d[D * part : D * part + D, :].astype(B16))
            s_ref[8 + 8 * part : 16 + 8 * part, 0:D] = fold_rows(piece)
        for place, ref in enumerate(outs):
            at = spot(group, place, ref.shape[0], 8)
            ref[:, 0:wide] = acc_u[at, :].astype(B16)
            ref[:, wo] = acc_o[at, :].astype(B16)
        for place, ref in enumerate(outs_down):
            ref[...] = acc_d[spot(group, place, ref.shape[0], 8), :].astype(B16)


def attend_back_kernel(p_ref, q_ref, k_ref, v_ref, dm_ref, cos_ref, sin_ref, da_ref):
    cosine, sine = cos_ref[...], sin_ref[...]
    parts = [[], [], []]
    for head in range(p_ref.shape[0]):
        probs = p_ref[head]
        grad = dm_ref[head]
        slope = nn(rows_of(v_ref[head]), grad)
        grad_scores = (probs.astype(F32) * slope).astype(B16)
        grad_value = nt(grad, probs)[0:HDIM]
        grad_keys = nt(q_ref[head], grad_scores)[0:HDIM]
        grad_query = nn(k_ref[head], grad_scores)[0:HDIM] * HDIM ** (-0.5)
        parts[0].append(grad_query * cosine + half_turn(grad_query * sine))
        parts[1].append(grad_keys * cosine + half_turn(grad_keys * sine))
        parts[2].append(grad_value)
    for index in range(3):
        da_ref[index] = jnp.concatenate(parts[index], 0).astype(B16)


def input_kernel(members, group, tok_ref, daa_ref, dab_ref, h_ref, x_ref, dx_ref, vec_ref, q_ref,
                 s_ref, serr_ref, e_ref, *refs):
    chunks, refs = refs[:members], refs[members:]
    outs, pieces, refs = refs[:members], refs[members : 2 * members], refs[2 * members :]
    out_ref, acc_w, acc_e, wide_s, w_s = refs
    pid = pl.program_id(0)
    step = x_ref.shape[0]

    @pl.when(pid == 0)
    def _():
        acc_w[...] = jnp.zeros_like(acc_w)
        acc_e[...] = jnp.zeros_like(acc_e)
        out_ref[...] = jnp.zeros_like(out_ref)
        assemble(group, chunks, wide_s, w_s)

    da = jnp.concatenate([ref[part] for part in range(3) for ref in (daa_ref, dab_ref)], 0)
    acc_w[...] += nt(h_ref[...], da)
    grad = nn(w_s[...], da).T
    unit, rstd = norm_parts(x_ref[...])
    grad_x, grad_g, grad_b = norm_back(grad, unit, rstd, vec_ref[:, 0:D])
    grad_x = grad_x + dx_ref[...]
    index = lax.broadcasted_iota(jnp.int32, (TOK, step), 0)
    hot = jnp.where(index == tok_ref[...], 1.0, 0.0).astype(B16)
    for part in thirds(grad_x):
        acc_e[...] += nn(hot, part)
    out_ref[40:41, 0:D] += grad_g
    out_ref[41:42, 0:D] += grad_b

    @pl.when(pid == pl.num_programs(0) - 1)
    def _():
        for part in range(3):
            out_ref[42 + part : 43 + part, 0:D] = acc_w[D : D + 1, D * part : D * part + D]
        out_ref[0:40, :] = s_ref[...] + serr_ref[...]
        out_ref[0:8, 0:D] += fold_rows(nt(thirds_rows(q_ref[:, 0 : 3 * D]), acc_w[0:D, :].astype(B16)))
        out_ref[45:48, :] = e_ref[8:11, :]
        out_ref[48:56, :] = e_ref[0:8, :]
        out_ref[56 : 56 + V, 0:D] = acc_e[0:V, :]
        out_ref[56 + V : 56 + 2 * V, :] = e_ref[16 : 16 + V, :]
        for place, ref in enumerate(outs):
            ref[...] = acc_w[spot(group, place, ref.shape[0], 8), :].astype(B16)
        for place, ref in enumerate(pieces):
            ref[...] = out_ref[spot(group, place, ref.shape[0], 8), :]


def orthonormal(sketch, gram):
    basis = jnp.zeros_like(sketch[0])
    count = gram.shape[0]
    index = lax.broadcasted_iota(jnp.int32, (count, 1), 0)
    out = [jnp.zeros_like(part) for part in sketch]
    left = list(sketch)
    for step in range(count):
        pivot = gram[step : step + 1, step : step + 1]
        scale = 1.0 / jnp.sqrt(pivot)
        column = gram[:, step : step + 1] * scale
        row = gram[step : step + 1, :] * scale
        column = jnp.where(index > step, column, 0.0)
        gram = gram - column * row
        for place in range(len(left)):
            base = left[place][step : step + 1, :] * scale
            out[place] = jnp.where(index == step, base, out[place])
            left[place] = left[place] - column * base
    return out


def factor_kernel(members, group, *refs):
    chunks, ins, rests, downs = (refs[members * part : members * part + members] for part in range(4))
    err_ref, errd_ref, a_ref, p_ref, own_ref, ownd_ref, *refs = refs[4 * members :]
    outs, f_s = refs[:members], refs[members]
    rows, wide_cols = err_ref.shape
    hidden = wide_cols - 4 * D
    parts = hidden // D
    for place, ref in enumerate(chunks):
        a_ref[spot(group, place, ref.shape[0], 8), :] = ref[...]
    wide = a_ref[0:8, 0:D]
    down = [a_ref[8 + 8 * part : 16 + 8 * part, 0:D] for part in range(parts)]
    gram = exact_nt(wide, wide)
    (wide,) = orthonormal([wide], gram)
    gram = exact_nt(down[0], down[0])
    for part in range(1, parts):
        gram = gram + exact_nt(down[part], down[part])
    down = orthonormal(down, gram)
    p_ref[...] = jnp.zeros_like(p_ref)
    p_ref[0:8, 0:D] = wide
    for part in range(parts):
        p_ref[8 + 8 * part : 16 + 8 * part, 0:D] = down[part]
    f_s[...] = jnp.zeros_like(f_s)
    for place in range(members):
        piece = pltpu.roll(p_ref[0:8, :], (WIDE - rows * (group[0] ^ place)) % WIDE, 1)[:, 0:rows]
        piece_down = p_ref[pl.ds(pl.multiple_of(8 + 8 * (group[0] ^ place), 8), 8), :][:, 0:D]
        if place == 0:
            own_ref[...] = piece
            ownd_ref[...] = piece_down
            f_s[:, 0:wide_cols] = exact_nn(piece, err_ref[...])
            f_s[:, wide_cols : wide_cols + D] = exact_nn(piece_down, errd_ref[...])
        three = thirds_rows(piece)
        f_s[:, 0 : 3 * D] += fold_rows(nn(three, ins[place][...]))
        f_s[:, 4 * D : wide_cols] += fold_rows(nn(three, rests[place][:, 0:hidden]))
        f_s[:, 3 * D : 4 * D] += fold_rows(nn(three, rests[place][:, hidden:]))
        f_s[:, wide_cols : wide_cols + D] += fold_rows(nn(thirds_rows(piece_down), downs[place][...]))
    for place, ref in enumerate(outs):
        ref[...] = f_s[:, spot(group, place, ref.shape[1], 128)]


def merge_kernel(*refs):
    *chunks, err_ref, out_ref = refs
    value = err_ref[...]
    for ref in chunks:
        value = value + ref[...].astype(F32)
    out_ref[...] = value


def merge_rest_kernel(*refs):
    *chunks, err_ref, out_ref = refs
    value = chunks[0][...].astype(F32)
    for ref in chunks[1:]:
        value = value + ref[...].astype(F32)
    hidden = value.shape[1] - D
    out_ref[:, 0:hidden] = value[:, 0:hidden] + err_ref[:, 4 * D :]
    out_ref[:, hidden:] = value[:, hidden:] + err_ref[:, 3 * D : 4 * D]


def merge_in_kernel(*refs):
    *chunks, err_ref, out_ref = refs
    value = err_ref[:, 0 : 3 * D]
    for ref in chunks:
        value = value + ref[...].astype(F32)
    out_ref[...] = value


def six(left, right):
    first, second = thirds(left), thirds(right)
    order = ((0, 0), (0, 1), (1, 0), (1, 1), (0, 2), (2, 0))
    left = jnp.concatenate([first[i].astype(F32) for i, _ in order], 0).astype(B16)
    right = jnp.concatenate([second[j].astype(F32) for _, j in order], 0).astype(B16)
    return tn(left, right)


def renew(weight, moment, grad, scale, rate):
    new_moment = BETA * moment + scale * grad
    return weight - rate * new_moment, new_moment


def finish_kernel(members, replicas, group, *refs):
    chunks, rest = refs[:members], refs[members:]
    (a_ref, p_ref, own_ref, ownd_ref,
     w_ref, wd_ref, m_ref, md_ref, ein_ref, erest_ref, errd_ref, count_ref,
     vec_ref, vmom_ref, fin_ref, fmom_ref, emb_ref, emom_ref, head_ref, hmom_ref,
     loss_ref, total_ref, norm_ref, nq_ref, nqd_ref, nw_ref, nwd_ref, nm_ref, nmd_ref, ne_ref, ned_ref,
     nvec_ref, nvmom_ref, nfin_ref, nfmom_ref, nemb_ref, nemom_ref, nhead_ref, nhmom_ref, f_s) = rest
    wide_cols = w_ref.shape[1]
    hidden = wide_cols - 4 * D
    for place, ref in enumerate(chunks):
        f_s[:, spot(group, place, ref.shape[1], 128)] = ref[...]
    factor, factor_down = f_s[:, 0:wide_cols], f_s[:, wide_cols : wide_cols + D]
    nq_ref[...] = factor
    nqd_ref[...] = factor_down
    a = a_ref[...]
    square = jnp.sum(a[40:47, 0:D] * a[40:47, 0:D]) + jnp.sum(a[48:56, 0:D] * a[48:56, 0:D])
    emb, top = a[56 : 56 + V, 0:D], a[56 + V : 56 + 2 * V, 0 : D + 1]
    square = square + jnp.sum(emb * emb) + jnp.sum(top * top)
    basis = p_ref[...]
    gram = exact_nt(basis[0:8, 0:D], basis[0:8, 0:D])
    square = square + jnp.sum(gram * exact_nt(factor, factor))
    gram = jnp.zeros((8, 8), F32)
    for part in range(1, basis.shape[0] // 8):
        piece = basis[8 * part : 8 * part + 8, 0:D]
        gram = gram + exact_nt(piece, piece)
    square = square + jnp.sum(gram * exact_nt(factor_down, factor_down))
    norm = jnp.sqrt(square)
    norm_ref[...] = jnp.broadcast_to(norm, norm_ref.shape)
    loss_ref[...] = a[47:48, 0:1]
    total_ref[...] = count_ref[0:1, 0:1]
    scale = jnp.minimum(1.0, CLIP / norm)

    approx = six(own_ref[...], factor)
    nw_ref[...], nm_ref[...] = renew(w_ref[...], m_ref[...], approx, scale, RATE_WIDE)
    share = approx * (1.0 / replicas)
    ne_ref[:, 0 : 3 * D] = ein_ref[...] - share[:, 0 : 3 * D]
    ne_ref[:, 3 * D : 4 * D] = erest_ref[:, hidden:] - share[:, 3 * D : 4 * D]
    ne_ref[:, 4 * D :] = erest_ref[:, 0:hidden] - share[:, 4 * D :]
    approx = six(ownd_ref[...], factor_down)
    nwd_ref[...], nmd_ref[...] = renew(wd_ref[...], md_ref[...], approx, scale, RATE_LOWER)
    ned_ref[...] = errd_ref[...] - approx * (1.0 / replicas)

    places = (40, 41, 42, 43, 44, 48, 49, 50, 51, 52, 53, 54, 55)
    for row, place in enumerate(places):
        cut = slice(D * row, D * row + D)
        nvec_ref[:, cut], nvmom_ref[:, cut] = renew(
            vec_ref[:, cut], vmom_ref[:, cut], a[place : place + 1, 0:D], scale, RATE_VECTOR
        )
    nfin_ref[...], nfmom_ref[...] = renew(fin_ref[...], fmom_ref[...], a[45:47, 0:D], scale, RATE_FINAL)
    nemb_ref[...], nemom_ref[...] = renew(emb_ref[...], emom_ref[...], emb, scale, RATE_EMBED)
    nhead_ref[...], nhmom_ref[...] = renew(head_ref[...], hmom_ref[...], top, scale, RATE_HEAD)


def swap(value, axis, bit):
    size = lax.axis_size(axis)
    return lax.ppermute(value, axis, [(i, i ^ bit) for i in range(size)])


def bits_of(axis):
    size, bit, out = lax.axis_size(axis), 1, []
    while bit < size:
        out.append(bit)
        bit *= 2
    return out


def tie(*values):
    return lax.optimization_barrier(values)


def send_chunks(pieces):
    return [pieces[0]] + [swap(piece, "grp", place) for place, piece in enumerate(pieces) if place]


def add_chunks(pieces, work=()):
    work, results = dict(work), {}

    def beside(turn, moved):
        if turn in work:
            moved, results[turn] = tie(moved, work[turn]())
        return moved

    got = beside(0, send_chunks(pieces))
    total = got[0]
    for piece in got[1:]:
        total = total + piece
    for turn, bit in enumerate(bits_of("rep")):
        total = total + beside(turn + 1, swap(total, "rep", bit))
    got = [total] + [swap(total, "grp", place) for place in range(1, len(pieces))]
    return beside(-1, got), results


def gather_start(value):
    first, *bits = reversed(bits_of("grp"))
    return [value, swap(value, "grp", first)]


def gather_end(pieces):
    first, *bits = reversed(bits_of("grp"))
    order = [0, first]
    for bit in bits:
        pieces = pieces + [swap(piece, "grp", bit) for piece in pieces]
        order = order + [place ^ bit for place in order]
    return [pieces[order.index(place)] for place in range(len(order))]


def halve_start(pieces):
    first, *bits = bits_of("grp")
    keep = [place for place in range(len(pieces)) if not place & first]
    return [(place, pieces[place], swap(pieces[place | first], "grp", first)) for place in keep]


def halve_end(pairs):
    first, *bits = bits_of("grp")
    (_, own, other), *others = pairs
    kept = [own, other]
    sums = {place: (mine.astype(F32) + theirs.astype(F32)).astype(B16) for place, mine, theirs in others}
    for bit in bits:
        kept.append(swap(sums[bit], "grp", bit))
        sums = {
            place: (sums[place].astype(F32) + swap(sums[place | bit], "grp", bit).astype(F32)).astype(B16)
            for place in sums
            if not place & bit
        }
    return kept


def whole(shape):
    return pl.BlockSpec(shape, lambda *_: (0,) * len(shape))


def shards(tokens, mask, targets, mats_d, mats_down, mom_d, mom_down, err_d, err_down, q_d, q_down,
           vectors, vec_mom, final_norm, final_mom, embed, embed_mom, head, head_mom):
    length = tokens.shape[1]
    wide = mats_d.shape[2]
    hidden = wide - 4 * D
    rows = mats_d.shape[1]
    rows_down = mats_down.shape[1]
    step = 256
    steps = length // step
    index = lax.axis_index("grp").astype(jnp.int32)
    group = index.reshape(1)
    members = lax.axis_size("grp")
    cosine, sine = tables(length)
    q_t, qd_t = q_d[0].T, q_down[0].T
    head_t = head.T
    err, errd = err_d[0, 0], err_down[0, 0]

    def call(kernel, name, grid, ins, outs, shapes, scratch=()):
        return pl.pallas_call(
            kernel,
            grid_spec=pltpu.PrefetchScalarGridSpec(
                num_scalar_prefetch=1, grid=grid, in_specs=ins, out_specs=outs, scratch_shapes=scratch
            ),
            out_shape=shapes,
            compiler_params=params(),
            name=name,
        )

    shape = jax.ShapeDtypeStruct
    rounds = [("grp", bit) for bit in bits_of("grp")] + [("rep", bit) for bit in bits_of("rep")]

    def advance(value, times=1):
        for _ in range(min(times, len(rounds))):
            value = value + swap(value, *rounds.pop(0))
        return value

    cols = pl.BlockSpec((1, step), lambda i, *_: (0, i))
    flat = pl.BlockSpec((step, D), lambda i, *_: (i, 0))
    heads = pl.BlockSpec((HEADS, PAD, step), lambda i, *_: (0, 0, i))
    wave = pl.BlockSpec((HDIM, step), lambda i, *_: (0, i))
    ext = pl.BlockSpec((D + 16, step), lambda i, *_: (0, i))

    w_in = gather_start(mats_d[0][:, : 3 * D].astype(B16))
    counted = jnp.broadcast_to(jnp.sum(mask.astype(F32)), (8, 128))
    more = advance(counted)
    err_sketch = call(
        error_kernel, "error_sketch", (1,),
        [whole((rows, wide)), whole((rows_down, D)), whole((8, wide)), whole((8, D))],
        whole((40, WIDE)), shape((40, WIDE), F32), [pltpu.VMEM((8, WIDE), F32)],
    )(group, err, errd, q_t, qd_t)
    x, h, h_t = pl.pallas_call(
        embed_kernel,
        grid=(steps,),
        in_specs=[cols, whole((V, D)), whole(vectors.shape)],
        out_specs=[flat, flat, ext],
        out_shape=[shape((length, D), F32), shape((length, D), B16), shape((D + 16, length), B16)],
        scratch_shapes=[pltpu.VMEM((TOK, D), F32)],
        compiler_params=params(),
        name="embed",
    )(tokens, embed, vectors)
    w_in, err_sketch, h, counted = tie(w_in, err_sketch, h, more)
    w_in = gather_end(w_in)
    rest = jnp.concatenate([mats_d[0][:, 4 * D :], mats_d[0][:, 3 * D : 4 * D]], 1).astype(B16)
    down = mats_down[0].astype(B16)
    more = advance(counted)
    w_in, counted, rest, down = tie(w_in, more, rest, down)
    w_rest, w_down = gather_start(rest), gather_start(down)
    more = advance(counted)
    query, keys, value = call(
        partial(project_kernel, members), "project", (steps,),
        [flat] + [whole((rows, 3 * D))] * members + [whole(vectors.shape), wave, wave],
        [heads] * 3, [shape((HEADS, PAD, length), B16)] * 3,
        [pltpu.VMEM((D, 3 * D), F32), pltpu.VMEM((D, 3 * D), B16)],
    )(group, h, *w_in, vectors, cosine, sine)
    query, counted = tie(query, more)

    half = HEADS // 2
    mixes, inverses, probs = [], [], []
    for part in range(2):
        one = pl.BlockSpec((1, PAD, length), lambda i, part=part: (i + half * part, 0, 0))
        more = advance(counted, 1 + part * len(rounds))
        mix, inverse, prob = pl.pallas_call(
            attend_kernel,
            grid=(half,),
            in_specs=[one, one, one],
            out_specs=[
                pl.BlockSpec((HDIM, length), lambda i: (i, 0)),
                pl.BlockSpec((1, 1, length), lambda i: (i, 0, 0)),
                pl.BlockSpec((1, length, length), lambda i: (i, 0, 0)),
            ],
            out_shape=[
                shape((half * HDIM, length), F32),
                shape((half, 1, length), F32),
                shape((half, length, length), B16),
            ],
            compiler_params=params(),
            name="attend",
        )(query, keys, value)
        mix, query, counted, w_rest, w_down = tie(mix, query, more, w_rest, w_down)
        if part == 0:
            w_rest, w_down = gather_end(w_rest), gather_end(w_down)
        mixes.append(mix)
        inverses.append(inverse)
        probs.append(prob)

    everyone = [(rows, D + hidden)] * members + [(rows_down, D)] * members
    grad_mix, grad_mid, sketch, early, *grads = call(
        partial(middle_kernel, members), "feed_and_loss", (steps,),
        [pl.BlockSpec((half * HDIM, step), lambda i, *_: (0, i))] * 2
        + [pl.BlockSpec((half, 1, step), lambda i, *_: (0, 0, i))] * 2
        + [
            flat, cols, cols, whole((8, 128)), whole(vectors.shape), whole((2, D)),
            whole((V, D + 1)), whole((8, wide)), whole((8, D)),
        ]
        + [whole(item) for item in everyone],
        [heads, flat, whole((40, WIDE)), whole((56, WIDE))] + [whole(item) for item in everyone],
        [
            shape((HEADS, PAD, length), B16),
            shape((length, D), F32),
            shape((40, WIDE), F32),
            shape((56, WIDE), F32),
        ]
        + [shape(item, B16) for item in everyone],
        [
            pltpu.VMEM((D + 16, D), F32),
            pltpu.VMEM((WIDE, hidden), F32),
            pltpu.VMEM((hidden, D), F32),
            pltpu.VMEM((TOK, WIDE), F32),
            pltpu.VMEM((step, hidden), B16),
            pltpu.VMEM((step, hidden), F32),
            pltpu.VMEM((D, D + hidden), F32),
            pltpu.VMEM((D, D + hidden), B16),
            pltpu.VMEM((hidden, D), B16),
        ],
    )(group, *mixes, *inverses, x, mask, targets, counted, vectors, final_norm, head_t, q_t, qd_t,
      *w_rest, *w_down)
    g_rest, g_down = grads[:members], grads[members:]
    all_down = send_chunks(g_down)
    all_rest = send_chunks(g_rest)

    pair = 2
    turned = half // pair
    grad_acts = []
    for part in range(2):
        two = pl.BlockSpec((pair, PAD, length), lambda i, part=part: (i + turned * part, 0, 0))
        grad_act = pl.pallas_call(
            attend_back_kernel,
            grid=(turned,),
            in_specs=[
                pl.BlockSpec((pair, length, length), lambda i: (i, 0, 0)),
                two, two, two, two, whole((HDIM, length)), whole((HDIM, length)),
            ],
            out_specs=pl.BlockSpec((3, pair * HDIM, length), lambda i: (0, i, 0)),
            out_shape=shape((3, half * HDIM, length), B16),
            compiler_params=params(),
            name="attend_back",
        )(probs[part], query, keys, value, grad_mix, cosine, sine)
        grad_acts.append(grad_act)
    all_down, all_rest, grad_acts = tie(all_down, all_rest, grad_acts)

    act = pl.BlockSpec((3, half * HDIM, step), lambda i, *_: (0, 0, i))
    size = 128 // members
    ins = [(rows, 3 * D)] * members
    grads = call(
        partial(input_kernel, members), "input_grads", (steps,),
        [
            cols, act, act, ext, flat, flat,
            whole(vectors.shape), whole((8, wide)), whole((40, WIDE)), whole((40, WIDE)), whole((56, WIDE)),
        ]
        + [whole(item) for item in ins],
        [whole(item) for item in ins] + [whole((size, WIDE))] * members,
        [shape(item, B16) for item in ins] + [shape((size, WIDE), F32)] * members,
        [
            pltpu.VMEM((128, WIDE), F32), pltpu.VMEM((D + 16, 3 * D), F32), pltpu.VMEM((TOK, D), F32),
            pltpu.VMEM((D, 3 * D), F32), pltpu.VMEM((D, 3 * D), B16),
        ],
    )(group, tokens, *grad_acts, h_t, x, grad_mid, vectors, q_t, sketch, err_sketch, early, *w_in)
    g_in, pieces = grads[:members], grads[members:]
    half_in = halve_start(g_in)

    def merge(kernel, name, chunks, err, result):
        return lambda: pl.pallas_call(
            kernel, out_shape=shape(result, F32), compiler_params=params(), name=name
        )(*chunks, err)

    chunks, merged = add_chunks(
        pieces,
        (
            (0, merge(merge_kernel, "merge_down", all_down, errd, errd.shape)),
            (1, lambda: halve_end(half_in)),
            (2, merge(merge_rest_kernel, "merge_rest", all_rest, err, (rows, D + hidden))),
        ),
    )
    merged_down, all_in, merged_rest = (merged[turn] for turn in range(3))
    span = -(-(wide + WIDE) // (128 * members)) * 128
    shared, basis, own, ownd, *pieces = call(
        partial(factor_kernel, members), "left_factors", (1,),
        [whole((size, WIDE))] * members + [whole(item) for item in ins + everyone]
        + [whole((rows, wide)), whole((rows_down, D))],
        [whole((128, WIDE)), whole((40, WIDE)), whole((8, rows)), whole((8, rows_down))]
        + [whole((8, span))] * members,
        [
            shape((128, WIDE), F32), shape((40, WIDE), F32), shape((8, rows), F32), shape((8, rows_down), F32),
        ]
        + [shape((8, span), F32)] * members,
        [pltpu.VMEM((8, span * members), F32)],
    )(group, *chunks, *g_in, *g_rest, *g_down, err, errd)

    chunks, merged = add_chunks(
        pieces, ((0, merge(merge_in_kernel, "merge_in", all_in, err, (rows, 3 * D))),)
    )
    merged_in = merged[0]

    same = lambda value: shape(value.shape, F32)
    replicas = lax.axis_size("rep")
    small = (vectors, vec_mom, final_norm, final_mom, embed, embed_mom, head_t, head_mom.T)
    given = (
        *chunks, shared, basis, own, ownd,
        mats_d[0], mats_down[0], mom_d[0], mom_down[0], merged_in, merged_rest, merged_down, counted, *small,
    )
    shapes = [
        shape((1, 1), F32), shape((1, 1), F32), shape((1, 1), F32), shape((8, wide), F32), shape((8, D), F32),
        same(mats_d[0]), same(mats_down[0]), same(mats_d[0]), same(mats_down[0]), same(err), same(errd),
    ] + [same(item) for item in small]
    outs = call(
        partial(finish_kernel, members, replicas), "finish", (1,),
        [whole(item.shape) for item in given], [whole(item.shape) for item in shapes], shapes,
        [pltpu.VMEM((8, span * members), F32)],
    )(group, *given)
    (loss, total, norm, new_q, new_qd, new_wide, new_down, new_mom_wide, new_mom_dn, new_err, new_errd,
     new_vec, new_vmom, new_fin, new_fmom, new_emb, new_emom, new_head, new_hmom) = outs
    return (
        loss.reshape(()),
        total.reshape(()),
        norm.reshape(()),
        new_wide[None],
        new_down[None],
        new_mom_wide[None],
        new_mom_dn[None],
        new_err[None, None],
        new_errd[None, None],
        own.T[None],
        ownd.T[None],
        new_q.T[None],
        new_qd.T[None],
        new_vec,
        new_vmom,
        new_fin,
        new_fmom,
        new_emb,
        new_emom,
        new_head.T,
        new_hmom.T,
    )


def solution(mesh):
    whole_seq = P(("rep", "grp"), None)
    by_rows = P(None, "grp", None)
    by_replica = P("rep", None, "grp", None)
    placed = (
        (whole_seq,) * 3 + (by_rows,) * 4 + (by_replica,) * 2 + (P(),) * 10
    )
    given = (P(),) * 3 + (by_rows,) * 4 + (by_replica,) * 2 + (by_rows,) * 2 + (P(),) * 10
    return jax.shard_map(shards, mesh=mesh, in_specs=placed, out_specs=given, check_vma=False)
```

```python
from functools import partial

import jax
import jax.numpy as jnp
import numpy as np
from jax import lax
from jax.experimental import pallas as pl
from jax.experimental.pallas import tpu as pltpu
from jax.sharding import PartitionSpec as P

D = 480
HEADS = 20
HDIM = 24
V = 33
PAD = 32
TOK = 40
WIDE = 512
EPS = 1e-05
BETA = 0.9
RATE_WIDE = 20000.0
RATE_LOWER = 3000.0
RATE_VECTOR = 20000.0
RATE_FINAL = 40000.0
RATE_EMBED = 60000.0
RATE_HEAD = 3000.0
CLIP = 0.005
F32 = jnp.float32
B16 = jnp.bfloat16
MIB = 2**20


ROOM = {
    "error_sketch": 16, "embed": 16, "project": 24, "attend": 30, "feed_and_loss": 56, "attend_back": 30,
    "input_grads": 30, "left_factors": 24, "merge_down": 12, "merge_rest": 16, "merge_in": 16, "finish": 30,
}


def params(name):
    return pltpu.CompilerParams(vmem_limit_bytes=ROOM[name] * MIB)


def nn(left, right):
    return jnp.dot(left, right, preferred_element_type=F32)


def nt(left, right):
    return lax.dot_general(left, right, (((1,), (1,)), ((), ())), preferred_element_type=F32)


def tn(left, right):
    return lax.dot_general(left, right, (((0,), (0,)), ((), ())), preferred_element_type=F32)


def thirds(value):
    top = value.astype(B16)
    rest = value - top.astype(F32)
    middle = rest.astype(B16)
    return top, middle, (rest - middle.astype(F32)).astype(B16)


def thirds_rows(value):
    return jnp.concatenate([part.astype(F32) for part in thirds(value)], 0).astype(B16)


def fold_rows(value):
    return value[0:8] + value[8:16] + value[16:24]


def exact_nt(left, right):
    return lax.dot_general(
        left, right, (((1,), (1,)), ((), ())),
        precision=lax.Precision.HIGHEST, preferred_element_type=F32,
    )


def exact_nn(left, right):
    return jnp.dot(left, right, precision=lax.Precision.HIGHEST, preferred_element_type=F32)


def three_nt(left, right):
    three = thirds_rows(left)
    top, middle, low = thirds(right)
    return fold_rows(nt(three, top) + nt(three, middle) + nt(three, low))


def three_nn(left, right):
    three = thirds_rows(left)
    top, middle, low = thirds(right)
    return fold_rows(nn(three, top) + nn(three, middle) + nn(three, low))


def norm_parts(value):
    center = value - jnp.mean(value, -1, keepdims=True)
    spread = jnp.mean(center * center, -1, keepdims=True)
    rstd = lax.rsqrt(spread + EPS)
    return center * rstd, rstd


def norm_back(grad, unit, rstd, gain):
    inner = grad * gain
    first = jnp.mean(inner, -1, keepdims=True)
    second = jnp.mean(inner * unit, -1, keepdims=True)
    return (
        rstd * (inner - first - unit * second),
        jnp.sum(grad * unit, 0, keepdims=True),
        jnp.sum(grad, 0, keepdims=True),
    )


def half_turn(value):
    return jnp.concatenate([value[HDIM // 2 :], value[: HDIM // 2]], 0)


def tail(rows, cols, ones):
    index = lax.broadcasted_iota(jnp.int32, (rows, cols), 0)
    return jnp.where(index < ones, 1.0, 0.0).astype(F32)


def lane_tail(rows, cols):
    index = lax.broadcasted_iota(jnp.int32, (rows, cols), 1)
    return jnp.where(index == 0, 1.0, 0.0).astype(F32)


def tables(length):
    half = HDIM // 2
    freq = np.float32(10000.0) ** (-np.arange(half, dtype=np.float32) * np.float32(2.0) / np.float32(HDIM))
    angle = np.arange(length, dtype=np.float32)[None, :] * freq.astype(np.float32)[:, None]
    cosine, sine = np.cos(angle), np.sin(angle)
    return (
        jnp.asarray(np.concatenate([cosine, cosine], 0), F32),
        jnp.asarray(np.concatenate([-sine, sine], 0), F32),
    )


def error_kernel(group, err_ref, errd_ref, q_ref, qd_ref, out_ref, row_ref):
    rows = err_ref.shape[0]
    out_ref[...] = jnp.zeros_like(out_ref)
    row_ref[...] = jnp.zeros_like(row_ref)
    row_ref[:, 0:rows] = three_nt(q_ref[...], err_ref[...])
    out_ref[0:8, :] = pltpu.roll(row_ref[...], rows * group[0], 1)
    start = pl.multiple_of(8 + 8 * group[0], 8)
    out_ref[pl.ds(start, 8), 0:D] = three_nt(qd_ref[...], errd_ref[...])


def embed_kernel(tok_ref, emb_ref, vec_ref, x_ref, h_ref, ht_ref, emb_s):
    step = tok_ref.shape[1]

    @pl.when(pl.program_id(0) == 0)
    def _():
        emb_s[...] = jnp.zeros_like(emb_s)
        emb_s[0:V, :] = emb_ref[...]

    index = lax.broadcasted_iota(jnp.int32, (TOK, step), 0)
    hot = jnp.where(index == tok_ref[...], 1.0, 0.0).astype(F32)
    hot = jnp.concatenate([hot, hot, hot], 0).astype(B16)
    x = tn(hot, thirds_rows(emb_s[...]))
    x_ref[...] = x
    unit, _ = norm_parts(x)
    normed = unit * vec_ref[:, 0:D] + vec_ref[:, D : 2 * D]
    h_ref[...] = normed.astype(B16)
    ht_ref[...] = jnp.concatenate([normed.T, tail(16, step, 1)], 0).astype(B16)


def spot(group, place, size, unit):
    return pl.ds(pl.multiple_of((group[0] ^ place) * size, unit), size)


def assemble(group, chunks, wide_s, out_s):
    for place, ref in enumerate(chunks):
        wide_s[spot(group, place, ref.shape[0], 8), :] = ref[...].astype(F32)
    out_s[...] = wide_s[...].astype(B16)


def project_kernel(members, group, h_ref, *refs):
    chunks = refs[:members]
    vec_ref, cos_ref, sin_ref, q_ref, k_ref, v_ref, wide_s, w_s = refs[members:]
    step = h_ref.shape[0]

    @pl.when(pl.program_id(0) == 0)
    def _():
        assemble(group, chunks, wide_s, w_s)

    act = nn(h_ref[...], w_s[...]) + vec_ref[:, 2 * D : 5 * D]
    turned = act.T
    cosine, sine = cos_ref[...], sin_ref[...]
    zeros = tail(PAD - HDIM, step, 0)
    ones = tail(PAD - HDIM, step, 3)
    for head in range(HEADS):
        low = HDIM * head
        query = turned[low : low + HDIM]
        query = (query * cosine + half_turn(query) * sine) * HDIM ** (-0.5)
        q_ref[head] = jnp.concatenate([query, zeros], 0).astype(B16)
        keys = turned[D + low : D + low + HDIM]
        keys = keys * cosine + half_turn(keys) * sine
        k_ref[head] = jnp.concatenate([keys, ones], 0).astype(B16)
        value = turned[2 * D + low : 2 * D + low + HDIM]
        v_ref[head] = jnp.concatenate([value, ones], 0).astype(B16)


def rows_of(value):
    return value.astype(F32).T.astype(B16)


def attend_kernel(q_ref, k_ref, v_ref, mix_ref, inv_ref, p_ref):
    count, _, length = q_ref.shape
    zeros = tail(PAD - HDIM - 3, length, 0)

    def first(head):
        keys = rows_of(k_ref[head])
        query = q_ref[head]
        top = jnp.max(nn(keys, query), 0, keepdims=True)
        parts = [part.astype(F32) for part in thirds(-top)]
        return keys, jnp.concatenate([query[0:HDIM].astype(F32)] + parts + [zeros], 0).astype(B16)

    def second(head, keys, query):
        probs = jnp.exp(nn(keys, query)).astype(B16)
        p_ref[head] = probs
        out = nn(v_ref[head], probs)
        inverse = 1.0 / out[HDIM : HDIM + 1]
        mix_ref[HDIM * head : HDIM * head + HDIM, :] = out[0:HDIM] * inverse
        inv_ref[head] = inverse

    held = first(0)
    for head in range(count):
        ahead = first(head + 1) if head + 1 < count else None
        second(head, *held)
        held = ahead


def gelu_parts(upper):
    size = jnp.abs(upper) * (0.5**0.5)
    bell = jnp.exp(-0.5 * upper * upper)
    t = 1.0 / (1.0 + 0.3275911 * size)
    poly = t * (0.254829592 + t * (-0.284496736 + t * (1.421413741 + t * (-1.453152027 + t * 1.061405429))))
    lower = 0.5 * poly * bell
    cdf = jnp.where(upper < 0, lower, 1.0 - lower)
    return upper * cdf, cdf + upper * (0.3989422804014327 * bell)


def middle_kernel(members, group, mixa_ref, mixb_ref, inva_ref, invb_ref, x_ref, mask_ref, tgt_ref,
                  count_ref, vec_ref, fin_ref, head_ref, q_ref, qd_ref, *refs):
    chunks, chunks_down, refs = refs[:members], refs[members : 2 * members], refs[2 * members :]
    dm_ref, dx_ref, s_ref, e_ref, *refs = refs
    outs, outs_down, refs = refs[:members], refs[members : 2 * members], refs[2 * members :]
    acc_o, acc_u, acc_d, head_s, hid_s, slope_s, wide_s, wr_ref, wd_ref = refs
    pid = pl.program_id(0)
    step = x_ref.shape[0]
    wide = wd_ref.shape[0]
    wo = slice(wide, wide + D)

    @pl.when(pid == 0)
    def _():
        acc_o[...] = jnp.zeros_like(acc_o)
        acc_u[...] = jnp.zeros_like(acc_u)
        acc_d[...] = jnp.zeros_like(acc_d)
        e_ref[...] = jnp.zeros_like(e_ref)
        s_ref[...] = jnp.zeros_like(s_ref)
        head_s[...] = jnp.zeros_like(head_s)
        head_s[0:V, 0 : D + 1] = head_ref[...]
        assemble(group, chunks, wide_s, wr_ref)
        for place, ref in enumerate(chunks_down):
            wd_ref[spot(group, place, ref.shape[0], 16), :] = ref[...]

    mix = jnp.concatenate([mixa_ref[...], mixb_ref[...]], 0)
    half = inva_ref.shape[0]
    mixed = jnp.concatenate([mix, tail(16, step, 1)], 0).astype(B16)
    middle = x_ref[...] + tn(mixed[0:D], wr_ref[:, wo]) + vec_ref[:, 5 * D : 6 * D]
    unit2, rstd2 = norm_parts(middle)
    gain2 = vec_ref[:, 6 * D : 7 * D]
    normed2 = unit2 * gain2 + vec_ref[:, 7 * D : 8 * D]
    normed2 = jnp.concatenate([normed2, lane_tail(step, WIDE - D)], 1).astype(B16)
    bias_up = vec_ref[:, 9 * D :]
    block = 384
    for low in range(0, wide, block):
        cut = slice(low, low + block)
        upper = nn(normed2[:, 0:D], wr_ref[:, cut]) + bias_up[:, cut]
        hidden, slope = gelu_parts(upper)
        hid_s[:, cut] = hidden.astype(B16)
        slope_s[:, cut] = slope
    resid = middle + nn(hid_s[...], wd_ref[...]) + vec_ref[:, 8 * D : 9 * D]
    unit3, rstd3 = norm_parts(resid)
    final = unit3 * fin_ref[0:1, :] + fin_ref[1:2, :]
    final = jnp.concatenate([final, lane_tail(step, WIDE - D)], 1).astype(B16)

    lanes = lax.broadcasted_iota(jnp.int32, (TOK, WIDE), 1)
    bias = jnp.sum(jnp.where(lanes == D, head_s[...], 0.0), 1, keepdims=True)
    table = head_s[:, 0:D].astype(B16)
    rows = lax.broadcasted_iota(jnp.int32, (TOK, step), 0)
    logits = jnp.where(rows < V, nt(table, final[:, 0:D]) + bias, -1e30)
    shifted = logits - jnp.max(logits, 0, keepdims=True)
    expo = jnp.exp(shifted)
    total = jnp.sum(expo, 0, keepdims=True)
    picks = rows == tgt_ref[...]
    weight = mask_ref[...].astype(F32)
    picked = jnp.sum(jnp.where(picks, shifted, 0.0), 0, keepdims=True)
    loss = jnp.sum((jnp.log(total) - picked) * weight, 1, keepdims=True)
    grad_logits = (expo / total - jnp.where(picks, 1.0, 0.0)) * (weight * (1.0 / count_ref[0:1, 0:1]))
    grad_logits = grad_logits.astype(B16)
    e_ref[16 : 16 + TOK, :] += nn(grad_logits, final)
    grad_resid, grad_fg, grad_fb = norm_back(tn(grad_logits, table), unit3, rstd3, fin_ref[0:1, :])

    grad_y = grad_resid.astype(B16)
    acc_d[...] += tn(hid_s[...], grad_y)
    for low in range(0, wide, block):
        cut = slice(low, low + block)
        grad_hidden = nt(grad_y, wd_ref[cut, :])
        hid_s[:, cut] = (grad_hidden * slope_s[:, cut]).astype(B16)
    acc_u[...] += tn(normed2, hid_s[...])
    grad_mid, grad_g2, grad_b2 = norm_back(nt(hid_s[...], wr_ref[:, 0:wide]), unit2, rstd2, gain2)
    grad_mid = grad_mid + grad_resid
    dx_ref[...] = grad_mid
    branch = grad_mid.astype(B16)
    acc_o[...] += nn(mixed, branch)
    grad_mixed = nt(wr_ref[:, wo], branch).astype(B16).astype(F32)
    zeros = tail(PAD - HDIM - 3, step, 0)
    for head in range(HEADS):
        cut = slice(HDIM * head, HDIM * head + HDIM)
        inverse = inva_ref[head] if head < half else invb_ref[head - half]
        scaled = (grad_mixed[cut] * inverse).astype(B16).astype(F32)
        delta = -jnp.sum(scaled * mix[cut], 0, keepdims=True)
        top, mid, low = thirds(delta)
        dm_ref[head] = jnp.concatenate(
            [scaled, top.astype(F32), mid.astype(F32), low.astype(F32), zeros], 0
        ).astype(B16)
    e_ref[1:2, 0:D] += grad_g2
    e_ref[2:3, 0:D] += grad_b2
    e_ref[3:4, 0:D] += jnp.sum(grad_y.astype(F32), 0, keepdims=True)
    e_ref[8:9, 0:D] += grad_fg
    e_ref[9:10, 0:D] += grad_fb
    e_ref[10:11, :] += jnp.broadcast_to(loss, (1, WIDE))

    @pl.when(pid == pl.num_programs(0) - 1)
    def _():
        e_ref[0:1, 0:D] = acc_o[D : D + 1, :]
        for part in range(wide // D):
            e_ref[4 + part : 5 + part, 0:D] = acc_u[D : D + 1, D * part : D * part + D]
        go = acc_o[0:D, :].astype(B16)
        gu = acc_u[0:D, :].astype(B16)
        sketch = nt(thirds_rows(q_ref[:, 3 * D : 4 * D]), go) + nt(thirds_rows(q_ref[:, 4 * D :]), gu)
        s_ref[0:8, 0:D] = fold_rows(sketch)
        start = thirds_rows(qd_ref[...])
        for part in range(wide // D):
            piece = nt(start, acc_d[D * part : D * part + D, :].astype(B16))
            s_ref[8 + 8 * part : 16 + 8 * part, 0:D] = fold_rows(piece)
        for place, ref in enumerate(outs):
            at = spot(group, place, ref.shape[0], 8)
            ref[:, 0:wide] = acc_u[at, :].astype(B16)
            ref[:, wo] = acc_o[at, :].astype(B16)
        for place, ref in enumerate(outs_down):
            ref[...] = acc_d[spot(group, place, ref.shape[0], 8), :].astype(B16)


def attend_back_kernel(p_ref, q_ref, k_ref, v_ref, dm_ref, cos_ref, sin_ref, da_ref):
    cosine, sine = cos_ref[...], sin_ref[...]
    parts = [[], [], []]
    for head in range(p_ref.shape[0]):
        probs = p_ref[head]
        grad = dm_ref[head]
        slope = nn(rows_of(v_ref[head]), grad)
        grad_scores = (probs.astype(F32) * slope).astype(B16)
        grad_value = nt(grad, probs)[0:HDIM]
        grad_keys = nt(q_ref[head], grad_scores)[0:HDIM]
        grad_query = nn(k_ref[head], grad_scores)[0:HDIM] * HDIM ** (-0.5)
        parts[0].append(grad_query * cosine + half_turn(grad_query * sine))
        parts[1].append(grad_keys * cosine + half_turn(grad_keys * sine))
        parts[2].append(grad_value)
    for index in range(3):
        da_ref[index] = jnp.concatenate(parts[index], 0).astype(B16)


def input_kernel(members, group, tok_ref, daa_ref, dab_ref, h_ref, x_ref, dx_ref, vec_ref, q_ref,
                 s_ref, serr_ref, e_ref, *refs):
    chunks, refs = refs[:members], refs[members:]
    outs, pieces, refs = refs[:members], refs[members : 2 * members], refs[2 * members :]
    out_ref, acc_w, acc_e, wide_s, w_s = refs
    pid = pl.program_id(0)
    step = x_ref.shape[0]

    @pl.when(pid == 0)
    def _():
        acc_w[...] = jnp.zeros_like(acc_w)
        acc_e[...] = jnp.zeros_like(acc_e)
        out_ref[...] = jnp.zeros_like(out_ref)
        assemble(group, chunks, wide_s, w_s)

    da = jnp.concatenate([ref[part] for part in range(3) for ref in (daa_ref, dab_ref)], 0)
    acc_w[...] += nt(h_ref[...], da)
    grad = nn(w_s[...], da).T
    unit, rstd = norm_parts(x_ref[...])
    grad_x, grad_g, grad_b = norm_back(grad, unit, rstd, vec_ref[:, 0:D])
    grad_x = grad_x + dx_ref[...]
    index = lax.broadcasted_iota(jnp.int32, (TOK, step), 0)
    hot = jnp.where(index == tok_ref[...], 1.0, 0.0).astype(B16)
    for part in thirds(grad_x):
        acc_e[...] += nn(hot, part)
    out_ref[40:41, 0:D] += grad_g
    out_ref[41:42, 0:D] += grad_b

    @pl.when(pid == pl.num_programs(0) - 1)
    def _():
        for part in range(3):
            out_ref[42 + part : 43 + part, 0:D] = acc_w[D : D + 1, D * part : D * part + D]
        out_ref[0:40, :] = s_ref[...] + serr_ref[...]
        out_ref[0:8, 0:D] += fold_rows(nt(thirds_rows(q_ref[:, 0 : 3 * D]), acc_w[0:D, :].astype(B16)))
        out_ref[45:48, :] = e_ref[8:11, :]
        out_ref[48:56, :] = e_ref[0:8, :]
        out_ref[56 : 56 + V, 0:D] = acc_e[0:V, :]
        out_ref[56 + V : 56 + 2 * V, :] = e_ref[16 : 16 + V, :]
        for place, ref in enumerate(outs):
            ref[...] = acc_w[spot(group, place, ref.shape[0], 8), :].astype(B16)
        for place, ref in enumerate(pieces):
            ref[...] = out_ref[spot(group, place, ref.shape[0], 8), :]


def orthonormal(sketch, gram):
    basis = jnp.zeros_like(sketch[0])
    count = gram.shape[0]
    index = lax.broadcasted_iota(jnp.int32, (count, 1), 0)
    out = [jnp.zeros_like(part) for part in sketch]
    left = list(sketch)
    for step in range(count):
        pivot = gram[step : step + 1, step : step + 1]
        scale = 1.0 / jnp.sqrt(pivot)
        column = gram[:, step : step + 1] * scale
        row = gram[step : step + 1, :] * scale
        column = jnp.where(index > step, column, 0.0)
        gram = gram - column * row
        for place in range(len(left)):
            base = left[place][step : step + 1, :] * scale
            out[place] = jnp.where(index == step, base, out[place])
            left[place] = left[place] - column * base
    return out


def factor_kernel(members, group, *refs):
    chunks, ins, rests, downs = (refs[members * part : members * part + members] for part in range(4))
    err_ref, errd_ref, a_ref, p_ref, own_ref, ownd_ref, *refs = refs[4 * members :]
    outs, f_s = refs[:members], refs[members]
    rows, wide_cols = err_ref.shape
    hidden = wide_cols - 4 * D
    parts = hidden // D
    for place, ref in enumerate(chunks):
        a_ref[spot(group, place, ref.shape[0], 8), :] = ref[...]
    wide = a_ref[0:8, 0:D]
    down = [a_ref[8 + 8 * part : 16 + 8 * part, 0:D] for part in range(parts)]
    gram = exact_nt(wide, wide)
    (wide,) = orthonormal([wide], gram)
    gram = exact_nt(down[0], down[0])
    for part in range(1, parts):
        gram = gram + exact_nt(down[part], down[part])
    down = orthonormal(down, gram)
    p_ref[...] = jnp.zeros_like(p_ref)
    p_ref[0:8, 0:D] = wide
    for part in range(parts):
        p_ref[8 + 8 * part : 16 + 8 * part, 0:D] = down[part]
    f_s[...] = jnp.zeros_like(f_s)
    for place in range(members):
        piece = pltpu.roll(p_ref[0:8, :], (WIDE - rows * (group[0] ^ place)) % WIDE, 1)[:, 0:rows]
        piece_down = p_ref[pl.ds(pl.multiple_of(8 + 8 * (group[0] ^ place), 8), 8), :][:, 0:D]
        if place == 0:
            own_ref[...] = piece
            ownd_ref[...] = piece_down
            f_s[:, 0:wide_cols] = three_nn(piece, err_ref[...])
            f_s[:, wide_cols : wide_cols + D] = three_nn(piece_down, errd_ref[...])
        three = thirds_rows(piece)
        f_s[:, 0 : 3 * D] += fold_rows(nn(three, ins[place][...]))
        f_s[:, 4 * D : wide_cols] += fold_rows(nn(three, rests[place][:, 0:hidden]))
        f_s[:, 3 * D : 4 * D] += fold_rows(nn(three, rests[place][:, hidden:]))
        f_s[:, wide_cols : wide_cols + D] += fold_rows(nn(thirds_rows(piece_down), downs[place][...]))
    for place, ref in enumerate(outs):
        ref[...] = f_s[:, spot(group, place, ref.shape[1], 128)]


def merge_kernel(*refs):
    *chunks, err_ref, out_ref = refs
    value = err_ref[...]
    for ref in chunks:
        value = value + ref[...].astype(F32)
    out_ref[...] = value


def merge_rest_kernel(*refs):
    *chunks, err_ref, out_ref = refs
    value = chunks[0][...].astype(F32)
    for ref in chunks[1:]:
        value = value + ref[...].astype(F32)
    hidden = value.shape[1] - D
    out_ref[:, 0:hidden] = value[:, 0:hidden] + err_ref[:, 4 * D :]
    out_ref[:, hidden:] = value[:, hidden:] + err_ref[:, 3 * D : 4 * D]


def merge_in_kernel(*refs):
    *chunks, err_ref, out_ref = refs
    value = err_ref[:, 0 : 3 * D]
    for ref in chunks:
        value = value + ref[...].astype(F32)
    out_ref[...] = value


def six(left, right):
    first, second = thirds(left), thirds(right)
    order = ((0, 0), (0, 1), (1, 0), (1, 1), (0, 2), (2, 0))
    left = jnp.concatenate([first[i].astype(F32) for i, _ in order], 0).astype(B16)
    right = jnp.concatenate([second[j].astype(F32) for _, j in order], 0).astype(B16)
    return tn(left, right)


def renew(weight, moment, grad, scale, rate):
    new_moment = BETA * moment + scale * grad
    return weight - rate * new_moment, new_moment


def finish_kernel(members, replicas, group, *refs):
    chunks, rest = refs[:members], refs[members:]
    (a_ref, p_ref, own_ref, ownd_ref,
     w_ref, wd_ref, m_ref, md_ref, ein_ref, erest_ref, errd_ref, count_ref,
     vec_ref, vmom_ref, fin_ref, fmom_ref, emb_ref, emom_ref, head_ref, hmom_ref,
     loss_ref, total_ref, norm_ref, nq_ref, nqd_ref, nw_ref, nwd_ref, nm_ref, nmd_ref, ne_ref, ned_ref,
     nvec_ref, nvmom_ref, nfin_ref, nfmom_ref, nemb_ref, nemom_ref, nhead_ref, nhmom_ref, f_s) = rest
    wide_cols = w_ref.shape[1]
    hidden = wide_cols - 4 * D
    for place, ref in enumerate(chunks):
        f_s[:, spot(group, place, ref.shape[1], 128)] = ref[...]
    factor, factor_down = f_s[:, 0:wide_cols], f_s[:, wide_cols : wide_cols + D]
    nq_ref[...] = factor
    nqd_ref[...] = factor_down
    a = a_ref[...]
    square = jnp.sum(a[40:47, 0:D] * a[40:47, 0:D]) + jnp.sum(a[48:56, 0:D] * a[48:56, 0:D])
    emb, top = a[56 : 56 + V, 0:D], a[56 + V : 56 + 2 * V, 0 : D + 1]
    square = square + jnp.sum(emb * emb) + jnp.sum(top * top)
    basis = p_ref[...]
    gram = exact_nt(basis[0:8, 0:D], basis[0:8, 0:D])
    square = square + jnp.sum(gram * exact_nt(factor, factor))
    gram = jnp.zeros((8, 8), F32)
    for part in range(1, basis.shape[0] // 8):
        piece = basis[8 * part : 8 * part + 8, 0:D]
        gram = gram + exact_nt(piece, piece)
    square = square + jnp.sum(gram * exact_nt(factor_down, factor_down))
    norm = jnp.sqrt(square)
    norm_ref[...] = jnp.broadcast_to(norm, norm_ref.shape)
    loss_ref[...] = a[47:48, 0:1]
    total_ref[...] = count_ref[0:1, 0:1]
    scale = jnp.minimum(1.0, CLIP / norm)

    approx = six(own_ref[...], factor)
    nw_ref[...], nm_ref[...] = renew(w_ref[...], m_ref[...], approx, scale, RATE_WIDE)
    share = approx * (1.0 / replicas)
    ne_ref[:, 0 : 3 * D] = ein_ref[...] - share[:, 0 : 3 * D]
    ne_ref[:, 3 * D : 4 * D] = erest_ref[:, hidden:] - share[:, 3 * D : 4 * D]
    ne_ref[:, 4 * D :] = erest_ref[:, 0:hidden] - share[:, 4 * D :]
    approx = six(ownd_ref[...], factor_down)
    nwd_ref[...], nmd_ref[...] = renew(wd_ref[...], md_ref[...], approx, scale, RATE_LOWER)
    ned_ref[...] = errd_ref[...] - approx * (1.0 / replicas)

    places = (40, 41, 42, 43, 44, 48, 49, 50, 51, 52, 53, 54, 55)
    for row, place in enumerate(places):
        cut = slice(D * row, D * row + D)
        nvec_ref[:, cut], nvmom_ref[:, cut] = renew(
            vec_ref[:, cut], vmom_ref[:, cut], a[place : place + 1, 0:D], scale, RATE_VECTOR
        )
    nfin_ref[...], nfmom_ref[...] = renew(fin_ref[...], fmom_ref[...], a[45:47, 0:D], scale, RATE_FINAL)
    nemb_ref[...], nemom_ref[...] = renew(emb_ref[...], emom_ref[...], emb, scale, RATE_EMBED)
    nhead_ref[...], nhmom_ref[...] = renew(head_ref[...], hmom_ref[...], top, scale, RATE_HEAD)


def swap(value, axis, bit):
    size = lax.axis_size(axis)
    return lax.ppermute(value, axis, [(i, i ^ bit) for i in range(size)])


def bits_of(axis):
    size, bit, out = lax.axis_size(axis), 1, []
    while bit < size:
        out.append(bit)
        bit *= 2
    return out


def tie(*values):
    return lax.optimization_barrier(values)


def send_chunks(pieces):
    return [pieces[0]] + [swap(piece, "grp", place) for place, piece in enumerate(pieces) if place]


def add_chunks(pieces, work=()):
    work, results = dict(work), {}

    def beside(turn, moved):
        if turn in work:
            moved, results[turn] = tie(moved, work[turn]())
        return moved

    got = beside(0, send_chunks(pieces))
    total = got[0]
    for piece in got[1:]:
        total = total + piece
    for turn, bit in enumerate(bits_of("rep")):
        total = total + beside(turn + 1, swap(total, "rep", bit))
    got = [total] + [swap(total, "grp", place) for place in range(1, len(pieces))]
    return beside(-1, got), results


def gather_start(value):
    first, *bits = reversed(bits_of("grp"))
    return [value, swap(value, "grp", first)]


def gather_end(pieces):
    first, *bits = reversed(bits_of("grp"))
    order = [0, first]
    for bit in bits:
        pieces = pieces + [swap(piece, "grp", bit) for piece in pieces]
        order = order + [place ^ bit for place in order]
    return [pieces[order.index(place)] for place in range(len(order))]


def halve_start(pieces):
    first, *bits = bits_of("grp")
    keep = [place for place in range(len(pieces)) if not place & first]
    return [(place, pieces[place], swap(pieces[place | first], "grp", first)) for place in keep]


def halve_end(pairs):
    first, *bits = bits_of("grp")
    (_, own, other), *others = pairs
    kept = [own, other]
    sums = {place: (mine.astype(F32) + theirs.astype(F32)).astype(B16) for place, mine, theirs in others}
    for bit in bits:
        kept.append(swap(sums[bit], "grp", bit))
        sums = {
            place: (sums[place].astype(F32) + swap(sums[place | bit], "grp", bit).astype(F32)).astype(B16)
            for place in sums
            if not place & bit
        }
    return kept


def whole(shape):
    return pl.BlockSpec(shape, lambda *_: (0,) * len(shape))


def shards(tokens, mask, targets, mats_d, mats_down, mom_d, mom_down, err_d, err_down, q_d, q_down,
           vectors, vec_mom, final_norm, final_mom, embed, embed_mom, head, head_mom):
    length = tokens.shape[1]
    wide = mats_d.shape[2]
    hidden = wide - 4 * D
    rows = mats_d.shape[1]
    rows_down = mats_down.shape[1]
    step = 256
    steps = length // step
    step_mid = 2 * step
    index = lax.axis_index("grp").astype(jnp.int32)
    group = index.reshape(1)
    members = lax.axis_size("grp")
    cosine, sine = tables(length)
    q_t, qd_t = q_d[0].T, q_down[0].T
    head_t = head.T
    err, errd = err_d[0, 0], err_down[0, 0]

    def call(kernel, name, grid, ins, outs, shapes, scratch=()):
        return pl.pallas_call(
            kernel,
            grid_spec=pltpu.PrefetchScalarGridSpec(
                num_scalar_prefetch=1, grid=grid, in_specs=ins, out_specs=outs, scratch_shapes=scratch
            ),
            out_shape=shapes,
            compiler_params=params(name),
            name=name,
        )

    shape = jax.ShapeDtypeStruct
    rounds = [("grp", bit) for bit in bits_of("grp")] + [("rep", bit) for bit in bits_of("rep")]

    def advance(value, times=1):
        for _ in range(min(times, len(rounds))):
            value = value + swap(value, *rounds.pop(0))
        return value

    cols = pl.BlockSpec((1, step), lambda i, *_: (0, i))
    flat = pl.BlockSpec((step, D), lambda i, *_: (i, 0))
    heads = pl.BlockSpec((HEADS, PAD, step), lambda i, *_: (0, 0, i))
    wave = pl.BlockSpec((HDIM, step), lambda i, *_: (0, i))
    ext = pl.BlockSpec((D + 16, step), lambda i, *_: (0, i))

    w_in = gather_start(mats_d[0][:, : 3 * D].astype(B16))
    counted = jnp.broadcast_to(jnp.sum(mask.astype(F32)), (8, 128))
    more = advance(counted)
    err_sketch = call(
        error_kernel, "error_sketch", (1,),
        [whole((rows, wide)), whole((rows_down, D)), whole((8, wide)), whole((8, D))],
        whole((40, WIDE)), shape((40, WIDE), F32), [pltpu.VMEM((8, WIDE), F32)],
    )(group, err, errd, q_t, qd_t)
    x, h, h_t = pl.pallas_call(
        embed_kernel,
        grid=(steps,),
        in_specs=[cols, whole((V, D)), whole(vectors.shape)],
        out_specs=[flat, flat, ext],
        out_shape=[shape((length, D), F32), shape((length, D), B16), shape((D + 16, length), B16)],
        scratch_shapes=[pltpu.VMEM((TOK, D), F32)],
        compiler_params=params("embed"),
        name="embed",
    )(tokens, embed, vectors)
    w_in, err_sketch, h, counted = tie(w_in, err_sketch, h, more)
    w_in = gather_end(w_in)
    rest = jnp.concatenate([mats_d[0][:, 4 * D :], mats_d[0][:, 3 * D : 4 * D]], 1).astype(B16)
    down = mats_down[0].astype(B16)
    more = advance(counted)
    w_in, counted, rest, down = tie(w_in, more, rest, down)
    w_rest, w_down = gather_start(rest), gather_start(down)
    more = advance(counted)
    query, keys, value = call(
        partial(project_kernel, members), "project", (steps,),
        [flat] + [whole((rows, 3 * D))] * members + [whole(vectors.shape), wave, wave],
        [heads] * 3, [shape((HEADS, PAD, length), B16)] * 3,
        [pltpu.VMEM((D, 3 * D), F32), pltpu.VMEM((D, 3 * D), B16)],
    )(group, h, *w_in, vectors, cosine, sine)
    query, counted = tie(query, more)

    half = HEADS // 2
    pair = 2
    turned = half // pair
    mixes, inverses, probs = [], [], []
    for part in range(2):
        one = pl.BlockSpec((pair, PAD, length), lambda i, part=part: (i + turned * part, 0, 0))
        more = advance(counted, 1 + part * len(rounds))
        mix, inverse, prob = pl.pallas_call(
            attend_kernel,
            grid=(turned,),
            in_specs=[one, one, one],
            out_specs=[
                pl.BlockSpec((pair * HDIM, length), lambda i: (i, 0)),
                pl.BlockSpec((pair, 1, length), lambda i: (i, 0, 0)),
                pl.BlockSpec((pair, length, length), lambda i: (i, 0, 0)),
            ],
            out_shape=[
                shape((half * HDIM, length), F32),
                shape((half, 1, length), F32),
                shape((half, length, length), B16),
            ],
            compiler_params=params("attend"),
            name="attend",
        )(query, keys, value)
        mix, query, counted, w_rest, w_down = tie(mix, query, more, w_rest, w_down)
        if part == 0:
            w_rest, w_down = gather_end(w_rest), gather_end(w_down)
        mixes.append(mix)
        inverses.append(inverse)
        probs.append(prob)

    cols2 = pl.BlockSpec((1, step_mid), lambda i, *_: (0, i))
    flat2 = pl.BlockSpec((step_mid, D), lambda i, *_: (i, 0))
    heads2 = pl.BlockSpec((HEADS, PAD, step_mid), lambda i, *_: (0, 0, i))
    everyone = [(rows, D + hidden)] * members + [(rows_down, D)] * members
    grad_mix, grad_mid, sketch, early, *grads = call(
        partial(middle_kernel, members), "feed_and_loss", (length // step_mid,),
        [pl.BlockSpec((half * HDIM, step_mid), lambda i, *_: (0, i))] * 2
        + [pl.BlockSpec((half, 1, step_mid), lambda i, *_: (0, 0, i))] * 2
        + [
            flat2, cols2, cols2, whole((8, 128)), whole(vectors.shape), whole((2, D)),
            whole((V, D + 1)), whole((8, wide)), whole((8, D)),
        ]
        + [whole(item) for item in everyone],
        [heads2, flat2, whole((40, WIDE)), whole((56, WIDE))] + [whole(item) for item in everyone],
        [
            shape((HEADS, PAD, length), B16),
            shape((length, D), F32),
            shape((40, WIDE), F32),
            shape((56, WIDE), F32),
        ]
        + [shape(item, B16) for item in everyone],
        [
            pltpu.VMEM((D + 16, D), F32),
            pltpu.VMEM((WIDE, hidden), F32),
            pltpu.VMEM((hidden, D), F32),
            pltpu.VMEM((TOK, WIDE), F32),
            pltpu.VMEM((step_mid, hidden), B16),
            pltpu.VMEM((step_mid, hidden), F32),
            pltpu.VMEM((D, D + hidden), F32),
            pltpu.VMEM((D, D + hidden), B16),
            pltpu.VMEM((hidden, D), B16),
        ],
    )(group, *mixes, *inverses, x, mask, targets, counted, vectors, final_norm, head_t, q_t, qd_t,
      *w_rest, *w_down)
    g_rest, g_down = grads[:members], grads[members:]
    all_down = send_chunks(g_down)
    all_rest = send_chunks(g_rest)

    grad_acts = []
    for part in range(2):
        two = pl.BlockSpec((pair, PAD, length), lambda i, part=part: (i + turned * part, 0, 0))
        grad_act = pl.pallas_call(
            attend_back_kernel,
            grid=(turned,),
            in_specs=[
                pl.BlockSpec((pair, length, length), lambda i: (i, 0, 0)),
                two, two, two, two, whole((HDIM, length)), whole((HDIM, length)),
            ],
            out_specs=pl.BlockSpec((3, pair * HDIM, length), lambda i: (0, i, 0)),
            out_shape=shape((3, half * HDIM, length), B16),
            compiler_params=params("attend_back"),
            name="attend_back",
        )(probs[part], query, keys, value, grad_mix, cosine, sine)
        grad_acts.append(grad_act)
    all_down, all_rest, grad_acts = tie(all_down, all_rest, grad_acts)

    act = pl.BlockSpec((3, half * HDIM, step), lambda i, *_: (0, 0, i))
    size = 128 // members
    ins = [(rows, 3 * D)] * members
    grads = call(
        partial(input_kernel, members), "input_grads", (steps,),
        [
            cols, act, act, ext, flat, flat,
            whole(vectors.shape), whole((8, wide)), whole((40, WIDE)), whole((40, WIDE)), whole((56, WIDE)),
        ]
        + [whole(item) for item in ins],
        [whole(item) for item in ins] + [whole((size, WIDE))] * members,
        [shape(item, B16) for item in ins] + [shape((size, WIDE), F32)] * members,
        [
            pltpu.VMEM((128, WIDE), F32), pltpu.VMEM((D + 16, 3 * D), F32), pltpu.VMEM((TOK, D), F32),
            pltpu.VMEM((D, 3 * D), F32), pltpu.VMEM((D, 3 * D), B16),
        ],
    )(group, tokens, *grad_acts, h_t, x, grad_mid, vectors, q_t, sketch, err_sketch, early, *w_in)
    g_in, pieces = grads[:members], grads[members:]
    half_in = halve_start(g_in)

    def merge(kernel, name, chunks, err, result):
        return lambda: pl.pallas_call(
            kernel, out_shape=shape(result, F32), compiler_params=params(name), name=name
        )(*chunks, err)

    chunks, merged = add_chunks(
        pieces,
        (
            (0, merge(merge_kernel, "merge_down", all_down, errd, errd.shape)),
            (1, lambda: halve_end(half_in)),
            (2, merge(merge_rest_kernel, "merge_rest", all_rest, err, (rows, D + hidden))),
        ),
    )
    merged_down, all_in, merged_rest = (merged[turn] for turn in range(3))
    span = -(-(wide + WIDE) // (128 * members)) * 128
    shared, basis, own, ownd, *pieces = call(
        partial(factor_kernel, members), "left_factors", (1,),
        [whole((size, WIDE))] * members + [whole(item) for item in ins + everyone]
        + [whole((rows, wide)), whole((rows_down, D))],
        [whole((128, WIDE)), whole((40, WIDE)), whole((8, rows)), whole((8, rows_down))]
        + [whole((8, span))] * members,
        [
            shape((128, WIDE), F32), shape((40, WIDE), F32), shape((8, rows), F32), shape((8, rows_down), F32),
        ]
        + [shape((8, span), F32)] * members,
        [pltpu.VMEM((8, span * members), F32)],
    )(group, *chunks, *g_in, *g_rest, *g_down, err, errd)

    chunks, merged = add_chunks(
        pieces, ((0, merge(merge_in_kernel, "merge_in", all_in, err, (rows, 3 * D))),)
    )
    merged_in = merged[0]

    same = lambda value: shape(value.shape, F32)
    replicas = lax.axis_size("rep")
    small = (vectors, vec_mom, final_norm, final_mom, embed, embed_mom, head_t, head_mom.T)
    given = (
        *chunks, shared, basis, own, ownd,
        mats_d[0], mats_down[0], mom_d[0], mom_down[0], merged_in, merged_rest, merged_down, counted, *small,
    )
    shapes = [
        shape((1, 1), F32), shape((1, 1), F32), shape((1, 1), F32), shape((8, wide), F32), shape((8, D), F32),
        same(mats_d[0]), same(mats_down[0]), same(mats_d[0]), same(mats_down[0]), same(err), same(errd),
    ] + [same(item) for item in small]
    outs = call(
        partial(finish_kernel, members, replicas), "finish", (1,),
        [whole(item.shape) for item in given], [whole(item.shape) for item in shapes], shapes,
        [pltpu.VMEM((8, span * members), F32)],
    )(group, *given)
    (loss, total, norm, new_q, new_qd, new_wide, new_down, new_mom_wide, new_mom_dn, new_err, new_errd,
     new_vec, new_vmom, new_fin, new_fmom, new_emb, new_emom, new_head, new_hmom) = outs
    return (
        loss.reshape(()),
        total.reshape(()),
        norm.reshape(()),
        new_wide[None],
        new_down[None],
        new_mom_wide[None],
        new_mom_dn[None],
        new_err[None, None],
        new_errd[None, None],
        own.T[None],
        ownd.T[None],
        new_q.T[None],
        new_qd.T[None],
        new_vec,
        new_vmom,
        new_fin,
        new_fmom,
        new_emb,
        new_emom,
        new_head.T,
        new_hmom.T,
    )


def solution(mesh):
    whole_seq = P(("rep", "grp"), None)
    by_rows = P(None, "grp", None)
    by_replica = P("rep", None, "grp", None)
    placed = (
        (whole_seq,) * 3 + (by_rows,) * 4 + (by_replica,) * 2 + (P(),) * 10
    )
    given = (P(),) * 3 + (by_rows,) * 4 + (by_replica,) * 2 + (by_rows,) * 2 + (P(),) * 10
    return jax.shard_map(shards, mesh=mesh, in_specs=placed, out_specs=given, check_vma=False)
```

```python
from functools import partial

import jax
import jax.numpy as jnp
import numpy as np
from jax import lax
from jax.experimental import pallas as pl
from jax.experimental.pallas import tpu as pltpu
from jax.sharding import PartitionSpec as P

D = 480
HEADS = 20
HDIM = 24
V = 33
PAD = 32
TOK = 40
WIDE = 512
EPS = 1e-05
BETA = 0.9
RATE_WIDE = 20000.0
RATE_LOWER = 3000.0
RATE_VECTOR = 20000.0
RATE_FINAL = 40000.0
RATE_EMBED = 60000.0
RATE_HEAD = 3000.0
CLIP = 0.005
F32 = jnp.float32
B16 = jnp.bfloat16
MIB = 2**20


ROOM = {
    "error_sketch": 16, "embed": 16, "project": 24, "attend": 30, "feed_and_loss": 56, "attend_back": 30,
    "input_grads": 30, "left_factors": 24, "merge_down": 12, "merge_rest": 16, "merge_in": 16, "finish": 30,
}


def params(name):
    return pltpu.CompilerParams(vmem_limit_bytes=ROOM[name] * MIB)


def nn(left, right):
    return jnp.dot(left, right, preferred_element_type=F32)


def nt(left, right):
    return lax.dot_general(left, right, (((1,), (1,)), ((), ())), preferred_element_type=F32)


def tn(left, right):
    return lax.dot_general(left, right, (((0,), (0,)), ((), ())), preferred_element_type=F32)


def thirds(value):
    top = value.astype(B16)
    rest = value - top.astype(F32)
    middle = rest.astype(B16)
    return top, middle, (rest - middle.astype(F32)).astype(B16)


def thirds_rows(value):
    return jnp.concatenate([part.astype(F32) for part in thirds(value)], 0).astype(B16)


def fold_rows(value):
    return value[0:8] + value[8:16] + value[16:24]


def exact_nt(left, right):
    return lax.dot_general(
        left, right, (((1,), (1,)), ((), ())),
        precision=lax.Precision.HIGHEST, preferred_element_type=F32,
    )


def exact_nn(left, right):
    return jnp.dot(left, right, precision=lax.Precision.HIGHEST, preferred_element_type=F32)


def three_nt(left, right):
    three = thirds_rows(left)
    top, middle, low = thirds(right)
    return fold_rows(nt(three, top) + nt(three, middle) + nt(three, low))


def three_nn(left, right):
    three = thirds_rows(left)
    top, middle, low = thirds(right)
    return fold_rows(nn(three, top) + nn(three, middle) + nn(three, low))


def norm_parts(value):
    center = value - jnp.mean(value, -1, keepdims=True)
    spread = jnp.mean(center * center, -1, keepdims=True)
    rstd = lax.rsqrt(spread + EPS)
    return center * rstd, rstd


def norm_back(grad, unit, rstd, gain):
    inner = grad * gain
    first = jnp.mean(inner, -1, keepdims=True)
    second = jnp.mean(inner * unit, -1, keepdims=True)
    return (
        rstd * (inner - first - unit * second),
        jnp.sum(grad * unit, 0, keepdims=True),
        jnp.sum(grad, 0, keepdims=True),
    )


def half_turn(value):
    return jnp.concatenate([value[HDIM // 2 :], value[: HDIM // 2]], 0)


def tail(rows, cols, ones):
    index = lax.broadcasted_iota(jnp.int32, (rows, cols), 0)
    return jnp.where(index < ones, 1.0, 0.0).astype(F32)


def lane_tail(rows, cols):
    index = lax.broadcasted_iota(jnp.int32, (rows, cols), 1)
    return jnp.where(index == 0, 1.0, 0.0).astype(F32)


def tables(length):
    half = HDIM // 2
    freq = np.float32(10000.0) ** (-np.arange(half, dtype=np.float32) * np.float32(2.0) / np.float32(HDIM))
    angle = np.arange(length, dtype=np.float32)[None, :] * freq.astype(np.float32)[:, None]
    cosine, sine = np.cos(angle), np.sin(angle)
    return (
        jnp.asarray(np.concatenate([cosine, cosine], 0), F32),
        jnp.asarray(np.concatenate([-sine, sine], 0), F32),
    )


def error_kernel(group, err_ref, errd_ref, q_ref, qd_ref, out_ref, row_ref):
    rows = err_ref.shape[0]
    out_ref[...] = jnp.zeros_like(out_ref)
    row_ref[...] = jnp.zeros_like(row_ref)
    row_ref[:, 0:rows] = three_nt(q_ref[...], err_ref[...])
    out_ref[0:8, :] = pltpu.roll(row_ref[...], rows * group[0], 1)
    start = pl.multiple_of(8 + 8 * group[0], 8)
    out_ref[pl.ds(start, 8), 0:D] = three_nt(qd_ref[...], errd_ref[...])


def embed_kernel(tok_ref, emb_ref, vec_ref, x_ref, h_ref, ht_ref, emb_s):
    step = tok_ref.shape[1]

    @pl.when(pl.program_id(0) == 0)
    def _():
        emb_s[...] = jnp.zeros_like(emb_s)
        emb_s[0:V, :] = emb_ref[...]

    index = lax.broadcasted_iota(jnp.int32, (TOK, step), 0)
    hot = jnp.where(index == tok_ref[...], 1.0, 0.0).astype(F32)
    hot = jnp.concatenate([hot, hot, hot], 0).astype(B16)
    x = tn(hot, thirds_rows(emb_s[...]))
    x_ref[...] = x
    unit, _ = norm_parts(x)
    normed = unit * vec_ref[:, 0:D] + vec_ref[:, D : 2 * D]
    h_ref[...] = normed.astype(B16)
    ht_ref[...] = jnp.concatenate([normed.T, tail(16, step, 1)], 0).astype(B16)


def spot(group, place, size, unit):
    return pl.ds(pl.multiple_of((group[0] ^ place) * size, unit), size)


def assemble(group, chunks, wide_s, out_s):
    for place, ref in enumerate(chunks):
        wide_s[spot(group, place, ref.shape[0], 8), :] = ref[...].astype(F32)
    out_s[...] = wide_s[...].astype(B16)


def project_kernel(members, group, h_ref, *refs):
    chunks = refs[:members]
    vec_ref, cos_ref, sin_ref, q_ref, k_ref, v_ref, wide_s, w_s = refs[members:]
    step = h_ref.shape[0]

    @pl.when(pl.program_id(0) == 0)
    def _():
        assemble(group, chunks, wide_s, w_s)

    act = nn(h_ref[...], w_s[...]) + vec_ref[:, 2 * D : 5 * D]
    turned = act.T
    cosine, sine = cos_ref[...], sin_ref[...]
    zeros = tail(PAD - HDIM, step, 0)
    ones = tail(PAD - HDIM, step, 3)
    for head in range(HEADS):
        low = HDIM * head
        query = turned[low : low + HDIM]
        query = (query * cosine + half_turn(query) * sine) * HDIM ** (-0.5)
        q_ref[head] = jnp.concatenate([query, zeros], 0).astype(B16)
        keys = turned[D + low : D + low + HDIM]
        keys = keys * cosine + half_turn(keys) * sine
        k_ref[head] = jnp.concatenate([keys, ones], 0).astype(B16)
        value = turned[2 * D + low : 2 * D + low + HDIM]
        v_ref[head] = jnp.concatenate([value, ones], 0).astype(B16)


def rows_of(value):
    return value.astype(F32).T.astype(B16)


def attend_kernel(q_ref, k_ref, v_ref, *refs):
    mix_ref, inv_ref, p_ref = refs[-3:]
    count, _, length = q_ref.shape
    zeros = tail(PAD - HDIM - 3, length, 0)

    def first(head):
        keys = rows_of(k_ref[head])
        query = q_ref[head]
        top = jnp.max(nn(keys, query), 0, keepdims=True)
        parts = [part.astype(F32) for part in thirds(-top)]
        return keys, jnp.concatenate([query[0:HDIM].astype(F32)] + parts + [zeros], 0).astype(B16)

    def second(head, keys, query):
        probs = jnp.exp(nn(keys, query)).astype(B16)
        p_ref[head] = probs
        out = nn(v_ref[head], probs)
        inverse = 1.0 / out[HDIM : HDIM + 1]
        mix_ref[HDIM * head : HDIM * head + HDIM, :] = out[0:HDIM] * inverse
        inv_ref[head] = inverse

    held = first(0)
    for head in range(count):
        ahead = first(head + 1) if head + 1 < count else None
        second(head, *held)
        held = ahead


def gelu_parts(upper):
    size = jnp.abs(upper) * (0.5**0.5)
    bell = jnp.exp(-0.5 * upper * upper)
    t = 1.0 / (1.0 + 0.3275911 * size)
    poly = t * (0.254829592 + t * (-0.284496736 + t * (1.421413741 + t * (-1.453152027 + t * 1.061405429))))
    lower = 0.5 * poly * bell
    cdf = jnp.where(upper < 0, lower, 1.0 - lower)
    return upper * cdf, cdf + upper * (0.3989422804014327 * bell)


def middle_kernel(members, group, mixa_ref, mixb_ref, inva_ref, invb_ref, x_ref, mask_ref, tgt_ref,
                  count_ref, vec_ref, fin_ref, head_ref, q_ref, qd_ref, *refs):
    chunks, chunks_down, refs = refs[:members], refs[members : 2 * members], refs[2 * members :]
    dm_ref, dx_ref, s_ref, e_ref, *refs = refs
    outs, outs_down, refs = refs[:members], refs[members : 2 * members], refs[2 * members :]
    acc_o, acc_u, acc_d, head_s, hid_s, slope_s, wide_s, wr_ref, wd_ref = refs
    pid = pl.program_id(0)
    step = x_ref.shape[0]
    wide = wd_ref.shape[0]
    wo = slice(wide, wide + D)

    @pl.when(pid == 0)
    def _():
        acc_o[...] = jnp.zeros_like(acc_o)
        acc_u[...] = jnp.zeros_like(acc_u)
        acc_d[...] = jnp.zeros_like(acc_d)
        e_ref[...] = jnp.zeros_like(e_ref)
        s_ref[...] = jnp.zeros_like(s_ref)
        head_s[...] = jnp.zeros_like(head_s)
        head_s[0:V, 0 : D + 1] = head_ref[...]
        assemble(group, chunks, wide_s, wr_ref)
        for place, ref in enumerate(chunks_down):
            wd_ref[spot(group, place, ref.shape[0], 16), :] = ref[...]

    mix = jnp.concatenate([mixa_ref[...], mixb_ref[...]], 0)
    half = inva_ref.shape[0]
    mixed = jnp.concatenate([mix, tail(16, step, 1)], 0).astype(B16)
    middle = x_ref[...] + tn(mixed[0:D], wr_ref[:, wo]) + vec_ref[:, 5 * D : 6 * D]
    unit2, rstd2 = norm_parts(middle)
    gain2 = vec_ref[:, 6 * D : 7 * D]
    normed2 = unit2 * gain2 + vec_ref[:, 7 * D : 8 * D]
    normed2 = jnp.concatenate([normed2, lane_tail(step, WIDE - D)], 1).astype(B16)
    bias_up = vec_ref[:, 9 * D :]
    block = 384
    for low in range(0, wide, block):
        cut = slice(low, low + block)
        upper = nn(normed2[:, 0:D], wr_ref[:, cut]) + bias_up[:, cut]
        hidden, slope = gelu_parts(upper)
        hid_s[:, cut] = hidden.astype(B16)
        slope_s[:, cut] = slope
    resid = middle + nn(hid_s[...], wd_ref[...]) + vec_ref[:, 8 * D : 9 * D]
    unit3, rstd3 = norm_parts(resid)
    final = unit3 * fin_ref[0:1, :] + fin_ref[1:2, :]
    final = jnp.concatenate([final, lane_tail(step, WIDE - D)], 1).astype(B16)

    lanes = lax.broadcasted_iota(jnp.int32, (TOK, WIDE), 1)
    bias = jnp.sum(jnp.where(lanes == D, head_s[...], 0.0), 1, keepdims=True)
    table = head_s[:, 0:D].astype(B16)
    rows = lax.broadcasted_iota(jnp.int32, (TOK, step), 0)
    logits = jnp.where(rows < V, nt(table, final[:, 0:D]) + bias, -1e30)
    shifted = logits - jnp.max(logits, 0, keepdims=True)
    expo = jnp.exp(shifted)
    total = jnp.sum(expo, 0, keepdims=True)
    picks = rows == tgt_ref[...]
    weight = mask_ref[...].astype(F32)
    picked = jnp.sum(jnp.where(picks, shifted, 0.0), 0, keepdims=True)
    loss = jnp.sum((jnp.log(total) - picked) * weight, 1, keepdims=True)
    grad_logits = (expo / total - jnp.where(picks, 1.0, 0.0)) * (weight * (1.0 / count_ref[0:1, 0:1]))
    grad_logits = grad_logits.astype(B16)
    e_ref[16 : 16 + TOK, :] += nn(grad_logits, final)
    grad_resid, grad_fg, grad_fb = norm_back(tn(grad_logits, table), unit3, rstd3, fin_ref[0:1, :])

    grad_y = grad_resid.astype(B16)
    acc_d[...] += tn(hid_s[...], grad_y)
    for low in range(0, wide, block):
        cut = slice(low, low + block)
        grad_hidden = nt(grad_y, wd_ref[cut, :])
        hid_s[:, cut] = (grad_hidden * slope_s[:, cut]).astype(B16)
    acc_u[...] += tn(normed2, hid_s[...])
    grad_mid, grad_g2, grad_b2 = norm_back(nt(hid_s[...], wr_ref[:, 0:wide]), unit2, rstd2, gain2)
    grad_mid = grad_mid + grad_resid
    dx_ref[...] = grad_mid
    branch = grad_mid.astype(B16)
    acc_o[...] += nn(mixed, branch)
    grad_mixed = nt(wr_ref[:, wo], branch).astype(B16).astype(F32)
    zeros = tail(PAD - HDIM - 3, step, 0)
    for head in range(HEADS):
        cut = slice(HDIM * head, HDIM * head + HDIM)
        inverse = inva_ref[head] if head < half else invb_ref[head - half]
        scaled = (grad_mixed[cut] * inverse).astype(B16).astype(F32)
        delta = -jnp.sum(scaled * mix[cut], 0, keepdims=True)
        top, mid, low = thirds(delta)
        dm_ref[head] = jnp.concatenate(
            [scaled, top.astype(F32), mid.astype(F32), low.astype(F32), zeros], 0
        ).astype(B16)
    e_ref[1:2, 0:D] += grad_g2
    e_ref[2:3, 0:D] += grad_b2
    e_ref[3:4, 0:D] += jnp.sum(grad_y.astype(F32), 0, keepdims=True)
    e_ref[8:9, 0:D] += grad_fg
    e_ref[9:10, 0:D] += grad_fb
    e_ref[10:11, :] += jnp.broadcast_to(loss, (1, WIDE))

    @pl.when(pid == pl.num_programs(0) - 1)
    def _():
        e_ref[0:1, 0:D] = acc_o[D : D + 1, :]
        for part in range(wide // D):
            e_ref[4 + part : 5 + part, 0:D] = acc_u[D : D + 1, D * part : D * part + D]
        go = acc_o[0:D, :].astype(B16)
        gu = acc_u[0:D, :].astype(B16)
        sketch = nt(thirds_rows(q_ref[:, 3 * D : 4 * D]), go) + nt(thirds_rows(q_ref[:, 4 * D :]), gu)
        s_ref[0:8, 0:D] = fold_rows(sketch)
        start = thirds_rows(qd_ref[...])
        for part in range(wide // D):
            piece = nt(start, acc_d[D * part : D * part + D, :].astype(B16))
            s_ref[8 + 8 * part : 16 + 8 * part, 0:D] = fold_rows(piece)
        for place, ref in enumerate(outs):
            at = spot(group, place, ref.shape[0], 8)
            ref[:, 0:wide] = acc_u[at, :].astype(B16)
            ref[:, wo] = acc_o[at, :].astype(B16)
        for place, ref in enumerate(outs_down):
            ref[...] = acc_d[spot(group, place, ref.shape[0], 8), :].astype(B16)


def attend_back_kernel(p_ref, q_ref, k_ref, v_ref, dm_ref, cos_ref, sin_ref, da_ref):
    cosine, sine = cos_ref[...], sin_ref[...]
    parts = [[], [], []]
    for head in range(p_ref.shape[0]):
        probs = p_ref[head]
        grad = dm_ref[head]
        slope = nn(rows_of(v_ref[head]), grad)
        grad_scores = (probs.astype(F32) * slope).astype(B16)
        grad_value = nt(grad, probs)[0:HDIM]
        grad_keys = nt(q_ref[head], grad_scores)[0:HDIM]
        grad_query = nn(k_ref[head], grad_scores)[0:HDIM] * HDIM ** (-0.5)
        parts[0].append(grad_query * cosine + half_turn(grad_query * sine))
        parts[1].append(grad_keys * cosine + half_turn(grad_keys * sine))
        parts[2].append(grad_value)
    for index in range(3):
        da_ref[index] = jnp.concatenate(parts[index], 0).astype(B16)


def input_kernel(members, group, tok_ref, da_ref, h_ref, x_ref, dx_ref, vec_ref, q_ref,
                 s_ref, serr_ref, e_ref, *refs):
    chunks, refs = refs[:members], refs[members:]
    outs, pieces, refs = refs[:members], refs[members : 2 * members], refs[2 * members :]
    out_ref, acc_w, acc_e, wide_s, w_s = refs
    pid = pl.program_id(0)
    step = x_ref.shape[0]

    @pl.when(pid == 0)
    def _():
        acc_w[...] = jnp.zeros_like(acc_w)
        acc_e[...] = jnp.zeros_like(acc_e)
        out_ref[...] = jnp.zeros_like(out_ref)
        assemble(group, chunks, wide_s, w_s)

    da = da_ref[...].reshape(3 * D, step)
    acc_w[...] += nt(h_ref[...], da)
    grad = nn(w_s[...], da).T
    unit, rstd = norm_parts(x_ref[...])
    grad_x, grad_g, grad_b = norm_back(grad, unit, rstd, vec_ref[:, 0:D])
    grad_x = grad_x + dx_ref[...]
    index = lax.broadcasted_iota(jnp.int32, (TOK, step), 0)
    hot = jnp.where(index == tok_ref[...], 1.0, 0.0).astype(B16)
    for part in thirds(grad_x):
        acc_e[...] += nn(hot, part)
    out_ref[40:41, 0:D] += grad_g
    out_ref[41:42, 0:D] += grad_b

    @pl.when(pid == pl.num_programs(0) - 1)
    def _():
        for part in range(3):
            out_ref[42 + part : 43 + part, 0:D] = acc_w[D : D + 1, D * part : D * part + D]
        out_ref[0:40, :] = s_ref[...] + serr_ref[...]
        out_ref[0:8, 0:D] += fold_rows(nt(thirds_rows(q_ref[:, 0 : 3 * D]), acc_w[0:D, :].astype(B16)))
        out_ref[45:48, :] = e_ref[8:11, :]
        out_ref[48:56, :] = e_ref[0:8, :]
        out_ref[56 : 56 + V, 0:D] = acc_e[0:V, :]
        out_ref[56 + V : 56 + 2 * V, :] = e_ref[16 : 16 + V, :]
        for place, ref in enumerate(outs):
            ref[...] = acc_w[spot(group, place, ref.shape[0], 8), :].astype(B16)
        for place, ref in enumerate(pieces):
            ref[...] = out_ref[spot(group, place, ref.shape[0], 8), :]


def orthonormal(sketch, gram):
    basis = jnp.zeros_like(sketch[0])
    count = gram.shape[0]
    index = lax.broadcasted_iota(jnp.int32, (count, 1), 0)
    out = [jnp.zeros_like(part) for part in sketch]
    left = list(sketch)
    for step in range(count):
        pivot = gram[step : step + 1, step : step + 1]
        scale = 1.0 / jnp.sqrt(pivot)
        column = gram[:, step : step + 1] * scale
        row = gram[step : step + 1, :] * scale
        column = jnp.where(index > step, column, 0.0)
        gram = gram - column * row
        for place in range(len(left)):
            base = left[place][step : step + 1, :] * scale
            out[place] = jnp.where(index == step, base, out[place])
            left[place] = left[place] - column * base
    return out


def factor_kernel(members, group, *refs):
    chunks, ins, rests, downs = (refs[members * part : members * part + members] for part in range(4))
    err_ref, errd_ref, a_ref, p_ref, own_ref, ownd_ref, *refs = refs[4 * members :]
    outs, f_s = refs[:members], refs[members]
    rows, wide_cols = err_ref.shape
    hidden = wide_cols - 4 * D
    parts = hidden // D
    for place, ref in enumerate(chunks):
        a_ref[spot(group, place, ref.shape[0], 8), :] = ref[...]
    wide = a_ref[0:8, 0:D]
    down = [a_ref[8 + 8 * part : 16 + 8 * part, 0:D] for part in range(parts)]
    gram = exact_nt(wide, wide)
    (wide,) = orthonormal([wide], gram)
    gram = exact_nt(down[0], down[0])
    for part in range(1, parts):
        gram = gram + exact_nt(down[part], down[part])
    down = orthonormal(down, gram)
    p_ref[...] = jnp.zeros_like(p_ref)
    p_ref[0:8, 0:D] = wide
    for part in range(parts):
        p_ref[8 + 8 * part : 16 + 8 * part, 0:D] = down[part]
    f_s[...] = jnp.zeros_like(f_s)
    for place in range(members):
        piece = pltpu.roll(p_ref[0:8, :], (WIDE - rows * (group[0] ^ place)) % WIDE, 1)[:, 0:rows]
        piece_down = p_ref[pl.ds(pl.multiple_of(8 + 8 * (group[0] ^ place), 8), 8), :][:, 0:D]
        if place == 0:
            own_ref[...] = piece
            ownd_ref[...] = piece_down
            f_s[:, 0:wide_cols] = three_nn(piece, err_ref[...])
            f_s[:, wide_cols : wide_cols + D] = three_nn(piece_down, errd_ref[...])
        three = thirds_rows(piece)
        f_s[:, 0 : 3 * D] += fold_rows(nn(three, ins[place][...]))
        f_s[:, 4 * D : wide_cols] += fold_rows(nn(three, rests[place][:, 0:hidden]))
        f_s[:, 3 * D : 4 * D] += fold_rows(nn(three, rests[place][:, hidden:]))
        f_s[:, wide_cols : wide_cols + D] += fold_rows(nn(thirds_rows(piece_down), downs[place][...]))
    for place, ref in enumerate(outs):
        ref[...] = f_s[:, spot(group, place, ref.shape[1], 128)]


def merge_kernel(*refs):
    *chunks, err_ref, out_ref = refs
    value = err_ref[...]
    for ref in chunks:
        value = value + ref[...].astype(F32)
    out_ref[...] = value


def merge_rest_kernel(*refs):
    *chunks, err_ref, out_ref = refs
    value = chunks[0][...].astype(F32)
    for ref in chunks[1:]:
        value = value + ref[...].astype(F32)
    hidden = value.shape[1] - D
    out_ref[:, 0:hidden] = value[:, 0:hidden] + err_ref[:, 4 * D :]
    out_ref[:, hidden:] = value[:, hidden:] + err_ref[:, 3 * D : 4 * D]


def merge_in_kernel(*refs):
    *chunks, err_ref, out_ref = refs
    value = err_ref[:, 0 : 3 * D]
    for ref in chunks:
        value = value + ref[...].astype(F32)
    out_ref[...] = value


def six(left, right):
    first, second = thirds(left), thirds(right)
    order = ((0, 0), (0, 1), (1, 0), (1, 1), (0, 2), (2, 0))
    left = jnp.concatenate([first[i].astype(F32) for i, _ in order], 0).astype(B16)
    right = jnp.concatenate([second[j].astype(F32) for _, j in order], 0).astype(B16)
    return tn(left, right)


def renew(weight, moment, grad, scale, rate):
    new_moment = BETA * moment + scale * grad
    return weight - rate * new_moment, new_moment


def finish_kernel(members, replicas, group, *refs):
    chunks, rest = refs[:members], refs[members:]
    (a_ref, p_ref, own_ref, ownd_ref,
     w_ref, wd_ref, m_ref, md_ref, ein_ref, erest_ref, errd_ref, count_ref,
     vec_ref, vmom_ref, fin_ref, fmom_ref, emb_ref, emom_ref, head_ref, hmom_ref,
     loss_ref, total_ref, norm_ref, nq_ref, nqd_ref, nw_ref, nwd_ref, nm_ref, nmd_ref, ne_ref, ned_ref,
     nvec_ref, nvmom_ref, nfin_ref, nfmom_ref, nemb_ref, nemom_ref, nhead_ref, nhmom_ref, f_s) = rest
    wide_cols = w_ref.shape[1]
    hidden = wide_cols - 4 * D
    for place, ref in enumerate(chunks):
        f_s[:, spot(group, place, ref.shape[1], 128)] = ref[...]
    factor, factor_down = f_s[:, 0:wide_cols], f_s[:, wide_cols : wide_cols + D]
    nq_ref[...] = factor
    nqd_ref[...] = factor_down
    a = a_ref[...]
    square = jnp.sum(a[40:47, 0:D] * a[40:47, 0:D]) + jnp.sum(a[48:56, 0:D] * a[48:56, 0:D])
    emb, top = a[56 : 56 + V, 0:D], a[56 + V : 56 + 2 * V, 0 : D + 1]
    square = square + jnp.sum(emb * emb) + jnp.sum(top * top)
    basis = p_ref[...]
    gram = exact_nt(basis[0:8, 0:D], basis[0:8, 0:D])
    square = square + jnp.sum(gram * exact_nt(factor, factor))
    gram = jnp.zeros((8, 8), F32)
    for part in range(1, basis.shape[0] // 8):
        piece = basis[8 * part : 8 * part + 8, 0:D]
        gram = gram + exact_nt(piece, piece)
    square = square + jnp.sum(gram * exact_nt(factor_down, factor_down))
    norm = jnp.sqrt(square)
    norm_ref[...] = jnp.broadcast_to(norm, norm_ref.shape)
    loss_ref[...] = a[47:48, 0:1]
    total_ref[...] = count_ref[0:1, 0:1]
    scale = jnp.minimum(1.0, CLIP / norm)

    approx = six(own_ref[...], factor)
    nw_ref[...], nm_ref[...] = renew(w_ref[...], m_ref[...], approx, scale, RATE_WIDE)
    share = approx * (1.0 / replicas)
    ne_ref[:, 0 : 3 * D] = ein_ref[...] - share[:, 0 : 3 * D]
    ne_ref[:, 3 * D : 4 * D] = erest_ref[:, hidden:] - share[:, 3 * D : 4 * D]
    ne_ref[:, 4 * D :] = erest_ref[:, 0:hidden] - share[:, 4 * D :]
    approx = six(ownd_ref[...], factor_down)
    nwd_ref[...], nmd_ref[...] = renew(wd_ref[...], md_ref[...], approx, scale, RATE_LOWER)
    ned_ref[...] = errd_ref[...] - approx * (1.0 / replicas)

    places = (40, 41, 42, 43, 44, 48, 49, 50, 51, 52, 53, 54, 55)
    for row, place in enumerate(places):
        cut = slice(D * row, D * row + D)
        nvec_ref[:, cut], nvmom_ref[:, cut] = renew(
            vec_ref[:, cut], vmom_ref[:, cut], a[place : place + 1, 0:D], scale, RATE_VECTOR
        )
    nfin_ref[...], nfmom_ref[...] = renew(fin_ref[...], fmom_ref[...], a[45:47, 0:D], scale, RATE_FINAL)
    nemb_ref[...], nemom_ref[...] = renew(emb_ref[...], emom_ref[...], emb, scale, RATE_EMBED)
    nhead_ref[...], nhmom_ref[...] = renew(head_ref[...], hmom_ref[...], top, scale, RATE_HEAD)


def swap(value, axis, bit):
    size = lax.axis_size(axis)
    return lax.ppermute(value, axis, [(i, i ^ bit) for i in range(size)])


def bits_of(axis):
    size, bit, out = lax.axis_size(axis), 1, []
    while bit < size:
        out.append(bit)
        bit *= 2
    return out


def tie(*values):
    return lax.optimization_barrier(values)


def send_chunks(pieces):
    return [pieces[0]] + [swap(piece, "grp", place) for place, piece in enumerate(pieces) if place]


def add_chunks(pieces, work=()):
    work, results = dict(work), {}

    def beside(turn, moved):
        if turn in work:
            moved, results[turn] = tie(moved, work[turn]())
        return moved

    got = beside(0, send_chunks(pieces))
    total = got[0]
    for piece in got[1:]:
        total = total + piece
    for turn, bit in enumerate(bits_of("rep")):
        total = total + beside(turn + 1, swap(total, "rep", bit))
    got = [total] + [swap(total, "grp", place) for place in range(1, len(pieces))]
    return beside(-1, got), results


def gather_start(value):
    first, *bits = reversed(bits_of("grp"))
    return [value, swap(value, "grp", first)]


def gather_end(pieces):
    first, *bits = reversed(bits_of("grp"))
    order = [0, first]
    for bit in bits:
        pieces = pieces + [swap(piece, "grp", bit) for piece in pieces]
        order = order + [place ^ bit for place in order]
    return [pieces[order.index(place)] for place in range(len(order))]


def halve_start(pieces):
    first, *bits = bits_of("grp")
    keep = [place for place in range(len(pieces)) if not place & first]
    return [(place, pieces[place], swap(pieces[place | first], "grp", first)) for place in keep]


def halve_end(pairs):
    first, *bits = bits_of("grp")
    (_, own, other), *others = pairs
    kept = [own, other]
    sums = {place: (mine.astype(F32) + theirs.astype(F32)).astype(B16) for place, mine, theirs in others}
    for bit in bits:
        kept.append(swap(sums[bit], "grp", bit))
        sums = {
            place: (sums[place].astype(F32) + swap(sums[place | bit], "grp", bit).astype(F32)).astype(B16)
            for place in sums
            if not place & bit
        }
    return kept


def whole(shape):
    return pl.BlockSpec(shape, lambda *_: (0,) * len(shape))


def shards(tokens, mask, targets, mats_d, mats_down, mom_d, mom_down, err_d, err_down, q_d, q_down,
           vectors, vec_mom, final_norm, final_mom, embed, embed_mom, head, head_mom):
    length = tokens.shape[1]
    wide = mats_d.shape[2]
    hidden = wide - 4 * D
    rows = mats_d.shape[1]
    rows_down = mats_down.shape[1]
    step = 256
    steps = length // step
    step_mid = 2 * step
    index = lax.axis_index("grp").astype(jnp.int32)
    group = index.reshape(1)
    members = lax.axis_size("grp")
    cosine, sine = tables(length)
    q_t, qd_t = q_d[0].T, q_down[0].T
    head_t = head.T
    err, errd = err_d[0, 0], err_down[0, 0]

    def call(kernel, name, grid, ins, outs, shapes, scratch=()):
        return pl.pallas_call(
            kernel,
            grid_spec=pltpu.PrefetchScalarGridSpec(
                num_scalar_prefetch=1, grid=grid, in_specs=ins, out_specs=outs, scratch_shapes=scratch
            ),
            out_shape=shapes,
            compiler_params=params(name),
            name=name,
        )

    shape = jax.ShapeDtypeStruct
    rounds = [("grp", bit) for bit in bits_of("grp")] + [("rep", bit) for bit in bits_of("rep")]

    def advance(value, times=1):
        for _ in range(min(times, len(rounds))):
            value = value + swap(value, *rounds.pop(0))
        return value

    cols = pl.BlockSpec((1, step), lambda i, *_: (0, i))
    flat = pl.BlockSpec((step, D), lambda i, *_: (i, 0))
    heads = pl.BlockSpec((HEADS, PAD, step), lambda i, *_: (0, 0, i))
    wave = pl.BlockSpec((HDIM, step), lambda i, *_: (0, i))
    ext = pl.BlockSpec((D + 16, step), lambda i, *_: (0, i))

    w_in = gather_start(mats_d[0][:, : 3 * D].astype(B16))
    counted = jnp.broadcast_to(jnp.sum(mask.astype(F32)), (8, 128))
    more = advance(counted)
    err_sketch = call(
        error_kernel, "error_sketch", (1,),
        [whole((rows, wide)), whole((rows_down, D)), whole((8, wide)), whole((8, D))],
        whole((40, WIDE)), shape((40, WIDE), F32), [pltpu.VMEM((8, WIDE), F32)],
    )(group, err, errd, q_t, qd_t)
    x, h, h_t = pl.pallas_call(
        embed_kernel,
        grid=(steps,),
        in_specs=[cols, whole((V, D)), whole(vectors.shape)],
        out_specs=[flat, flat, ext],
        out_shape=[shape((length, D), F32), shape((length, D), B16), shape((D + 16, length), B16)],
        scratch_shapes=[pltpu.VMEM((TOK, D), F32)],
        compiler_params=params("embed"),
        name="embed",
    )(tokens, embed, vectors)
    w_in, err_sketch, h, counted = tie(w_in, err_sketch, h, more)
    w_in = gather_end(w_in)
    rest = jnp.concatenate([mats_d[0][:, 4 * D :], mats_d[0][:, 3 * D : 4 * D]], 1).astype(B16)
    down = mats_down[0].astype(B16)
    more = advance(counted)
    w_in, counted, rest, down = tie(w_in, more, rest, down)
    w_rest, w_down = gather_start(rest), gather_start(down)
    more = advance(counted)
    query, keys, value = call(
        partial(project_kernel, members), "project", (steps,),
        [flat] + [whole((rows, 3 * D))] * members + [whole(vectors.shape), wave, wave],
        [heads] * 3, [shape((HEADS, PAD, length), B16)] * 3,
        [pltpu.VMEM((D, 3 * D), F32), pltpu.VMEM((D, 3 * D), B16)],
    )(group, h, *w_in, vectors, cosine, sine)
    query, counted = tie(query, more)

    half = HEADS // 2
    pair = 2
    turned = half // pair
    mixes, inverses, probs = [], [], []
    for part in range(2):
        one = pl.BlockSpec((1, PAD, length), lambda i, part=part: (i + half * part, 0, 0))
        more = advance(counted, 1 + part * len(rounds))
        mix, inverse, *probs = pl.pallas_call(
            attend_kernel,
            grid=(half,),
            in_specs=[one, one, one] + [pl.BlockSpec(memory_space=pl.ANY)] * len(probs),
            out_specs=[
                pl.BlockSpec((HDIM, length), lambda i: (i, 0)),
                pl.BlockSpec((1, 1, length), lambda i: (i, 0, 0)),
                pl.BlockSpec((1, length, length), lambda i, part=part: (i + half * part, 0, 0)),
            ],
            out_shape=[
                shape((half * HDIM, length), F32),
                shape((half, 1, length), F32),
                shape((HEADS, length, length), B16),
            ],
            input_output_aliases={3: 2} if probs else {},
            compiler_params=params("attend"),
            name="attend",
        )(query, keys, value, *probs)
        mix, query, counted, w_rest, w_down = tie(mix, query, more, w_rest, w_down)
        if part == 0:
            w_rest, w_down = gather_end(w_rest), gather_end(w_down)
        mixes.append(mix)
        inverses.append(inverse)

    cols2 = pl.BlockSpec((1, step_mid), lambda i, *_: (0, i))
    flat2 = pl.BlockSpec((step_mid, D), lambda i, *_: (i, 0))
    heads2 = pl.BlockSpec((HEADS, PAD, step_mid), lambda i, *_: (0, 0, i))
    everyone = [(rows, D + hidden)] * members + [(rows_down, D)] * members
    grad_mix, grad_mid, sketch, early, *grads = call(
        partial(middle_kernel, members), "feed_and_loss", (length // step_mid,),
        [pl.BlockSpec((half * HDIM, step_mid), lambda i, *_: (0, i))] * 2
        + [pl.BlockSpec((half, 1, step_mid), lambda i, *_: (0, 0, i))] * 2
        + [
            flat2, cols2, cols2, whole((8, 128)), whole(vectors.shape), whole((2, D)),
            whole((V, D + 1)), whole((8, wide)), whole((8, D)),
        ]
        + [whole(item) for item in everyone],
        [heads2, flat2, whole((40, WIDE)), whole((56, WIDE))] + [whole(item) for item in everyone],
        [
            shape((HEADS, PAD, length), B16),
            shape((length, D), F32),
            shape((40, WIDE), F32),
            shape((56, WIDE), F32),
        ]
        + [shape(item, B16) for item in everyone],
        [
            pltpu.VMEM((D + 16, D), F32),
            pltpu.VMEM((WIDE, hidden), F32),
            pltpu.VMEM((hidden, D), F32),
            pltpu.VMEM((TOK, WIDE), F32),
            pltpu.VMEM((step_mid, hidden), B16),
            pltpu.VMEM((step_mid, hidden), F32),
            pltpu.VMEM((D, D + hidden), F32),
            pltpu.VMEM((D, D + hidden), B16),
            pltpu.VMEM((hidden, D), B16),
        ],
    )(group, *mixes, *inverses, x, mask, targets, counted, vectors, final_norm, head_t, q_t, qd_t,
      *w_rest, *w_down)
    g_rest, g_down = grads[:members], grads[members:]
    all_down = send_chunks(g_down)
    all_rest = send_chunks(g_rest)

    two = pl.BlockSpec((pair, PAD, length), lambda i: (i, 0, 0))
    grad_act = pl.pallas_call(
        attend_back_kernel,
        grid=(HEADS // pair,),
        in_specs=[
            pl.BlockSpec((pair, length, length), lambda i: (i, 0, 0)),
            two, two, two, two, whole((HDIM, length)), whole((HDIM, length)),
        ],
        out_specs=pl.BlockSpec((3, pair * HDIM, length), lambda i: (0, i, 0)),
        out_shape=shape((3, D, length), B16),
        compiler_params=params("attend_back"),
        name="attend_back",
    )(*probs, query, keys, value, grad_mix, cosine, sine)
    all_down, all_rest, grad_act = tie(all_down, all_rest, grad_act)

    act = pl.BlockSpec((3, D, step), lambda i, *_: (0, 0, i))
    size = 128 // members
    ins = [(rows, 3 * D)] * members
    grads = call(
        partial(input_kernel, members), "input_grads", (steps,),
        [
            cols, act, ext, flat, flat,
            whole(vectors.shape), whole((8, wide)), whole((40, WIDE)), whole((40, WIDE)), whole((56, WIDE)),
        ]
        + [whole(item) for item in ins],
        [whole(item) for item in ins] + [whole((size, WIDE))] * members,
        [shape(item, B16) for item in ins] + [shape((size, WIDE), F32)] * members,
        [
            pltpu.VMEM((128, WIDE), F32), pltpu.VMEM((D + 16, 3 * D), F32), pltpu.VMEM((TOK, D), F32),
            pltpu.VMEM((D, 3 * D), F32), pltpu.VMEM((D, 3 * D), B16),
        ],
    )(group, tokens, grad_act, h_t, x, grad_mid, vectors, q_t, sketch, err_sketch, early, *w_in)
    g_in, pieces = grads[:members], grads[members:]
    half_in = halve_start(g_in)

    def merge(kernel, name, chunks, err, result):
        return lambda: pl.pallas_call(
            kernel, out_shape=shape(result, F32), compiler_params=params(name), name=name
        )(*chunks, err)

    chunks, merged = add_chunks(
        pieces,
        (
            (0, merge(merge_kernel, "merge_down", all_down, errd, errd.shape)),
            (1, lambda: halve_end(half_in)),
            (2, merge(merge_rest_kernel, "merge_rest", all_rest, err, (rows, D + hidden))),
        ),
    )
    merged_down, all_in, merged_rest = (merged[turn] for turn in range(3))
    span = -(-(wide + WIDE) // (128 * members)) * 128
    shared, basis, own, ownd, *pieces = call(
        partial(factor_kernel, members), "left_factors", (1,),
        [whole((size, WIDE))] * members + [whole(item) for item in ins + everyone]
        + [whole((rows, wide)), whole((rows_down, D))],
        [whole((128, WIDE)), whole((40, WIDE)), whole((8, rows)), whole((8, rows_down))]
        + [whole((8, span))] * members,
        [
            shape((128, WIDE), F32), shape((40, WIDE), F32), shape((8, rows), F32), shape((8, rows_down), F32),
        ]
        + [shape((8, span), F32)] * members,
        [pltpu.VMEM((8, span * members), F32)],
    )(group, *chunks, *g_in, *g_rest, *g_down, err, errd)

    chunks, merged = add_chunks(
        pieces, ((0, merge(merge_in_kernel, "merge_in", all_in, err, (rows, 3 * D))),)
    )
    merged_in = merged[0]

    same = lambda value: shape(value.shape, F32)
    replicas = lax.axis_size("rep")
    small = (vectors, vec_mom, final_norm, final_mom, embed, embed_mom, head_t, head_mom.T)
    given = (
        *chunks, shared, basis, own, ownd,
        mats_d[0], mats_down[0], mom_d[0], mom_down[0], merged_in, merged_rest, merged_down, counted, *small,
    )
    shapes = [
        shape((1, 1), F32), shape((1, 1), F32), shape((1, 1), F32), shape((8, wide), F32), shape((8, D), F32),
        same(mats_d[0]), same(mats_down[0]), same(mats_d[0]), same(mats_down[0]), same(err), same(errd),
    ] + [same(item) for item in small]
    outs = call(
        partial(finish_kernel, members, replicas), "finish", (1,),
        [whole(item.shape) for item in given], [whole(item.shape) for item in shapes], shapes,
        [pltpu.VMEM((8, span * members), F32)],
    )(group, *given)
    (loss, total, norm, new_q, new_qd, new_wide, new_down, new_mom_wide, new_mom_dn, new_err, new_errd,
     new_vec, new_vmom, new_fin, new_fmom, new_emb, new_emom, new_head, new_hmom) = outs
    return (
        loss.reshape(()),
        total.reshape(()),
        norm.reshape(()),
        new_wide[None],
        new_down[None],
        new_mom_wide[None],
        new_mom_dn[None],
        new_err[None, None],
        new_errd[None, None],
        own.T[None],
        ownd.T[None],
        new_q.T[None],
        new_qd.T[None],
        new_vec,
        new_vmom,
        new_fin,
        new_fmom,
        new_emb,
        new_emom,
        new_head.T,
        new_hmom.T,
    )


def solution(mesh):
    whole_seq = P(("rep", "grp"), None)
    by_rows = P(None, "grp", None)
    by_replica = P("rep", None, "grp", None)
    placed = (
        (whole_seq,) * 3 + (by_rows,) * 4 + (by_replica,) * 2 + (P(),) * 10
    )
    given = (P(),) * 3 + (by_rows,) * 4 + (by_replica,) * 2 + (by_rows,) * 2 + (P(),) * 10
    return jax.shard_map(shards, mesh=mesh, in_specs=placed, out_specs=given, check_vma=False)
```

```python
from functools import partial

import jax
import jax.numpy as jnp
import numpy as np
from jax import lax
from jax.experimental import pallas as pl
from jax.experimental.pallas import tpu as pltpu
from jax.sharding import PartitionSpec as P

D = 480
HEADS = 20
HDIM = 24
V = 33
PAD = 32
TOK = 40
WIDE = 512
EPS = 1e-05
BETA = 0.9
RATE_WIDE = 20000.0
RATE_LOWER = 3000.0
RATE_VECTOR = 20000.0
RATE_FINAL = 40000.0
RATE_EMBED = 60000.0
RATE_HEAD = 3000.0
CLIP = 0.005
F32 = jnp.float32
B16 = jnp.bfloat16
MIB = 2**20


ROOM = {
    "error_sketch": 16, "embed": 16, "project": 24, "attend": 30, "feed_and_loss": 56, "attend_back": 30,
    "input_grads": 30, "left_factors": 24, "merge_down": 12, "merge_rest": 16, "merge_in": 16, "finish": 30,
}


def params(name):
    return pltpu.CompilerParams(vmem_limit_bytes=ROOM[name] * MIB)


def nn(left, right):
    return jnp.dot(left, right, preferred_element_type=F32)


def nt(left, right):
    return lax.dot_general(left, right, (((1,), (1,)), ((), ())), preferred_element_type=F32)


def tn(left, right):
    return lax.dot_general(left, right, (((0,), (0,)), ((), ())), preferred_element_type=F32)


def thirds(value):
    top = value.astype(B16)
    rest = value - top.astype(F32)
    middle = rest.astype(B16)
    return top, middle, (rest - middle.astype(F32)).astype(B16)


def thirds_rows(value):
    return jnp.concatenate([part.astype(F32) for part in thirds(value)], 0).astype(B16)


def fold_rows(value):
    return value[0:8] + value[8:16] + value[16:24]


def exact_nt(left, right):
    return lax.dot_general(
        left, right, (((1,), (1,)), ((), ())),
        precision=lax.Precision.HIGHEST, preferred_element_type=F32,
    )


def exact_nn(left, right):
    return jnp.dot(left, right, precision=lax.Precision.HIGHEST, preferred_element_type=F32)


def three_nt(left, right):
    three = thirds_rows(left)
    top, middle, low = thirds(right)
    return fold_rows(nt(three, top) + nt(three, middle) + nt(three, low))


def three_nn(left, right):
    three = thirds_rows(left)
    top, middle, low = thirds(right)
    return fold_rows(nn(three, top) + nn(three, middle) + nn(three, low))


def norm_parts(value):
    center = value - jnp.mean(value, -1, keepdims=True)
    spread = jnp.mean(center * center, -1, keepdims=True)
    rstd = lax.rsqrt(spread + EPS)
    return center * rstd, rstd


def norm_back(grad, unit, rstd, gain):
    inner = grad * gain
    first = jnp.mean(inner, -1, keepdims=True)
    second = jnp.mean(inner * unit, -1, keepdims=True)
    return (
        rstd * (inner - first - unit * second),
        jnp.sum(grad * unit, 0, keepdims=True),
        jnp.sum(grad, 0, keepdims=True),
    )


def half_turn(value):
    return jnp.concatenate([value[HDIM // 2 :], value[: HDIM // 2]], 0)


def tail(rows, cols, ones):
    index = lax.broadcasted_iota(jnp.int32, (rows, cols), 0)
    return jnp.where(index < ones, 1.0, 0.0).astype(F32)


def lane_tail(rows, cols):
    index = lax.broadcasted_iota(jnp.int32, (rows, cols), 1)
    return jnp.where(index == 0, 1.0, 0.0).astype(F32)


def tables(length):
    half = HDIM // 2
    freq = np.float32(10000.0) ** (-np.arange(half, dtype=np.float32) * np.float32(2.0) / np.float32(HDIM))
    angle = np.arange(length, dtype=np.float32)[None, :] * freq.astype(np.float32)[:, None]
    cosine, sine = np.cos(angle), np.sin(angle)
    return (
        jnp.asarray(np.concatenate([cosine, cosine], 0), F32),
        jnp.asarray(np.concatenate([-sine, sine], 0), F32),
    )


def error_kernel(group, err_ref, errd_ref, q_ref, qd_ref, out_ref, row_ref):
    rows = err_ref.shape[0]
    out_ref[...] = jnp.zeros_like(out_ref)
    row_ref[...] = jnp.zeros_like(row_ref)
    row_ref[:, 0:rows] = three_nt(q_ref[...], err_ref[...])
    out_ref[0:8, :] = pltpu.roll(row_ref[...], rows * group[0], 1)
    start = pl.multiple_of(8 + 8 * group[0], 8)
    out_ref[pl.ds(start, 8), 0:D] = three_nt(qd_ref[...], errd_ref[...])


def embed_kernel(tok_ref, emb_ref, vec_ref, x_ref, h_ref, ht_ref, emb_s):
    step = tok_ref.shape[1]

    @pl.when(pl.program_id(0) == 0)
    def _():
        emb_s[...] = jnp.zeros_like(emb_s)
        emb_s[0:V, :] = emb_ref[...]

    index = lax.broadcasted_iota(jnp.int32, (TOK, step), 0)
    hot = jnp.where(index == tok_ref[...], 1.0, 0.0).astype(F32)
    hot = jnp.concatenate([hot, hot, hot], 0).astype(B16)
    x = tn(hot, thirds_rows(emb_s[...]))
    x_ref[...] = x
    unit, _ = norm_parts(x)
    normed = unit * vec_ref[:, 0:D] + vec_ref[:, D : 2 * D]
    h_ref[...] = normed.astype(B16)
    ht_ref[...] = jnp.concatenate([normed.T, tail(16, step, 1)], 0).astype(B16)


def spot(group, place, size, unit):
    return pl.ds(pl.multiple_of((group[0] ^ place) * size, unit), size)


def assemble(group, chunks, wide_s, out_s):
    for place, ref in enumerate(chunks):
        wide_s[spot(group, place, ref.shape[0], 8), :] = ref[...].astype(F32)
    out_s[...] = wide_s[...].astype(B16)


def project_kernel(members, group, h_ref, *refs):
    chunks = refs[:members]
    vec_ref, cos_ref, sin_ref, q_ref, k_ref, v_ref, wide_s, w_s = refs[members:]
    step = h_ref.shape[0]

    @pl.when(pl.program_id(0) == 0)
    def _():
        assemble(group, chunks, wide_s, w_s)

    act = nn(h_ref[...], w_s[...]) + vec_ref[:, 2 * D : 5 * D]
    turned = act.T
    cosine, sine = cos_ref[...], sin_ref[...]
    zeros = tail(PAD - HDIM, step, 0)
    ones = tail(PAD - HDIM, step, 3)
    for head in range(HEADS):
        low = HDIM * head
        query = turned[low : low + HDIM]
        query = (query * cosine + half_turn(query) * sine) * HDIM ** (-0.5)
        q_ref[head] = jnp.concatenate([query, zeros], 0).astype(B16)
        keys = turned[D + low : D + low + HDIM]
        keys = keys * cosine + half_turn(keys) * sine
        k_ref[head] = jnp.concatenate([keys, ones], 0).astype(B16)
        value = turned[2 * D + low : 2 * D + low + HDIM]
        v_ref[head] = jnp.concatenate([value, ones], 0).astype(B16)


def rows_of(value):
    return value.astype(F32).T.astype(B16)


def attend_kernel(q_ref, k_ref, v_ref, *refs):
    mix_ref, inv_ref, p_ref = refs[-3:]
    count, _, length = q_ref.shape
    zeros = tail(PAD - HDIM - 3, length, 0)

    def first(head):
        keys = rows_of(k_ref[head])
        query = q_ref[head]
        top = jnp.max(nn(keys, query), 0, keepdims=True)
        parts = [part.astype(F32) for part in thirds(-top)]
        return keys, jnp.concatenate([query[0:HDIM].astype(F32)] + parts + [zeros], 0).astype(B16)

    def second(head, keys, query):
        probs = jnp.exp(nn(keys, query)).astype(B16)
        p_ref[head] = probs
        out = nn(v_ref[head], probs)
        inverse = 1.0 / out[HDIM : HDIM + 1]
        mix_ref[HDIM * head : HDIM * head + HDIM, :] = out[0:HDIM] * inverse
        inv_ref[head] = inverse

    held = first(0)
    for head in range(count):
        ahead = first(head + 1) if head + 1 < count else None
        second(head, *held)
        held = ahead


def gelu_parts(upper):
    size = jnp.abs(upper) * (0.5**0.5)
    bell = jnp.exp(-0.5 * upper * upper)
    t = 1.0 / (1.0 + 0.3275911 * size)
    poly = t * (0.254829592 + t * (-0.284496736 + t * (1.421413741 + t * (-1.453152027 + t * 1.061405429))))
    lower = 0.5 * poly * bell
    cdf = jnp.where(upper < 0, lower, 1.0 - lower)
    return upper * cdf, cdf + upper * (0.3989422804014327 * bell)


def middle_kernel(members, group, mixa_ref, mixb_ref, inva_ref, invb_ref, x_ref, mask_ref, tgt_ref,
                  count_ref, vec_ref, fin_ref, head_ref, q_ref, qd_ref, *refs):
    chunks, chunks_down, refs = refs[:members], refs[members : 2 * members], refs[2 * members :]
    dm_ref, dx_ref, s_ref, e_ref, *refs = refs
    outs, outs_down, refs = refs[:members], refs[members : 2 * members], refs[2 * members :]
    acc_o, acc_u, acc_d, head_s, hid_s, slope_s, wide_s, wr_ref, wd_ref = refs
    pid = pl.program_id(0)
    step = x_ref.shape[0]
    wide = wd_ref.shape[0]
    wo = slice(wide, wide + D)

    @pl.when(pid == 0)
    def _():
        acc_o[...] = jnp.zeros_like(acc_o)
        acc_u[...] = jnp.zeros_like(acc_u)
        acc_d[...] = jnp.zeros_like(acc_d)
        e_ref[...] = jnp.zeros_like(e_ref)
        s_ref[...] = jnp.zeros_like(s_ref)
        head_s[...] = jnp.zeros_like(head_s)
        head_s[0:V, 0 : D + 1] = head_ref[...]
        assemble(group, chunks, wide_s, wr_ref)
        for place, ref in enumerate(chunks_down):
            wd_ref[spot(group, place, ref.shape[0], 16), :] = ref[...]

    mix = jnp.concatenate([mixa_ref[...], mixb_ref[...]], 0)
    half = inva_ref.shape[0]
    mixed = jnp.concatenate([mix, tail(16, step, 1)], 0).astype(B16)
    middle = x_ref[...] + tn(mixed[0:D], wr_ref[:, wo]) + vec_ref[:, 5 * D : 6 * D]
    unit2, rstd2 = norm_parts(middle)
    gain2 = vec_ref[:, 6 * D : 7 * D]
    normed2 = unit2 * gain2 + vec_ref[:, 7 * D : 8 * D]
    normed2 = jnp.concatenate([normed2, lane_tail(step, WIDE - D)], 1).astype(B16)
    bias_up = vec_ref[:, 9 * D :]
    block = 384
    for low in range(0, wide, block):
        cut = slice(low, low + block)
        upper = nn(normed2[:, 0:D], wr_ref[:, cut]) + bias_up[:, cut]
        hidden, slope = gelu_parts(upper)
        hid_s[:, cut] = hidden.astype(B16)
        slope_s[:, cut] = slope
    resid = middle + nn(hid_s[...], wd_ref[...]) + vec_ref[:, 8 * D : 9 * D]
    unit3, rstd3 = norm_parts(resid)
    final = unit3 * fin_ref[0:1, :] + fin_ref[1:2, :]
    final = jnp.concatenate([final, lane_tail(step, WIDE - D)], 1).astype(B16)

    lanes = lax.broadcasted_iota(jnp.int32, (TOK, WIDE), 1)
    bias = jnp.sum(jnp.where(lanes == D, head_s[...], 0.0), 1, keepdims=True)
    table = head_s[:, 0:D].astype(B16)
    rows = lax.broadcasted_iota(jnp.int32, (TOK, step), 0)
    logits = jnp.where(rows < V, nt(table, final[:, 0:D]) + bias, -1e30)
    shifted = logits - jnp.max(logits, 0, keepdims=True)
    expo = jnp.exp(shifted)
    total = jnp.sum(expo, 0, keepdims=True)
    picks = rows == tgt_ref[...]
    weight = mask_ref[...].astype(F32)
    picked = jnp.sum(jnp.where(picks, shifted, 0.0), 0, keepdims=True)
    loss = jnp.sum((jnp.log(total) - picked) * weight, 1, keepdims=True)
    grad_logits = (expo / total - jnp.where(picks, 1.0, 0.0)) * (weight * (1.0 / count_ref[0:1, 0:1]))
    grad_logits = grad_logits.astype(B16)
    e_ref[16 : 16 + TOK, :] += nn(grad_logits, final)
    grad_resid, grad_fg, grad_fb = norm_back(tn(grad_logits, table), unit3, rstd3, fin_ref[0:1, :])

    grad_y = grad_resid.astype(B16)
    acc_d[...] += tn(hid_s[...], grad_y)
    for low in range(0, wide, block):
        cut = slice(low, low + block)
        grad_hidden = nt(grad_y, wd_ref[cut, :])
        hid_s[:, cut] = (grad_hidden * slope_s[:, cut]).astype(B16)
    acc_u[...] += tn(normed2, hid_s[...])
    grad_mid, grad_g2, grad_b2 = norm_back(nt(hid_s[...], wr_ref[:, 0:wide]), unit2, rstd2, gain2)
    grad_mid = grad_mid + grad_resid
    dx_ref[...] = grad_mid
    branch = grad_mid.astype(B16)
    acc_o[...] += nn(mixed, branch)
    grad_mixed = nt(wr_ref[:, wo], branch).astype(B16).astype(F32)
    zeros = tail(PAD - HDIM - 3, step, 0)
    for head in range(HEADS):
        cut = slice(HDIM * head, HDIM * head + HDIM)
        inverse = inva_ref[head] if head < half else invb_ref[head - half]
        scaled = (grad_mixed[cut] * inverse).astype(B16).astype(F32)
        delta = -jnp.sum(scaled * mix[cut], 0, keepdims=True)
        top, mid, low = thirds(delta)
        dm_ref[head] = jnp.concatenate(
            [scaled, top.astype(F32), mid.astype(F32), low.astype(F32), zeros], 0
        ).astype(B16)
    e_ref[1:2, 0:D] += grad_g2
    e_ref[2:3, 0:D] += grad_b2
    e_ref[3:4, 0:D] += jnp.sum(grad_y.astype(F32), 0, keepdims=True)
    e_ref[8:9, 0:D] += grad_fg
    e_ref[9:10, 0:D] += grad_fb
    e_ref[10:11, :] += jnp.broadcast_to(loss, (1, WIDE))

    @pl.when(pid == pl.num_programs(0) - 1)
    def _():
        e_ref[0:1, 0:D] = acc_o[D : D + 1, :]
        for part in range(wide // D):
            e_ref[4 + part : 5 + part, 0:D] = acc_u[D : D + 1, D * part : D * part + D]
        go = acc_o[0:D, :].astype(B16)
        gu = acc_u[0:D, :].astype(B16)
        sketch = nt(thirds_rows(q_ref[:, 3 * D : 4 * D]), go) + nt(thirds_rows(q_ref[:, 4 * D :]), gu)
        s_ref[0:8, 0:D] = fold_rows(sketch)
        start = thirds_rows(qd_ref[...])
        for part in range(wide // D):
            piece = nt(start, acc_d[D * part : D * part + D, :].astype(B16))
            s_ref[8 + 8 * part : 16 + 8 * part, 0:D] = fold_rows(piece)
        for place, ref in enumerate(outs):
            at = spot(group, place, ref.shape[0], 8)
            ref[:, 0:wide] = acc_u[at, :].astype(B16)
            ref[:, wo] = acc_o[at, :].astype(B16)
        for place, ref in enumerate(outs_down):
            ref[...] = acc_d[spot(group, place, ref.shape[0], 8), :].astype(B16)


def attend_back_kernel(p_ref, q_ref, k_ref, v_ref, dm_ref, cos_ref, sin_ref, da_ref):
    cosine, sine = cos_ref[...], sin_ref[...]
    parts = [[], [], []]
    for head in range(p_ref.shape[0]):
        probs = p_ref[head]
        grad = dm_ref[head]
        slope = nn(rows_of(v_ref[head]), grad)
        grad_scores = (probs.astype(F32) * slope).astype(B16)
        grad_value = nt(grad, probs)[0:HDIM]
        grad_keys = nt(q_ref[head], grad_scores)[0:HDIM]
        grad_query = nn(k_ref[head], grad_scores)[0:HDIM] * HDIM ** (-0.5)
        parts[0].append(grad_query * cosine + half_turn(grad_query * sine))
        parts[1].append(grad_keys * cosine + half_turn(grad_keys * sine))
        parts[2].append(grad_value)
    for index in range(3):
        da_ref[index] = jnp.concatenate(parts[index], 0).astype(B16)


def input_kernel(members, group, tok_ref, da_ref, h_ref, x_ref, dx_ref, vec_ref, q_ref,
                 s_ref, serr_ref, e_ref, *refs):
    chunks, refs = refs[:members], refs[members:]
    outs, pieces, refs = refs[:members], refs[members : 2 * members], refs[2 * members :]
    out_ref, acc_w, acc_e, wide_s, w_s = refs
    pid = pl.program_id(0)
    step = x_ref.shape[0]

    @pl.when(pid == 0)
    def _():
        acc_w[...] = jnp.zeros_like(acc_w)
        acc_e[...] = jnp.zeros_like(acc_e)
        out_ref[...] = jnp.zeros_like(out_ref)
        assemble(group, chunks, wide_s, w_s)

    da = da_ref[...].reshape(3 * D, step)
    acc_w[...] += nt(h_ref[...], da)
    grad = nn(w_s[...], da).T
    unit, rstd = norm_parts(x_ref[...])
    grad_x, grad_g, grad_b = norm_back(grad, unit, rstd, vec_ref[:, 0:D])
    grad_x = grad_x + dx_ref[...]
    index = lax.broadcasted_iota(jnp.int32, (TOK, step), 0)
    hot = jnp.where(index == tok_ref[...], 1.0, 0.0).astype(B16)
    for part in thirds(grad_x):
        acc_e[...] += nn(hot, part)
    out_ref[40:41, 0:D] += grad_g
    out_ref[41:42, 0:D] += grad_b

    @pl.when(pid == pl.num_programs(0) - 1)
    def _():
        for part in range(3):
            out_ref[42 + part : 43 + part, 0:D] = acc_w[D : D + 1, D * part : D * part + D]
        out_ref[0:40, :] = s_ref[...] + serr_ref[...]
        out_ref[0:8, 0:D] += fold_rows(nt(thirds_rows(q_ref[:, 0 : 3 * D]), acc_w[0:D, :].astype(B16)))
        out_ref[45:48, :] = e_ref[8:11, :]
        out_ref[48:56, :] = e_ref[0:8, :]
        out_ref[56 : 56 + V, 0:D] = acc_e[0:V, :]
        out_ref[56 + V : 56 + 2 * V, :] = e_ref[16 : 16 + V, :]
        for place, ref in enumerate(outs):
            ref[...] = acc_w[spot(group, place, ref.shape[0], 8), :].astype(B16)
        for place, ref in enumerate(pieces):
            ref[...] = out_ref[spot(group, place, ref.shape[0], 8), :]


def orthonormal(sketch, gram):
    basis = jnp.zeros_like(sketch[0])
    count = gram.shape[0]
    index = lax.broadcasted_iota(jnp.int32, (count, 1), 0)
    out = [jnp.zeros_like(part) for part in sketch]
    left = list(sketch)
    for step in range(count):
        pivot = gram[step : step + 1, step : step + 1]
        scale = 1.0 / jnp.sqrt(pivot)
        column = gram[:, step : step + 1] * scale
        row = gram[step : step + 1, :] * scale
        column = jnp.where(index > step, column, 0.0)
        gram = gram - column * row
        for place in range(len(left)):
            base = left[place][step : step + 1, :] * scale
            out[place] = jnp.where(index == step, base, out[place])
            left[place] = left[place] - column * base
    return out


def factor_kernel(members, group, *refs):
    chunks, ins, rests, downs = (refs[members * part : members * part + members] for part in range(4))
    err_ref, errd_ref, a_ref, p_ref, own_ref, ownd_ref, *refs = refs[4 * members :]
    outs, f_s = refs[:members], refs[members]
    rows, wide_cols = err_ref.shape
    hidden = wide_cols - 4 * D
    parts = hidden // D
    for place, ref in enumerate(chunks):
        a_ref[spot(group, place, ref.shape[0], 8), :] = ref[...]
    wide = a_ref[0:8, 0:D]
    down = [a_ref[8 + 8 * part : 16 + 8 * part, 0:D] for part in range(parts)]
    gram = exact_nt(wide, wide)
    (wide,) = orthonormal([wide], gram)
    gram = exact_nt(down[0], down[0])
    for part in range(1, parts):
        gram = gram + exact_nt(down[part], down[part])
    down = orthonormal(down, gram)
    p_ref[...] = jnp.zeros_like(p_ref)
    p_ref[0:8, 0:D] = wide
    for part in range(parts):
        p_ref[8 + 8 * part : 16 + 8 * part, 0:D] = down[part]
    f_s[...] = jnp.zeros_like(f_s)
    for place in range(members):
        piece = pltpu.roll(p_ref[0:8, :], (WIDE - rows * (group[0] ^ place)) % WIDE, 1)[:, 0:rows]
        piece_down = p_ref[pl.ds(pl.multiple_of(8 + 8 * (group[0] ^ place), 8), 8), :][:, 0:D]
        if place == 0:
            own_ref[...] = piece
            ownd_ref[...] = piece_down
            f_s[:, 0:wide_cols] = three_nn(piece, err_ref[...])
            f_s[:, wide_cols : wide_cols + D] = three_nn(piece_down, errd_ref[...])
        three = thirds_rows(piece)
        f_s[:, 0 : 3 * D] += fold_rows(nn(three, ins[place][...]))
        f_s[:, 4 * D : wide_cols] += fold_rows(nn(three, rests[place][:, 0:hidden]))
        f_s[:, 3 * D : 4 * D] += fold_rows(nn(three, rests[place][:, hidden:]))
        f_s[:, wide_cols : wide_cols + D] += fold_rows(nn(thirds_rows(piece_down), downs[place][...]))
    for place, ref in enumerate(outs):
        ref[...] = f_s[:, spot(group, place, ref.shape[1], 128)]


def merge_kernel(*refs):
    *chunks, err_ref, out_ref = refs
    value = err_ref[...]
    for ref in chunks:
        value = value + ref[...].astype(F32)
    out_ref[...] = value


def merge_rest_kernel(*refs):
    *chunks, err_ref, out_ref = refs
    value = chunks[0][...].astype(F32)
    for ref in chunks[1:]:
        value = value + ref[...].astype(F32)
    hidden = value.shape[1] - D
    out_ref[:, 0:hidden] = value[:, 0:hidden] + err_ref[:, 4 * D :]
    out_ref[:, hidden:] = value[:, hidden:] + err_ref[:, 3 * D : 4 * D]


def merge_in_kernel(*refs):
    *chunks, err_ref, out_ref = refs
    value = err_ref[:, 0 : 3 * D]
    for ref in chunks:
        value = value + ref[...].astype(F32)
    out_ref[...] = value


def six(left, right):
    first, second = thirds(left), thirds(right)
    order = ((0, 0), (0, 1), (1, 0), (1, 1), (0, 2), (2, 0))
    left = jnp.concatenate([first[i].astype(F32) for i, _ in order], 0).astype(B16)
    right = jnp.concatenate([second[j].astype(F32) for _, j in order], 0).astype(B16)
    return tn(left, right)


def renew(weight, moment, grad, scale, rate):
    new_moment = BETA * moment + scale * grad
    return weight - rate * new_moment, new_moment


def finish_kernel(members, replicas, group, *refs):
    chunks, rest = refs[:members], refs[members:]
    (a_ref, p_ref, own_ref, ownd_ref,
     w_ref, wd_ref, m_ref, md_ref, ein_ref, erest_ref, errd_ref, count_ref,
     vec_ref, vmom_ref, fin_ref, fmom_ref, emb_ref, emom_ref, head_ref, hmom_ref,
     loss_ref, total_ref, norm_ref, nq_ref, nqd_ref, nw_ref, nwd_ref, nm_ref, nmd_ref, ne_ref, ned_ref,
     nvec_ref, nvmom_ref, nfin_ref, nfmom_ref, nemb_ref, nemom_ref, nhead_ref, nhmom_ref, f_s) = rest
    wide_cols = w_ref.shape[1]
    hidden = wide_cols - 4 * D
    for place, ref in enumerate(chunks):
        f_s[:, spot(group, place, ref.shape[1], 128)] = ref[...]
    factor, factor_down = f_s[:, 0:wide_cols], f_s[:, wide_cols : wide_cols + D]
    nq_ref[...] = factor
    nqd_ref[...] = factor_down
    a = a_ref[...]
    square = jnp.sum(a[40:47, 0:D] * a[40:47, 0:D]) + jnp.sum(a[48:56, 0:D] * a[48:56, 0:D])
    emb, top = a[56 : 56 + V, 0:D], a[56 + V : 56 + 2 * V, 0 : D + 1]
    square = square + jnp.sum(emb * emb) + jnp.sum(top * top)
    basis = p_ref[...]
    gram = exact_nt(basis[0:8, 0:D], basis[0:8, 0:D])
    square = square + jnp.sum(gram * exact_nt(factor, factor))
    gram = jnp.zeros((8, 8), F32)
    for part in range(1, basis.shape[0] // 8):
        piece = basis[8 * part : 8 * part + 8, 0:D]
        gram = gram + exact_nt(piece, piece)
    square = square + jnp.sum(gram * exact_nt(factor_down, factor_down))
    norm = jnp.sqrt(square)
    norm_ref[...] = jnp.broadcast_to(norm, norm_ref.shape)
    loss_ref[...] = a[47:48, 0:1]
    total_ref[...] = count_ref[0:1, 0:1]
    scale = jnp.minimum(1.0, CLIP / norm)

    approx = six(own_ref[...], factor)
    nw_ref[...], nm_ref[...] = renew(w_ref[...], m_ref[...], approx, scale, RATE_WIDE)
    share = approx * (1.0 / replicas)
    ne_ref[:, 0 : 3 * D] = ein_ref[...] - share[:, 0 : 3 * D]
    ne_ref[:, 3 * D : 4 * D] = erest_ref[:, hidden:] - share[:, 3 * D : 4 * D]
    ne_ref[:, 4 * D :] = erest_ref[:, 0:hidden] - share[:, 4 * D :]
    approx = six(ownd_ref[...], factor_down)
    nwd_ref[...], nmd_ref[...] = renew(wd_ref[...], md_ref[...], approx, scale, RATE_LOWER)
    ned_ref[...] = errd_ref[...] - approx * (1.0 / replicas)

    places = (40, 41, 42, 43, 44, 48, 49, 50, 51, 52, 53, 54, 55)
    for row, place in enumerate(places):
        cut = slice(D * row, D * row + D)
        nvec_ref[:, cut], nvmom_ref[:, cut] = renew(
            vec_ref[:, cut], vmom_ref[:, cut], a[place : place + 1, 0:D], scale, RATE_VECTOR
        )
    nfin_ref[...], nfmom_ref[...] = renew(fin_ref[...], fmom_ref[...], a[45:47, 0:D], scale, RATE_FINAL)
    nemb_ref[...], nemom_ref[...] = renew(emb_ref[...], emom_ref[...], emb, scale, RATE_EMBED)
    nhead_ref[...], nhmom_ref[...] = renew(head_ref[...], hmom_ref[...], top, scale, RATE_HEAD)


def swap(value, axis, bit):
    size = lax.axis_size(axis)
    return lax.ppermute(value, axis, [(i, i ^ bit) for i in range(size)])


def bits_of(axis):
    size, bit, out = lax.axis_size(axis), 1, []
    while bit < size:
        out.append(bit)
        bit *= 2
    return out


def tie(*values):
    return lax.optimization_barrier(values)


def send_chunks(pieces):
    return [pieces[0]] + [swap(piece, "grp", place) for place, piece in enumerate(pieces) if place]


def add_chunks(pieces, work=()):
    work, results = dict(work), {}

    def beside(turn, moved):
        if turn in work:
            moved, results[turn] = tie(moved, work[turn]())
        return moved

    got = beside(0, send_chunks(pieces))
    total = got[0]
    for piece in got[1:]:
        total = total + piece
    first, *bits = bits_of("rep")
    for turn, pair in enumerate([[first]] + [bits[at : at + 2] for at in range(0, len(bits), 2)]):
        moves = pair + [sum(pair)] * (len(pair) - 1)
        for piece in beside(turn + 1, [swap(total, "rep", move) for move in moves]):
            total = total + piece
    got = [total] + [swap(total, "grp", place) for place in range(1, len(pieces))]
    return beside(-1, got), results


def gather_start(value):
    first, *bits = reversed(bits_of("grp"))
    return [value, swap(value, "grp", first)]


def gather_end(pieces):
    first, *bits = reversed(bits_of("grp"))
    order = [0, first]
    for bit in bits:
        pieces = pieces + [swap(piece, "grp", bit) for piece in pieces]
        order = order + [place ^ bit for place in order]
    return [pieces[order.index(place)] for place in range(len(order))]


def halve_start(pieces):
    first, *bits = bits_of("grp")
    keep = [place for place in range(len(pieces)) if not place & first]
    return [(place, pieces[place], swap(pieces[place | first], "grp", first)) for place in keep]


def halve_end(pairs):
    first, *bits = bits_of("grp")
    (_, own, other), *others = pairs
    kept = [own, other]
    sums = {place: (mine.astype(F32) + theirs.astype(F32)).astype(B16) for place, mine, theirs in others}
    for bit in bits:
        kept.append(swap(sums[bit], "grp", bit))
        sums = {
            place: (sums[place].astype(F32) + swap(sums[place | bit], "grp", bit).astype(F32)).astype(B16)
            for place in sums
            if not place & bit
        }
    return kept


def whole(shape):
    return pl.BlockSpec(shape, lambda *_: (0,) * len(shape))


def shards(tokens, mask, targets, mats_d, mats_down, mom_d, mom_down, err_d, err_down, q_d, q_down,
           vectors, vec_mom, final_norm, final_mom, embed, embed_mom, head, head_mom):
    length = tokens.shape[1]
    wide = mats_d.shape[2]
    hidden = wide - 4 * D
    rows = mats_d.shape[1]
    rows_down = mats_down.shape[1]
    step = 256
    steps = length // step
    step_mid = 2 * step
    index = lax.axis_index("grp").astype(jnp.int32)
    group = index.reshape(1)
    members = lax.axis_size("grp")
    cosine, sine = tables(length)
    q_t, qd_t = q_d[0].T, q_down[0].T
    head_t = head.T
    err, errd = err_d[0, 0], err_down[0, 0]

    def call(kernel, name, grid, ins, outs, shapes, scratch=()):
        return pl.pallas_call(
            kernel,
            grid_spec=pltpu.PrefetchScalarGridSpec(
                num_scalar_prefetch=1, grid=grid, in_specs=ins, out_specs=outs, scratch_shapes=scratch
            ),
            out_shape=shapes,
            compiler_params=params(name),
            name=name,
        )

    shape = jax.ShapeDtypeStruct
    rounds = [("grp", bit) for bit in bits_of("grp")] + [("rep", bit) for bit in bits_of("rep")]

    def advance(value, times=1):
        for _ in range(min(times, len(rounds))):
            value = value + swap(value, *rounds.pop(0))
        return value

    cols = pl.BlockSpec((1, step), lambda i, *_: (0, i))
    flat = pl.BlockSpec((step, D), lambda i, *_: (i, 0))
    heads = pl.BlockSpec((HEADS, PAD, step), lambda i, *_: (0, 0, i))
    wave = pl.BlockSpec((HDIM, step), lambda i, *_: (0, i))
    ext = pl.BlockSpec((D + 16, step), lambda i, *_: (0, i))

    w_in = gather_start(mats_d[0][:, : 3 * D].astype(B16))
    counted = jnp.broadcast_to(jnp.sum(mask.astype(F32)), (8, 128))
    more = advance(counted)
    err_sketch = call(
        error_kernel, "error_sketch", (1,),
        [whole((rows, wide)), whole((rows_down, D)), whole((8, wide)), whole((8, D))],
        whole((40, WIDE)), shape((40, WIDE), F32), [pltpu.VMEM((8, WIDE), F32)],
    )(group, err, errd, q_t, qd_t)
    x, h, h_t = pl.pallas_call(
        embed_kernel,
        grid=(steps,),
        in_specs=[cols, whole((V, D)), whole(vectors.shape)],
        out_specs=[flat, flat, ext],
        out_shape=[shape((length, D), F32), shape((length, D), B16), shape((D + 16, length), B16)],
        scratch_shapes=[pltpu.VMEM((TOK, D), F32)],
        compiler_params=params("embed"),
        name="embed",
    )(tokens, embed, vectors)
    w_in, err_sketch, h, counted = tie(w_in, err_sketch, h, more)
    w_in = gather_end(w_in)
    rest = jnp.concatenate([mats_d[0][:, 4 * D :], mats_d[0][:, 3 * D : 4 * D]], 1).astype(B16)
    down = mats_down[0].astype(B16)
    more = advance(counted)
    w_in, counted, rest, down = tie(w_in, more, rest, down)
    w_rest, w_down = gather_start(rest), gather_start(down)
    more = advance(counted)
    query, keys, value = call(
        partial(project_kernel, members), "project", (steps,),
        [flat] + [whole((rows, 3 * D))] * members + [whole(vectors.shape), wave, wave],
        [heads] * 3, [shape((HEADS, PAD, length), B16)] * 3,
        [pltpu.VMEM((D, 3 * D), F32), pltpu.VMEM((D, 3 * D), B16)],
    )(group, h, *w_in, vectors, cosine, sine)
    query, counted = tie(query, more)

    half = HEADS // 2
    pair = 2
    turned = half // pair
    mixes, inverses, probs = [], [], []
    for part in range(2):
        one = pl.BlockSpec((1, PAD, length), lambda i, part=part: (i + half * part, 0, 0))
        more = advance(counted, 1 + part * len(rounds))
        mix, inverse, *probs = pl.pallas_call(
            attend_kernel,
            grid=(half,),
            in_specs=[one, one, one] + [pl.BlockSpec(memory_space=pl.ANY)] * len(probs),
            out_specs=[
                pl.BlockSpec((HDIM, length), lambda i: (i, 0)),
                pl.BlockSpec((1, 1, length), lambda i: (i, 0, 0)),
                pl.BlockSpec((1, length, length), lambda i, part=part: (i + half * part, 0, 0)),
            ],
            out_shape=[
                shape((half * HDIM, length), F32),
                shape((half, 1, length), F32),
                shape((HEADS, length, length), B16),
            ],
            input_output_aliases={3: 2} if probs else {},
            compiler_params=params("attend"),
            name="attend",
        )(query, keys, value, *probs)
        mix, query, counted, w_rest, w_down = tie(mix, query, more, w_rest, w_down)
        if part == 0:
            w_rest, w_down = gather_end(w_rest), gather_end(w_down)
        mixes.append(mix)
        inverses.append(inverse)

    cols2 = pl.BlockSpec((1, step_mid), lambda i, *_: (0, i))
    flat2 = pl.BlockSpec((step_mid, D), lambda i, *_: (i, 0))
    heads2 = pl.BlockSpec((HEADS, PAD, step_mid), lambda i, *_: (0, 0, i))
    everyone = [(rows, D + hidden)] * members + [(rows_down, D)] * members
    grad_mix, grad_mid, sketch, early, *grads = call(
        partial(middle_kernel, members), "feed_and_loss", (length // step_mid,),
        [pl.BlockSpec((half * HDIM, step_mid), lambda i, *_: (0, i))] * 2
        + [pl.BlockSpec((half, 1, step_mid), lambda i, *_: (0, 0, i))] * 2
        + [
            flat2, cols2, cols2, whole((8, 128)), whole(vectors.shape), whole((2, D)),
            whole((V, D + 1)), whole((8, wide)), whole((8, D)),
        ]
        + [whole(item) for item in everyone],
        [heads2, flat2, whole((40, WIDE)), whole((56, WIDE))] + [whole(item) for item in everyone],
        [
            shape((HEADS, PAD, length), B16),
            shape((length, D), F32),
            shape((40, WIDE), F32),
            shape((56, WIDE), F32),
        ]
        + [shape(item, B16) for item in everyone],
        [
            pltpu.VMEM((D + 16, D), F32),
            pltpu.VMEM((WIDE, hidden), F32),
            pltpu.VMEM((hidden, D), F32),
            pltpu.VMEM((TOK, WIDE), F32),
            pltpu.VMEM((step_mid, hidden), B16),
            pltpu.VMEM((step_mid, hidden), F32),
            pltpu.VMEM((D, D + hidden), F32),
            pltpu.VMEM((D, D + hidden), B16),
            pltpu.VMEM((hidden, D), B16),
        ],
    )(group, *mixes, *inverses, x, mask, targets, counted, vectors, final_norm, head_t, q_t, qd_t,
      *w_rest, *w_down)
    g_rest, g_down = grads[:members], grads[members:]
    all_down = send_chunks(g_down)
    all_rest = send_chunks(g_rest)

    two = pl.BlockSpec((pair, PAD, length), lambda i: (i, 0, 0))
    grad_act = pl.pallas_call(
        attend_back_kernel,
        grid=(HEADS // pair,),
        in_specs=[
            pl.BlockSpec((pair, length, length), lambda i: (i, 0, 0)),
            two, two, two, two, whole((HDIM, length)), whole((HDIM, length)),
        ],
        out_specs=pl.BlockSpec((3, pair * HDIM, length), lambda i: (0, i, 0)),
        out_shape=shape((3, D, length), B16),
        compiler_params=params("attend_back"),
        name="attend_back",
    )(*probs, query, keys, value, grad_mix, cosine, sine)
    all_down, all_rest, grad_act = tie(all_down, all_rest, grad_act)

    act = pl.BlockSpec((3, D, step), lambda i, *_: (0, 0, i))
    size = 128 // members
    ins = [(rows, 3 * D)] * members
    grads = call(
        partial(input_kernel, members), "input_grads", (steps,),
        [
            cols, act, ext, flat, flat,
            whole(vectors.shape), whole((8, wide)), whole((40, WIDE)), whole((40, WIDE)), whole((56, WIDE)),
        ]
        + [whole(item) for item in ins],
        [whole(item) for item in ins] + [whole((size, WIDE))] * members,
        [shape(item, B16) for item in ins] + [shape((size, WIDE), F32)] * members,
        [
            pltpu.VMEM((128, WIDE), F32), pltpu.VMEM((D + 16, 3 * D), F32), pltpu.VMEM((TOK, D), F32),
            pltpu.VMEM((D, 3 * D), F32), pltpu.VMEM((D, 3 * D), B16),
        ],
    )(group, tokens, grad_act, h_t, x, grad_mid, vectors, q_t, sketch, err_sketch, early, *w_in)
    g_in, pieces = grads[:members], grads[members:]
    half_in = halve_start(g_in)

    def merge(kernel, name, chunks, err, result):
        return lambda: pl.pallas_call(
            kernel, out_shape=shape(result, F32), compiler_params=params(name), name=name
        )(*chunks, err)

    chunks, merged = add_chunks(
        pieces,
        (
            (0, merge(merge_kernel, "merge_down", all_down, errd, errd.shape)),
            (1, lambda: halve_end(half_in)),
            (2, merge(merge_rest_kernel, "merge_rest", all_rest, err, (rows, D + hidden))),
        ),
    )
    merged_down, all_in, merged_rest = (merged[turn] for turn in range(3))
    span = -(-(wide + WIDE) // (128 * members)) * 128
    shared, basis, own, ownd, *pieces = call(
        partial(factor_kernel, members), "left_factors", (1,),
        [whole((size, WIDE))] * members + [whole(item) for item in ins + everyone]
        + [whole((rows, wide)), whole((rows_down, D))],
        [whole((128, WIDE)), whole((40, WIDE)), whole((8, rows)), whole((8, rows_down))]
        + [whole((8, span))] * members,
        [
            shape((128, WIDE), F32), shape((40, WIDE), F32), shape((8, rows), F32), shape((8, rows_down), F32),
        ]
        + [shape((8, span), F32)] * members,
        [pltpu.VMEM((8, span * members), F32)],
    )(group, *chunks, *g_in, *g_rest, *g_down, err, errd)

    chunks, merged = add_chunks(
        pieces, ((0, merge(merge_in_kernel, "merge_in", all_in, err, (rows, 3 * D))),)
    )
    merged_in = merged[0]

    same = lambda value: shape(value.shape, F32)
    replicas = lax.axis_size("rep")
    small = (vectors, vec_mom, final_norm, final_mom, embed, embed_mom, head_t, head_mom.T)
    given = (
        *chunks, shared, basis, own, ownd,
        mats_d[0], mats_down[0], mom_d[0], mom_down[0], merged_in, merged_rest, merged_down, counted, *small,
    )
    shapes = [
        shape((1, 1), F32), shape((1, 1), F32), shape((1, 1), F32), shape((8, wide), F32), shape((8, D), F32),
        same(mats_d[0]), same(mats_down[0]), same(mats_d[0]), same(mats_down[0]), same(err), same(errd),
    ] + [same(item) for item in small]
    outs = call(
        partial(finish_kernel, members, replicas), "finish", (1,),
        [whole(item.shape) for item in given], [whole(item.shape) for item in shapes], shapes,
        [pltpu.VMEM((8, span * members), F32)],
    )(group, *given)
    (loss, total, norm, new_q, new_qd, new_wide, new_down, new_mom_wide, new_mom_dn, new_err, new_errd,
     new_vec, new_vmom, new_fin, new_fmom, new_emb, new_emom, new_head, new_hmom) = outs
    return (
        loss.reshape(()),
        total.reshape(()),
        norm.reshape(()),
        new_wide[None],
        new_down[None],
        new_mom_wide[None],
        new_mom_dn[None],
        new_err[None, None],
        new_errd[None, None],
        own.T[None],
        ownd.T[None],
        new_q.T[None],
        new_qd.T[None],
        new_vec,
        new_vmom,
        new_fin,
        new_fmom,
        new_emb,
        new_emom,
        new_head.T,
        new_hmom.T,
    )


def solution(mesh):
    whole_seq = P(("rep", "grp"), None)
    by_rows = P(None, "grp", None)
    by_replica = P("rep", None, "grp", None)
    placed = (
        (whole_seq,) * 3 + (by_rows,) * 4 + (by_replica,) * 2 + (P(),) * 10
    )
    given = (P(),) * 3 + (by_rows,) * 4 + (by_replica,) * 2 + (by_rows,) * 2 + (P(),) * 10
    return jax.shard_map(shards, mesh=mesh, in_specs=placed, out_specs=given, check_vma=False)
```

```python
from functools import partial

import jax
import jax.numpy as jnp
import numpy as np
from jax import lax
from jax.experimental import pallas as pl
from jax.experimental.pallas import tpu as pltpu
from jax.sharding import PartitionSpec as P

D = 480
HEADS = 20
HDIM = 24
V = 33
PAD = 32
TOK = 40
WIDE = 512
EPS = 1e-05
BETA = 0.9
RATE_WIDE = 20000.0
RATE_LOWER = 3000.0
RATE_VECTOR = 20000.0
RATE_FINAL = 40000.0
RATE_EMBED = 60000.0
RATE_HEAD = 3000.0
CLIP = 0.005
F32 = jnp.float32
B16 = jnp.bfloat16
MIB = 2**20


ROOM = {
    "error_sketch": 16, "embed": 16, "project": 24, "attend": 30, "feed_and_loss": 56, "attend_back": 30,
    "input_grads": 30, "left_factors": 24, "merge_down": 12, "merge_rest": 16, "merge_in": 16, "finish": 30,
}


def params(name):
    return pltpu.CompilerParams(vmem_limit_bytes=ROOM[name] * MIB)


def nn(left, right):
    return jnp.dot(left, right, preferred_element_type=F32)


def nt(left, right):
    return lax.dot_general(left, right, (((1,), (1,)), ((), ())), preferred_element_type=F32)


def tn(left, right):
    return lax.dot_general(left, right, (((0,), (0,)), ((), ())), preferred_element_type=F32)


def thirds(value):
    top = value.astype(B16)
    rest = value - top.astype(F32)
    middle = rest.astype(B16)
    return top, middle, (rest - middle.astype(F32)).astype(B16)


def thirds_rows(value):
    return jnp.concatenate([part.astype(F32) for part in thirds(value)], 0).astype(B16)


def fold_rows(value):
    return value[0:8] + value[8:16] + value[16:24]


def exact_nt(left, right):
    return lax.dot_general(
        left, right, (((1,), (1,)), ((), ())),
        precision=lax.Precision.HIGHEST, preferred_element_type=F32,
    )


def exact_nn(left, right):
    return jnp.dot(left, right, precision=lax.Precision.HIGHEST, preferred_element_type=F32)


def three_nt(left, right):
    three = thirds_rows(left)
    top, middle, low = thirds(right)
    return fold_rows(nt(three, top) + nt(three, middle) + nt(three, low))


def three_nn(left, right):
    three = thirds_rows(left)
    top, middle, low = thirds(right)
    return fold_rows(nn(three, top) + nn(three, middle) + nn(three, low))


def norm_parts(value):
    center = value - jnp.mean(value, -1, keepdims=True)
    spread = jnp.mean(center * center, -1, keepdims=True)
    rstd = lax.rsqrt(spread + EPS)
    return center * rstd, rstd


def norm_back(grad, unit, rstd, gain):
    inner = grad * gain
    first = jnp.mean(inner, -1, keepdims=True)
    second = jnp.mean(inner * unit, -1, keepdims=True)
    return (
        rstd * (inner - first - unit * second),
        jnp.sum(grad * unit, 0, keepdims=True),
        jnp.sum(grad, 0, keepdims=True),
    )


def half_turn(value):
    return jnp.concatenate([value[HDIM // 2 :], value[: HDIM // 2]], 0)


def tail(rows, cols, ones):
    index = lax.broadcasted_iota(jnp.int32, (rows, cols), 0)
    return jnp.where(index < ones, 1.0, 0.0).astype(F32)


def lane_tail(rows, cols):
    index = lax.broadcasted_iota(jnp.int32, (rows, cols), 1)
    return jnp.where(index == 0, 1.0, 0.0).astype(F32)


def tables(length):
    half = HDIM // 2
    freq = np.float32(10000.0) ** (-np.arange(half, dtype=np.float32) * np.float32(2.0) / np.float32(HDIM))
    angle = np.arange(length, dtype=np.float32)[None, :] * freq.astype(np.float32)[:, None]
    cosine, sine = np.cos(angle), np.sin(angle)
    return (
        jnp.asarray(np.concatenate([cosine, cosine], 0), F32),
        jnp.asarray(np.concatenate([-sine, sine], 0), F32),
    )


def error_kernel(group, err_ref, errd_ref, q_ref, qd_ref, out_ref, row_ref):
    rows = err_ref.shape[0]
    out_ref[...] = jnp.zeros_like(out_ref)
    row_ref[...] = jnp.zeros_like(row_ref)
    row_ref[:, 0:rows] = three_nt(q_ref[...], err_ref[...])
    out_ref[0:8, :] = pltpu.roll(row_ref[...], rows * group[0], 1)
    start = pl.multiple_of(8 + 8 * group[0], 8)
    out_ref[pl.ds(start, 8), 0:D] = three_nt(qd_ref[...], errd_ref[...])


def embed_kernel(tok_ref, emb_ref, vec_ref, x_ref, h_ref, ht_ref, emb_s):
    step = tok_ref.shape[1]

    @pl.when(pl.program_id(0) == 0)
    def _():
        emb_s[...] = jnp.zeros_like(emb_s)
        emb_s[0:V, :] = emb_ref[...]

    index = lax.broadcasted_iota(jnp.int32, (TOK, step), 0)
    hot = jnp.where(index == tok_ref[...], 1.0, 0.0).astype(F32)
    hot = jnp.concatenate([hot, hot, hot], 0).astype(B16)
    x = tn(hot, thirds_rows(emb_s[...]))
    x_ref[...] = x
    unit, _ = norm_parts(x)
    normed = unit * vec_ref[:, 0:D] + vec_ref[:, D : 2 * D]
    h_ref[...] = normed.astype(B16)
    ht_ref[...] = jnp.concatenate([normed.T, tail(16, step, 1)], 0).astype(B16)


def spot(group, place, size, unit):
    return pl.ds(pl.multiple_of((group[0] ^ place) * size, unit), size)


def assemble(group, chunks, wide_s, out_s):
    for place, ref in enumerate(chunks):
        wide_s[spot(group, place, ref.shape[0], 8), :] = ref[...].astype(F32)
    out_s[...] = wide_s[...].astype(B16)


def project_kernel(members, group, h_ref, *refs):
    chunks = refs[:members]
    vec_ref, cos_ref, sin_ref, q_ref, k_ref, v_ref, wide_s, w_s = refs[members:]
    step = h_ref.shape[0]

    @pl.when(pl.program_id(0) == 0)
    def _():
        assemble(group, chunks, wide_s, w_s)

    act = nn(h_ref[...], w_s[...]) + vec_ref[:, 2 * D : 5 * D]
    turned = act.T
    cosine, sine = cos_ref[...], sin_ref[...]
    zeros = tail(PAD - HDIM, step, 0)
    ones = tail(PAD - HDIM, step, 3)
    for head in range(HEADS):
        low = HDIM * head
        query = turned[low : low + HDIM]
        query = (query * cosine + half_turn(query) * sine) * HDIM ** (-0.5)
        q_ref[head] = jnp.concatenate([query, zeros], 0).astype(B16)
        keys = turned[D + low : D + low + HDIM]
        keys = keys * cosine + half_turn(keys) * sine
        k_ref[head] = jnp.concatenate([keys, ones], 0).astype(B16)
        value = turned[2 * D + low : 2 * D + low + HDIM]
        v_ref[head] = jnp.concatenate([value, ones], 0).astype(B16)


def rows_of(value):
    return value.astype(F32).T.astype(B16)


def attend_kernel(q_ref, k_ref, v_ref, *refs):
    mix_ref, inv_ref, p_ref = refs[-3:]
    count, _, length = q_ref.shape
    zeros = tail(PAD - HDIM - 3, length, 0)

    def first(head):
        keys = rows_of(k_ref[head])
        query = q_ref[head]
        top = jnp.max(nn(keys, query), 0, keepdims=True)
        parts = [part.astype(F32) for part in thirds(-top)]
        return keys, jnp.concatenate([query[0:HDIM].astype(F32)] + parts + [zeros], 0).astype(B16)

    def second(head, keys, query):
        probs = jnp.exp(nn(keys, query)).astype(B16)
        p_ref[head] = probs
        out = nn(v_ref[head], probs)
        inverse = 1.0 / out[HDIM : HDIM + 1]
        mix_ref[HDIM * head : HDIM * head + HDIM, :] = out[0:HDIM] * inverse
        inv_ref[head] = inverse

    held = first(0)
    for head in range(count):
        ahead = first(head + 1) if head + 1 < count else None
        second(head, *held)
        held = ahead


def gelu_parts(upper):
    size = jnp.abs(upper) * (0.5**0.5)
    bell = jnp.exp(-0.5 * upper * upper)
    t = 1.0 / (1.0 + 0.3275911 * size)
    poly = t * (0.254829592 + t * (-0.284496736 + t * (1.421413741 + t * (-1.453152027 + t * 1.061405429))))
    lower = 0.5 * poly * bell
    cdf = jnp.where(upper < 0, lower, 1.0 - lower)
    return upper * cdf, cdf + upper * (0.3989422804014327 * bell)


def middle_kernel(members, group, mixa_ref, mixb_ref, inva_ref, invb_ref, x_ref, mask_ref, tgt_ref,
                  count_ref, vec_ref, fin_ref, head_ref, q_ref, qd_ref, *refs):
    chunks, chunks_down, refs = refs[:members], refs[members : 2 * members], refs[2 * members :]
    dm_ref, dx_ref, s_ref, e_ref, *refs = refs
    outs, outs_down, refs = refs[:members], refs[members : 2 * members], refs[2 * members :]
    acc_o, acc_u, acc_d, head_s, hid_s, slope_s, wide_s, wr_ref, wd_ref = refs
    pid = pl.program_id(0)
    step = x_ref.shape[0]
    wide = wd_ref.shape[0]
    wo = slice(wide, wide + D)

    @pl.when(pid == 0)
    def _():
        acc_o[...] = jnp.zeros_like(acc_o)
        acc_u[...] = jnp.zeros_like(acc_u)
        acc_d[...] = jnp.zeros_like(acc_d)
        e_ref[...] = jnp.zeros_like(e_ref)
        s_ref[...] = jnp.zeros_like(s_ref)
        head_s[...] = jnp.zeros_like(head_s)
        head_s[0:V, 0 : D + 1] = head_ref[...]
        assemble(group, chunks, wide_s, wr_ref)
        for place, ref in enumerate(chunks_down):
            wd_ref[spot(group, place, ref.shape[0], 16), :] = ref[...]

    mix = jnp.concatenate([mixa_ref[...], mixb_ref[...]], 0)
    half = inva_ref.shape[0]
    mixed = jnp.concatenate([mix, tail(16, step, 1)], 0).astype(B16)
    middle = x_ref[...] + tn(mixed[0:D], wr_ref[:, wo]) + vec_ref[:, 5 * D : 6 * D]
    unit2, rstd2 = norm_parts(middle)
    gain2 = vec_ref[:, 6 * D : 7 * D]
    normed2 = unit2 * gain2 + vec_ref[:, 7 * D : 8 * D]
    normed2 = jnp.concatenate([normed2, lane_tail(step, WIDE - D)], 1).astype(B16)
    bias_up = vec_ref[:, 9 * D :]
    block = 384
    for low in range(0, wide, block):
        cut = slice(low, low + block)
        upper = nn(normed2[:, 0:D], wr_ref[:, cut]) + bias_up[:, cut]
        hidden, slope = gelu_parts(upper)
        hid_s[:, cut] = hidden.astype(B16)
        slope_s[:, cut] = slope
    resid = middle + nn(hid_s[...], wd_ref[...]) + vec_ref[:, 8 * D : 9 * D]
    unit3, rstd3 = norm_parts(resid)
    final = unit3 * fin_ref[0:1, :] + fin_ref[1:2, :]
    final = jnp.concatenate([final, lane_tail(step, WIDE - D)], 1).astype(B16)

    lanes = lax.broadcasted_iota(jnp.int32, (TOK, WIDE), 1)
    bias = jnp.sum(jnp.where(lanes == D, head_s[...], 0.0), 1, keepdims=True)
    table = head_s[:, 0:D].astype(B16)
    rows = lax.broadcasted_iota(jnp.int32, (TOK, step), 0)
    logits = jnp.where(rows < V, nt(table, final[:, 0:D]) + bias, -1e30)
    shifted = logits - jnp.max(logits, 0, keepdims=True)
    expo = jnp.exp(shifted)
    total = jnp.sum(expo, 0, keepdims=True)
    picks = rows == tgt_ref[...]
    weight = mask_ref[...].astype(F32)
    picked = jnp.sum(jnp.where(picks, shifted, 0.0), 0, keepdims=True)
    loss = jnp.sum((jnp.log(total) - picked) * weight, 1, keepdims=True)
    grad_logits = (expo / total - jnp.where(picks, 1.0, 0.0)) * (weight * (1.0 / count_ref[0:1, 0:1]))
    grad_logits = grad_logits.astype(B16)
    e_ref[16 : 16 + TOK, :] += nn(grad_logits, final)
    grad_resid, grad_fg, grad_fb = norm_back(tn(grad_logits, table), unit3, rstd3, fin_ref[0:1, :])

    grad_y = grad_resid.astype(B16)
    acc_d[...] += tn(hid_s[...], grad_y)
    for low in range(0, wide, block):
        cut = slice(low, low + block)
        grad_hidden = nt(grad_y, wd_ref[cut, :])
        hid_s[:, cut] = (grad_hidden * slope_s[:, cut]).astype(B16)
    acc_u[...] += tn(normed2, hid_s[...])
    grad_mid, grad_g2, grad_b2 = norm_back(nt(hid_s[...], wr_ref[:, 0:wide]), unit2, rstd2, gain2)
    grad_mid = grad_mid + grad_resid
    dx_ref[...] = grad_mid
    branch = grad_mid.astype(B16)
    acc_o[...] += nn(mixed, branch)
    grad_mixed = nt(wr_ref[:, wo], branch).astype(B16).astype(F32)
    zeros = tail(PAD - HDIM - 3, step, 0)
    for head in range(HEADS):
        cut = slice(HDIM * head, HDIM * head + HDIM)
        inverse = inva_ref[head] if head < half else invb_ref[head - half]
        scaled = (grad_mixed[cut] * inverse).astype(B16).astype(F32)
        delta = -jnp.sum(scaled * mix[cut], 0, keepdims=True)
        top, mid, low = thirds(delta)
        dm_ref[head] = jnp.concatenate(
            [scaled, top.astype(F32), mid.astype(F32), low.astype(F32), zeros], 0
        ).astype(B16)
    e_ref[1:2, 0:D] += grad_g2
    e_ref[2:3, 0:D] += grad_b2
    e_ref[3:4, 0:D] += jnp.sum(grad_y.astype(F32), 0, keepdims=True)
    e_ref[8:9, 0:D] += grad_fg
    e_ref[9:10, 0:D] += grad_fb
    e_ref[10:11, :] += jnp.broadcast_to(loss, (1, WIDE))

    @pl.when(pid == pl.num_programs(0) - 1)
    def _():
        e_ref[0:1, 0:D] = acc_o[D : D + 1, :]
        for part in range(wide // D):
            e_ref[4 + part : 5 + part, 0:D] = acc_u[D : D + 1, D * part : D * part + D]
        go = acc_o[0:D, :].astype(B16)
        gu = acc_u[0:D, :].astype(B16)
        sketch = nt(thirds_rows(q_ref[:, 3 * D : 4 * D]), go) + nt(thirds_rows(q_ref[:, 4 * D :]), gu)
        s_ref[0:8, 0:D] = fold_rows(sketch)
        start = thirds_rows(qd_ref[...])
        for part in range(wide // D):
            piece = nt(start, acc_d[D * part : D * part + D, :].astype(B16))
            s_ref[8 + 8 * part : 16 + 8 * part, 0:D] = fold_rows(piece)
        for place, ref in enumerate(outs):
            at = spot(group, place, ref.shape[0], 8)
            ref[:, 0:wide] = acc_u[at, :].astype(B16)
            ref[:, wo] = acc_o[at, :].astype(B16)
        for place, ref in enumerate(outs_down):
            ref[...] = acc_d[spot(group, place, ref.shape[0], 8), :].astype(B16)


def attend_back_kernel(p_ref, q_ref, k_ref, v_ref, dm_ref, cos_ref, sin_ref, da_ref):
    cosine, sine = cos_ref[...], sin_ref[...]
    parts = [[], [], []]
    for head in range(p_ref.shape[0]):
        probs = p_ref[head]
        grad = dm_ref[head]
        slope = nn(rows_of(v_ref[head]), grad)
        grad_scores = (probs.astype(F32) * slope).astype(B16)
        grad_value = nt(grad, probs)[0:HDIM]
        grad_keys = nt(q_ref[head], grad_scores)[0:HDIM]
        grad_query = nn(k_ref[head], grad_scores)[0:HDIM] * HDIM ** (-0.5)
        parts[0].append(grad_query * cosine + half_turn(grad_query * sine))
        parts[1].append(grad_keys * cosine + half_turn(grad_keys * sine))
        parts[2].append(grad_value)
    for index in range(3):
        da_ref[index] = jnp.concatenate(parts[index], 0).astype(B16)


def input_kernel(members, group, tok_ref, da_ref, h_ref, x_ref, dx_ref, vec_ref, q_ref,
                 s_ref, serr_ref, e_ref, *refs):
    chunks, refs = refs[:members], refs[members:]
    outs, pieces, refs = refs[:members], refs[members : 2 * members], refs[2 * members :]
    out_ref, acc_w, acc_e, wide_s, w_s = refs
    pid = pl.program_id(0)
    step = x_ref.shape[0]

    @pl.when(pid == 0)
    def _():
        acc_w[...] = jnp.zeros_like(acc_w)
        acc_e[...] = jnp.zeros_like(acc_e)
        out_ref[...] = jnp.zeros_like(out_ref)
        assemble(group, chunks, wide_s, w_s)

    da = da_ref[...].reshape(3 * D, step)
    acc_w[...] += nt(h_ref[...], da)
    grad = nn(w_s[...], da).T
    unit, rstd = norm_parts(x_ref[...])
    grad_x, grad_g, grad_b = norm_back(grad, unit, rstd, vec_ref[:, 0:D])
    grad_x = grad_x + dx_ref[...]
    index = lax.broadcasted_iota(jnp.int32, (TOK, step), 0)
    hot = jnp.where(index == tok_ref[...], 1.0, 0.0).astype(B16)
    for part in thirds(grad_x):
        acc_e[...] += nn(hot, part)
    out_ref[40:41, 0:D] += grad_g
    out_ref[41:42, 0:D] += grad_b

    @pl.when(pid == pl.num_programs(0) - 1)
    def _():
        for part in range(3):
            out_ref[42 + part : 43 + part, 0:D] = acc_w[D : D + 1, D * part : D * part + D]
        out_ref[0:40, :] = s_ref[...] + serr_ref[...]
        out_ref[0:8, 0:D] += fold_rows(nt(thirds_rows(q_ref[:, 0 : 3 * D]), acc_w[0:D, :].astype(B16)))
        out_ref[45:48, :] = e_ref[8:11, :]
        out_ref[48:56, :] = e_ref[0:8, :]
        out_ref[56 : 56 + V, 0:D] = acc_e[0:V, :]
        out_ref[56 + V : 56 + 2 * V, :] = e_ref[16 : 16 + V, :]
        for place, ref in enumerate(outs):
            ref[...] = acc_w[spot(group, place, ref.shape[0], 8), :].astype(B16)
        for place, ref in enumerate(pieces):
            ref[...] = out_ref[spot(group, place, ref.shape[0], 8), :]


def orthonormal(sketch, gram):
    basis = jnp.zeros_like(sketch[0])
    count = gram.shape[0]
    index = lax.broadcasted_iota(jnp.int32, (count, 1), 0)
    out = [jnp.zeros_like(part) for part in sketch]
    left = list(sketch)
    for step in range(count):
        pivot = gram[step : step + 1, step : step + 1]
        scale = 1.0 / jnp.sqrt(pivot)
        column = gram[:, step : step + 1] * scale
        row = gram[step : step + 1, :] * scale
        column = jnp.where(index > step, column, 0.0)
        gram = gram - column * row
        for place in range(len(left)):
            base = left[place][step : step + 1, :] * scale
            out[place] = jnp.where(index == step, base, out[place])
            left[place] = left[place] - column * base
    return out


def factor_kernel(members, group, *refs):
    chunks, ins, rests, downs = (refs[members * part : members * part + members] for part in range(4))
    err_ref, errd_ref, a_ref, p_ref, own_ref, ownd_ref, *refs = refs[4 * members :]
    outs, f_s = refs[:members], refs[members]
    rows, wide_cols = err_ref.shape
    hidden = wide_cols - 4 * D
    parts = hidden // D
    for place, ref in enumerate(chunks):
        a_ref[spot(group, place, ref.shape[0], 8), :] = ref[...]
    wide = a_ref[0:8, 0:D]
    down = [a_ref[8 + 8 * part : 16 + 8 * part, 0:D] for part in range(parts)]
    gram = exact_nt(wide, wide)
    (wide,) = orthonormal([wide], gram)
    gram = exact_nt(down[0], down[0])
    for part in range(1, parts):
        gram = gram + exact_nt(down[part], down[part])
    down = orthonormal(down, gram)
    p_ref[...] = jnp.zeros_like(p_ref)
    p_ref[0:8, 0:D] = wide
    for part in range(parts):
        p_ref[8 + 8 * part : 16 + 8 * part, 0:D] = down[part]
    f_s[...] = jnp.zeros_like(f_s)
    for place in range(members):
        piece = pltpu.roll(p_ref[0:8, :], (WIDE - rows * (group[0] ^ place)) % WIDE, 1)[:, 0:rows]
        piece_down = p_ref[pl.ds(pl.multiple_of(8 + 8 * (group[0] ^ place), 8), 8), :][:, 0:D]
        if place == 0:
            own_ref[...] = piece
            ownd_ref[...] = piece_down
            f_s[:, 0:wide_cols] = three_nn(piece, err_ref[...])
            f_s[:, wide_cols : wide_cols + D] = three_nn(piece_down, errd_ref[...])
        three = thirds_rows(piece)
        f_s[:, 0 : 3 * D] += fold_rows(nn(three, ins[place][...]))
        f_s[:, 4 * D : wide_cols] += fold_rows(nn(three, rests[place][:, 0:hidden]))
        f_s[:, 3 * D : 4 * D] += fold_rows(nn(three, rests[place][:, hidden:]))
        f_s[:, wide_cols : wide_cols + D] += fold_rows(nn(thirds_rows(piece_down), downs[place][...]))
    for place, ref in enumerate(outs):
        ref[...] = f_s[:, spot(group, place, ref.shape[1], 128)]


def merge_kernel(*refs):
    *chunks, err_ref, out_ref = refs
    value = err_ref[...]
    for ref in chunks:
        value = value + ref[...].astype(F32)
    out_ref[...] = value


def merge_rest_kernel(*refs):
    *chunks, err_ref, out_ref = refs
    value = chunks[0][...].astype(F32)
    for ref in chunks[1:]:
        value = value + ref[...].astype(F32)
    hidden = value.shape[1] - D
    out_ref[:, 0:hidden] = value[:, 0:hidden] + err_ref[:, 4 * D :]
    out_ref[:, hidden:] = value[:, hidden:] + err_ref[:, 3 * D : 4 * D]


def merge_in_kernel(*refs):
    *chunks, err_ref, out_ref = refs
    value = err_ref[:, 0 : 3 * D]
    for ref in chunks:
        value = value + ref[...].astype(F32)
    out_ref[...] = value


def six(left, right):
    first, second = thirds(left), thirds(right)
    order = ((0, 0), (0, 1), (1, 0), (1, 1), (0, 2), (2, 0))
    left = jnp.concatenate([first[i].astype(F32) for i, _ in order], 0).astype(B16)
    right = jnp.concatenate([second[j].astype(F32) for _, j in order], 0).astype(B16)
    return tn(left, right)


def renew(weight, moment, grad, scale, rate):
    new_moment = BETA * moment + scale * grad
    return weight - rate * new_moment, new_moment


def finish_kernel(members, replicas, group, *refs):
    chunks, rest = refs[:members], refs[members:]
    (a_ref, p_ref, own_ref, ownd_ref,
     w_ref, wd_ref, m_ref, md_ref, ein_ref, erest_ref, errd_ref, count_ref,
     vec_ref, vmom_ref, fin_ref, fmom_ref, emb_ref, emom_ref, head_ref, hmom_ref,
     loss_ref, total_ref, norm_ref, nq_ref, nqd_ref, nw_ref, nwd_ref, nm_ref, nmd_ref, ne_ref, ned_ref,
     nvec_ref, nvmom_ref, nfin_ref, nfmom_ref, nemb_ref, nemom_ref, nhead_ref, nhmom_ref, f_s) = rest
    wide_cols = w_ref.shape[1]
    hidden = wide_cols - 4 * D
    for place, ref in enumerate(chunks):
        f_s[:, spot(group, place, ref.shape[1], 128)] = ref[...]
    factor, factor_down = f_s[:, 0:wide_cols], f_s[:, wide_cols : wide_cols + D]
    nq_ref[...] = factor
    nqd_ref[...] = factor_down
    a = a_ref[...]
    square = jnp.sum(a[40:47, 0:D] * a[40:47, 0:D]) + jnp.sum(a[48:56, 0:D] * a[48:56, 0:D])
    emb, top = a[56 : 56 + V, 0:D], a[56 + V : 56 + 2 * V, 0 : D + 1]
    square = square + jnp.sum(emb * emb) + jnp.sum(top * top)
    basis = p_ref[...]
    gram = exact_nt(basis[0:8, 0:D], basis[0:8, 0:D])
    square = square + jnp.sum(gram * exact_nt(factor, factor))
    gram = jnp.zeros((8, 8), F32)
    for part in range(1, basis.shape[0] // 8):
        piece = basis[8 * part : 8 * part + 8, 0:D]
        gram = gram + exact_nt(piece, piece)
    square = square + jnp.sum(gram * exact_nt(factor_down, factor_down))
    norm = jnp.sqrt(square)
    norm_ref[...] = jnp.broadcast_to(norm, norm_ref.shape)
    loss_ref[...] = a[47:48, 0:1]
    total_ref[...] = count_ref[0:1, 0:1]
    scale = jnp.minimum(1.0, CLIP / norm)

    approx = six(own_ref[...], factor)
    nw_ref[...], nm_ref[...] = renew(w_ref[...], m_ref[...], approx, scale, RATE_WIDE)
    share = approx * (1.0 / replicas)
    ne_ref[:, 0 : 3 * D] = ein_ref[...] - share[:, 0 : 3 * D]
    ne_ref[:, 3 * D : 4 * D] = erest_ref[:, hidden:] - share[:, 3 * D : 4 * D]
    ne_ref[:, 4 * D :] = erest_ref[:, 0:hidden] - share[:, 4 * D :]
    approx = six(ownd_ref[...], factor_down)
    nwd_ref[...], nmd_ref[...] = renew(wd_ref[...], md_ref[...], approx, scale, RATE_LOWER)
    ned_ref[...] = errd_ref[...] - approx * (1.0 / replicas)

    places = (40, 41, 42, 43, 44, 48, 49, 50, 51, 52, 53, 54, 55)
    for row, place in enumerate(places):
        cut = slice(D * row, D * row + D)
        nvec_ref[:, cut], nvmom_ref[:, cut] = renew(
            vec_ref[:, cut], vmom_ref[:, cut], a[place : place + 1, 0:D], scale, RATE_VECTOR
        )
    nfin_ref[...], nfmom_ref[...] = renew(fin_ref[...], fmom_ref[...], a[45:47, 0:D], scale, RATE_FINAL)
    nemb_ref[...], nemom_ref[...] = renew(emb_ref[...], emom_ref[...], emb, scale, RATE_EMBED)
    nhead_ref[...], nhmom_ref[...] = renew(head_ref[...], hmom_ref[...], top, scale, RATE_HEAD)


def swap(value, axis, bit):
    size = lax.axis_size(axis)
    return lax.ppermute(value, axis, [(i, i ^ bit) for i in range(size)])


def bits_of(axis):
    size, bit, out = lax.axis_size(axis), 1, []
    while bit < size:
        out.append(bit)
        bit *= 2
    return out


def tie(*values):
    return lax.optimization_barrier(values)


def send_chunks(pieces):
    return [pieces[0]] + [swap(piece, "grp", place) for place, piece in enumerate(pieces) if place]


def moves_of(axis):
    first, *bits = bits_of(axis)
    pairs = [[first]] + [bits[at : at + 2] for at in range(0, len(bits), 2)]
    return [pair + [sum(pair)] * (len(pair) - 1) for pair in pairs]


def add_chunks(pieces, work=()):
    work, results = dict(work), {}

    def beside(turn, moved):
        if turn in work:
            moved, results[turn] = tie(moved, work[turn]())
        return moved

    got = beside(0, send_chunks(pieces))
    total = got[0]
    for piece in got[1:]:
        total = total + piece
    for turn, moves in enumerate(moves_of("rep")):
        for piece in beside(turn + 1, [swap(total, "rep", move) for move in moves]):
            total = total + piece
    got = [total] + [swap(total, "grp", place) for place in range(1, len(pieces))]
    return beside(-1, got), results


def gather_start(value):
    first, *bits = reversed(bits_of("grp"))
    return [value, swap(value, "grp", first)]


def gather_end(pieces):
    first, *bits = reversed(bits_of("grp"))
    order = [0, first]
    for bit in bits:
        pieces = pieces + [swap(piece, "grp", bit) for piece in pieces]
        order = order + [place ^ bit for place in order]
    return [pieces[order.index(place)] for place in range(len(order))]


def halve_start(pieces):
    first, *bits = bits_of("grp")
    keep = [place for place in range(len(pieces)) if not place & first]
    return [(place, pieces[place], swap(pieces[place | first], "grp", first)) for place in keep]


def halve_end(pairs):
    first, *bits = bits_of("grp")
    (_, own, other), *others = pairs
    kept = [own, other]
    sums = {place: (mine.astype(F32) + theirs.astype(F32)).astype(B16) for place, mine, theirs in others}
    for bit in bits:
        kept.append(swap(sums[bit], "grp", bit))
        sums = {
            place: (sums[place].astype(F32) + swap(sums[place | bit], "grp", bit).astype(F32)).astype(B16)
            for place in sums
            if not place & bit
        }
    return kept


def whole(shape):
    return pl.BlockSpec(shape, lambda *_: (0,) * len(shape))


def shards(tokens, mask, targets, mats_d, mats_down, mom_d, mom_down, err_d, err_down, q_d, q_down,
           vectors, vec_mom, final_norm, final_mom, embed, embed_mom, head, head_mom):
    length = tokens.shape[1]
    wide = mats_d.shape[2]
    hidden = wide - 4 * D
    rows = mats_d.shape[1]
    rows_down = mats_down.shape[1]
    step = 256
    steps = length // step
    step_mid = 2 * step
    index = lax.axis_index("grp").astype(jnp.int32)
    group = index.reshape(1)
    members = lax.axis_size("grp")
    cosine, sine = tables(length)
    q_t, qd_t = q_d[0].T, q_down[0].T
    head_t = head.T
    err, errd = err_d[0, 0], err_down[0, 0]

    def call(kernel, name, grid, ins, outs, shapes, scratch=()):
        return pl.pallas_call(
            kernel,
            grid_spec=pltpu.PrefetchScalarGridSpec(
                num_scalar_prefetch=1, grid=grid, in_specs=ins, out_specs=outs, scratch_shapes=scratch
            ),
            out_shape=shapes,
            compiler_params=params(name),
            name=name,
        )

    shape = jax.ShapeDtypeStruct
    rounds = [("grp", [bit]) for bit in bits_of("grp")] + [("rep", moves) for moves in moves_of("rep")]

    def advance(value, times=1):
        for _ in range(min(times, len(rounds))):
            axis, moves = rounds.pop(0)
            for piece in [swap(value, axis, move) for move in moves]:
                value = value + piece
        return value

    cols = pl.BlockSpec((1, step), lambda i, *_: (0, i))
    flat = pl.BlockSpec((step, D), lambda i, *_: (i, 0))
    heads = pl.BlockSpec((HEADS, PAD, step), lambda i, *_: (0, 0, i))
    wave = pl.BlockSpec((HDIM, step), lambda i, *_: (0, i))
    ext = pl.BlockSpec((D + 16, step), lambda i, *_: (0, i))

    w_in = gather_start(mats_d[0][:, : 3 * D].astype(B16))
    counted = jnp.broadcast_to(jnp.sum(mask.astype(F32)), (8, 128))
    more = advance(counted)
    err_sketch = call(
        error_kernel, "error_sketch", (1,),
        [whole((rows, wide)), whole((rows_down, D)), whole((8, wide)), whole((8, D))],
        whole((40, WIDE)), shape((40, WIDE), F32), [pltpu.VMEM((8, WIDE), F32)],
    )(group, err, errd, q_t, qd_t)
    x, h, h_t = pl.pallas_call(
        embed_kernel,
        grid=(steps,),
        in_specs=[cols, whole((V, D)), whole(vectors.shape)],
        out_specs=[flat, flat, ext],
        out_shape=[shape((length, D), F32), shape((length, D), B16), shape((D + 16, length), B16)],
        scratch_shapes=[pltpu.VMEM((TOK, D), F32)],
        compiler_params=params("embed"),
        name="embed",
    )(tokens, embed, vectors)
    w_in, err_sketch, h, counted = tie(w_in, err_sketch, h, more)
    w_in = gather_end(w_in)
    rest = jnp.concatenate([mats_d[0][:, 4 * D :], mats_d[0][:, 3 * D : 4 * D]], 1).astype(B16)
    down = mats_down[0].astype(B16)
    w_in, counted, rest, down = tie(w_in, counted, rest, down)
    w_rest, w_down = gather_start(rest), gather_start(down)
    more = advance(counted)
    query, keys, value = call(
        partial(project_kernel, members), "project", (steps,),
        [flat] + [whole((rows, 3 * D))] * members + [whole(vectors.shape), wave, wave],
        [heads] * 3, [shape((HEADS, PAD, length), B16)] * 3,
        [pltpu.VMEM((D, 3 * D), F32), pltpu.VMEM((D, 3 * D), B16)],
    )(group, h, *w_in, vectors, cosine, sine)
    query, counted = tie(query, more)

    half = HEADS // 2
    pair = 2
    turned = half // pair
    mixes, inverses, probs = [], [], []
    for part in range(2):
        one = pl.BlockSpec((1, PAD, length), lambda i, part=part: (i + half * part, 0, 0))
        more = advance(counted, 1 + part * len(rounds))
        mix, inverse, *probs = pl.pallas_call(
            attend_kernel,
            grid=(half,),
            in_specs=[one, one, one] + [pl.BlockSpec(memory_space=pl.ANY)] * len(probs),
            out_specs=[
                pl.BlockSpec((HDIM, length), lambda i: (i, 0)),
                pl.BlockSpec((1, 1, length), lambda i: (i, 0, 0)),
                pl.BlockSpec((1, length, length), lambda i, part=part: (i + half * part, 0, 0)),
            ],
            out_shape=[
                shape((half * HDIM, length), F32),
                shape((half, 1, length), F32),
                shape((HEADS, length, length), B16),
            ],
            input_output_aliases={3: 2} if probs else {},
            compiler_params=params("attend"),
            name="attend",
        )(query, keys, value, *probs)
        mix, query, counted, w_rest, w_down = tie(mix, query, more, w_rest, w_down)
        if part == 0:
            w_rest, w_down = gather_end(w_rest), gather_end(w_down)
        mixes.append(mix)
        inverses.append(inverse)

    cols2 = pl.BlockSpec((1, step_mid), lambda i, *_: (0, i))
    flat2 = pl.BlockSpec((step_mid, D), lambda i, *_: (i, 0))
    heads2 = pl.BlockSpec((HEADS, PAD, step_mid), lambda i, *_: (0, 0, i))
    everyone = [(rows, D + hidden)] * members + [(rows_down, D)] * members
    grad_mix, grad_mid, sketch, early, *grads = call(
        partial(middle_kernel, members), "feed_and_loss", (length // step_mid,),
        [pl.BlockSpec((half * HDIM, step_mid), lambda i, *_: (0, i))] * 2
        + [pl.BlockSpec((half, 1, step_mid), lambda i, *_: (0, 0, i))] * 2
        + [
            flat2, cols2, cols2, whole((8, 128)), whole(vectors.shape), whole((2, D)),
            whole((V, D + 1)), whole((8, wide)), whole((8, D)),
        ]
        + [whole(item) for item in everyone],
        [heads2, flat2, whole((40, WIDE)), whole((56, WIDE))] + [whole(item) for item in everyone],
        [
            shape((HEADS, PAD, length), B16),
            shape((length, D), F32),
            shape((40, WIDE), F32),
            shape((56, WIDE), F32),
        ]
        + [shape(item, B16) for item in everyone],
        [
            pltpu.VMEM((D + 16, D), F32),
            pltpu.VMEM((WIDE, hidden), F32),
            pltpu.VMEM((hidden, D), F32),
            pltpu.VMEM((TOK, WIDE), F32),
            pltpu.VMEM((step_mid, hidden), B16),
            pltpu.VMEM((step_mid, hidden), F32),
            pltpu.VMEM((D, D + hidden), F32),
            pltpu.VMEM((D, D + hidden), B16),
            pltpu.VMEM((hidden, D), B16),
        ],
    )(group, *mixes, *inverses, x, mask, targets, counted, vectors, final_norm, head_t, q_t, qd_t,
      *w_rest, *w_down)
    g_rest, g_down = grads[:members], grads[members:]
    all_down = send_chunks(g_down)
    all_rest = send_chunks(g_rest)

    two = pl.BlockSpec((pair, PAD, length), lambda i: (i, 0, 0))
    grad_act = pl.pallas_call(
        attend_back_kernel,
        grid=(HEADS // pair,),
        in_specs=[
            pl.BlockSpec((pair, length, length), lambda i: (i, 0, 0)),
            two, two, two, two, whole((HDIM, length)), whole((HDIM, length)),
        ],
        out_specs=pl.BlockSpec((3, pair * HDIM, length), lambda i: (0, i, 0)),
        out_shape=shape((3, D, length), B16),
        compiler_params=params("attend_back"),
        name="attend_back",
    )(*probs, query, keys, value, grad_mix, cosine, sine)
    all_down, all_rest, grad_act = tie(all_down, all_rest, grad_act)

    act = pl.BlockSpec((3, D, step), lambda i, *_: (0, 0, i))
    size = 128 // members
    ins = [(rows, 3 * D)] * members
    grads = call(
        partial(input_kernel, members), "input_grads", (steps,),
        [
            cols, act, ext, flat, flat,
            whole(vectors.shape), whole((8, wide)), whole((40, WIDE)), whole((40, WIDE)), whole((56, WIDE)),
        ]
        + [whole(item) for item in ins],
        [whole(item) for item in ins] + [whole((size, WIDE))] * members,
        [shape(item, B16) for item in ins] + [shape((size, WIDE), F32)] * members,
        [
            pltpu.VMEM((128, WIDE), F32), pltpu.VMEM((D + 16, 3 * D), F32), pltpu.VMEM((TOK, D), F32),
            pltpu.VMEM((D, 3 * D), F32), pltpu.VMEM((D, 3 * D), B16),
        ],
    )(group, tokens, grad_act, h_t, x, grad_mid, vectors, q_t, sketch, err_sketch, early, *w_in)
    g_in, pieces = grads[:members], grads[members:]
    half_in = halve_start(g_in)

    def merge(kernel, name, chunks, err, result):
        return lambda: pl.pallas_call(
            kernel, out_shape=shape(result, F32), compiler_params=params(name), name=name
        )(*chunks, err)

    chunks, merged = add_chunks(
        pieces,
        (
            (0, merge(merge_kernel, "merge_down", all_down, errd, errd.shape)),
            (1, lambda: halve_end(half_in)),
            (2, merge(merge_rest_kernel, "merge_rest", all_rest, err, (rows, D + hidden))),
        ),
    )
    merged_down, all_in, merged_rest = (merged[turn] for turn in range(3))
    span = -(-(wide + WIDE) // (128 * members)) * 128
    shared, basis, own, ownd, *pieces = call(
        partial(factor_kernel, members), "left_factors", (1,),
        [whole((size, WIDE))] * members + [whole(item) for item in ins + everyone]
        + [whole((rows, wide)), whole((rows_down, D))],
        [whole((128, WIDE)), whole((40, WIDE)), whole((8, rows)), whole((8, rows_down))]
        + [whole((8, span))] * members,
        [
            shape((128, WIDE), F32), shape((40, WIDE), F32), shape((8, rows), F32), shape((8, rows_down), F32),
        ]
        + [shape((8, span), F32)] * members,
        [pltpu.VMEM((8, span * members), F32)],
    )(group, *chunks, *g_in, *g_rest, *g_down, err, errd)

    chunks, merged = add_chunks(
        pieces, ((0, merge(merge_in_kernel, "merge_in", all_in, err, (rows, 3 * D))),)
    )
    merged_in = merged[0]

    same = lambda value: shape(value.shape, F32)
    replicas = lax.axis_size("rep")
    small = (vectors, vec_mom, final_norm, final_mom, embed, embed_mom, head_t, head_mom.T)
    given = (
        *chunks, shared, basis, own, ownd,
        mats_d[0], mats_down[0], mom_d[0], mom_down[0], merged_in, merged_rest, merged_down, counted, *small,
    )
    shapes = [
        shape((1, 1), F32), shape((1, 1), F32), shape((1, 1), F32), shape((8, wide), F32), shape((8, D), F32),
        same(mats_d[0]), same(mats_down[0]), same(mats_d[0]), same(mats_down[0]), same(err), same(errd),
    ] + [same(item) for item in small]
    outs = call(
        partial(finish_kernel, members, replicas), "finish", (1,),
        [whole(item.shape) for item in given], [whole(item.shape) for item in shapes], shapes,
        [pltpu.VMEM((8, span * members), F32)],
    )(group, *given)
    (loss, total, norm, new_q, new_qd, new_wide, new_down, new_mom_wide, new_mom_dn, new_err, new_errd,
     new_vec, new_vmom, new_fin, new_fmom, new_emb, new_emom, new_head, new_hmom) = outs
    return (
        loss.reshape(()),
        total.reshape(()),
        norm.reshape(()),
        new_wide[None],
        new_down[None],
        new_mom_wide[None],
        new_mom_dn[None],
        new_err[None, None],
        new_errd[None, None],
        own.T[None],
        ownd.T[None],
        new_q.T[None],
        new_qd.T[None],
        new_vec,
        new_vmom,
        new_fin,
        new_fmom,
        new_emb,
        new_emom,
        new_head.T,
        new_hmom.T,
    )


def solution(mesh):
    whole_seq = P(("rep", "grp"), None)
    by_rows = P(None, "grp", None)
    by_replica = P("rep", None, "grp", None)
    placed = (
        (whole_seq,) * 3 + (by_rows,) * 4 + (by_replica,) * 2 + (P(),) * 10
    )
    given = (P(),) * 3 + (by_rows,) * 4 + (by_replica,) * 2 + (by_rows,) * 2 + (P(),) * 10
    return jax.shard_map(shards, mesh=mesh, in_specs=placed, out_specs=given, check_vma=False)
```
